32 devices in a mesh: dp: 16 (over z, x, core), ctx: 2 (over y).
Axes of the slice: x: 2, y: 2, z: 4, core: 2. Of those that a mesh axis runs over, the one named last changes fastest.
Arguments:
- tokens: bfloat16 [32, 1024, 1024], P('dp', 'ctx'), may hold values from -6 to 6
- w_in: bfloat16 [1024, 3072], P('dp', 'ctx'), may hold values from -0.1875 to 0.1875
- w_out: bfloat16 [1024, 1024], P('dp', 'ctx'), may hold values from -0.1875 to 0.1875
- w_gate: bfloat16 [1024, 4608], P('dp', 'ctx'), may hold values from -0.1875 to 0.1875
- w_up: bfloat16 [1024, 4608], P('dp', 'ctx'), may hold values from -0.1875 to 0.1875
- w_down: bfloat16 [4608, 1024], P('dp', 'ctx'), may hold values from -0.09375 to 0.09375
- gain_mix: bfloat16 [1024], P('dp'), may hold values from 0.099609375 to 1.8984375
- gain_ffn: bfloat16 [1024], P('dp'), may hold values from 0.099609375 to 1.8984375
- kernel: bfloat16 [3, 1024], P(None, 'dp'), may hold values from -3.5 to 3.5
- cotangent: bfloat16 [32, 1024, 1024], P('dp', 'ctx'), may hold values from -6 to 6
Outputs:
- result: bfloat16 [32, 1024, 1024], P('dp', 'ctx')
- grad_tokens: float32 [32, 1024, 1024], P('dp', 'ctx')
- grad_w_in: float32 [1024, 3072], P('dp', 'ctx')
- grad_w_out: float32 [1024, 1024], P('dp', 'ctx')
- grad_w_gate: float32 [1024, 4608], P('dp', 'ctx')
- grad_w_up: float32 [1024, 4608], P('dp', 'ctx')
- grad_w_down: float32 [4608, 1024], P('dp', 'ctx')
- grad_gain_mix: float32 [1024], P('dp')
- grad_gain_ffn: float32 [1024], P('dp')
- grad_kernel: float32 [3, 1024], P(None, 'dp')
The draws below stay inside these ranges and needn't reach their ends.
All inputs are finite; a program needn't handle non-finite values.
Results may differ from the reference program's by a relative error of at most 0.0092.
Values may be sent and summed in bfloat16 or wider, within the bound.
No kernel may reach another device: no remote copies, remote signals or barrier semaphores. Data moves between devices by JAX's collectives and lax.ppermute only.
A program may use at most 256 MiB of HBM per device.

```python
import math
import jax
import jax.numpy as jnp
from jax import lax

D = 1024
FF = 4608
LENGTH = 1024
SEQUENCES_TOTAL = 32


def block_scale(rng, shape, split, smallest, top_value):
    def one(position, blocks):
        heights = jax.random.uniform(jax.random.fold_in(jax.random.fold_in(rng, 6), position), (blocks,), jnp.float32, smallest / len(split), top_value / len(split))
        return jnp.repeat(jnp.exp(heights), shape[position] // blocks).reshape((-1,) + (1,) * (len(shape) - position - 1))

    level = one(*split[0])
    for cut in split[1:]:
        level = level * one(*cut)
    return level


def bell_draw(own_key, extent, deviation, most, cuts=(), held_as=jnp.bfloat16):
    entries = deviation * jax.random.normal(own_key, extent, jnp.float32)
    if cuts:
        entries = entries * block_scale(own_key, extent, cuts, -0.22, 0.18)
    return jnp.clip(entries, -most, most).astype(held_as)


def setup_inputs(seed: int = 0) -> dict:
    splits = jax.random.split(jax.random.key(seed), 11)
    tokens = bell_draw(splits[0], (SEQUENCES_TOTAL, LENGTH, D), 1.0, 6.0, ((0, 16), (1, 2)))
    w_in = bell_draw(splits[1], (D, 3 * D), D ** -0.5, 0.1875, ((0, 16), (1, 2)))
    w_out = bell_draw(splits[2], (D, D), D ** -0.5, 0.1875, ((0, 16), (1, 2)))
    w_gate = bell_draw(splits[3], (D, FF), D ** -0.5, 0.1875, ((0, 16), (1, 2)))
    w_up = bell_draw(splits[4], (D, FF), D ** -0.5, 0.1875, ((0, 16), (1, 2)))
    w_down = bell_draw(splits[5], (FF, D), FF ** -0.5, 0.09375, ((0, 16), (1, 2)))
    gain_mix = jnp.clip(1.0 + 0.18 * jax.random.normal(splits[6], (D,), jnp.float32), 0.099609375, 1.8984375).astype(jnp.bfloat16)
    gain_ffn = jnp.clip(1.0 + 0.18 * jax.random.normal(splits[7], (D,), jnp.float32), 0.099609375, 1.8984375).astype(jnp.bfloat16)
    kernel = bell_draw(splits[8], (3, D), 3 ** -0.5, 3.5, ((1, 16),))
    cotangent = bell_draw(splits[9], (SEQUENCES_TOTAL, LENGTH, D), 1.0, 6.0, ((0, 16), (1, 2)))
    return dict(tokens=tokens, w_in=w_in, w_out=w_out, w_gate=w_gate, w_up=w_up, w_down=w_down, gain_mix=gain_mix, gain_ffn=gain_ffn, kernel=kernel, cotangent=cotangent)


@jax.custom_vjp
def low(v):
    return lax.optimization_barrier(v.astype(jnp.bfloat16)).astype(jnp.float32)

@jax.custom_vjp
def low_back(v):
    return v

def low_keep(v):
    return (low(v), None)

def low_pass(kept, grad):
    return (grad,)

def back_keep(v):
    return (v, None)

def back_low(kept, grad):
    return (low(grad),)
low.defvjp(low_keep, low_pass)
low_back.defvjp(back_keep, back_low)
EPSILON = 1e-05

def matmul(left_operand, right_operand):
    return jnp.einsum('mya,aw->myw', left_operand, right_operand, precision=lax.Precision.HIGHEST)

def rms_scale(values, gain):
    return values * lax.rsqrt(lax.optimization_barrier(jnp.mean(values * values, axis=-1, keepdims=True)) + EPSILON) * gain

def forward(params, inputs):
    w_in, w_out, w_gate, w_up, w_down, gain_mix, gain_ffn, kernel = params
    width = inputs.shape[-1]
    normed = low(rms_scale(inputs, gain_mix))
    projected = low_back(matmul(normed, w_in))
    gate_b = projected[..., :width]
    gate_c = projected[..., width:2 * width]
    values = projected[..., 2 * width:]
    product = gate_b * values
    padded = jnp.pad(product, ((0, 0), (2, 0), (0, 0)))
    convolved = kernel[0] * padded[:, :-2] + kernel[1] * padded[:, 1:-1] + kernel[2] * padded[:, 2:]
    mixer_out = low(gate_c * convolved)
    residual = inputs + low_back(matmul(mixer_out, w_out))
    feedforward_normed = low(rms_scale(residual, gain_ffn))
    gate = low_back(matmul(feedforward_normed, w_gate))
    up_value = low_back(matmul(feedforward_normed, w_up))
    hidden = low(jax.nn.silu(gate) * up_value)
    return residual + low_back(matmul(hidden, w_down))

def reference(tokens, w_in, w_out, w_gate, w_up, w_down, gain_mix, gain_ffn, kernel, cotangent):
    params = tuple((p.astype(jnp.float32) for p in (w_in, w_out, w_gate, w_up, w_down, gain_mix, gain_ffn, kernel)))
    seq_total, seq_len, width = tokens.shape
    group = math.gcd(seq_total, max(1, 4096 // seq_len))
    blocks = seq_total // group
    token_blocks = tokens.reshape(blocks, group, seq_len, width)
    cot_blocks = cotangent.reshape(blocks, group, seq_len, width)

    def step(total, block):
        token_block, cot_block = block
        output, pull = jax.vjp(forward, params, token_block.astype(jnp.float32))
        grads, grad_inputs = pull(cot_block.astype(jnp.float32))
        total = jax.tree.map(jnp.add, total, grads)
        return (total, (output.astype(jnp.bfloat16), grad_inputs))
    zeros = jax.tree.map(jnp.zeros_like, params)
    total, (outputs, grad_inputs) = lax.scan(step, zeros, (token_blocks, cot_blocks))
    result = outputs.reshape(seq_total, seq_len, width)
    grad_tokens = grad_inputs.reshape(seq_total, seq_len, width)
    return (result, grad_tokens, total[0], total[1], total[2], total[3], total[4], total[5], total[6], total[7])
```

```python
import functools
import jax
import jax.numpy as jnp
from jax import lax
from jax.experimental import pallas as pl
from jax.experimental.pallas import tpu as pltpu
from jax.sharding import Mesh
from jax.sharding import PartitionSpec as P

EPSILON = 1e-05
CHUNKS = 3
f32 = jnp.float32
bf16 = jnp.bfloat16


def passed_along(block, axis, distance):
    devices = range(lax.axis_size(axis))
    route = [(i - distance, i) for i in devices if i - distance in devices]
    return lax.ppermute(block, axis, route)


def cross_rows(left_operand, right_operand):
    return lax.dot_general(
        left_operand, right_operand, (((0,), (0,)), ((), ())), preferred_element_type=jnp.float32
    )


def cross_cols(left_operand, right_operand):
    return lax.dot_general(
        left_operand, right_operand, (((1,), (1,)), ((), ())), preferred_element_type=jnp.float32
    )


def norm_forward(values, gain):
    scale = lax.rsqrt(jnp.mean(values * values, axis=-1, keepdims=True) + EPSILON)
    return (values * scale * gain, scale)


def norm_backward(values, scale, gain, incoming):
    weighted = incoming * gain
    gain_grad = jnp.sum(incoming * values * scale, axis=0)
    inner = jnp.mean(weighted * values, axis=-1, keepdims=True)
    return (scale * weighted - values * (scale * scale * scale) * inner, gain_grad)


def plain_shards(tokens, w_in, w_out, w_gate, w_up, w_down, gain_mix, gain_ffn, kernel, cotangent):
    seq_count, piece_len, model_width = tokens.shape
    row_count = seq_count * piece_len
    small_params = jnp.concatenate([gain_mix[None], gain_ffn[None], kernel], axis=0)
    input_columns, out_cols, gate_cols, up_cols, down_cols = (
        lax.all_gather(w_in, "ctx", axis=1, tiled=True),
        lax.all_gather(w_out, "ctx", axis=1, tiled=True),
        lax.all_gather(w_gate, "ctx", axis=1, tiled=True),
        lax.all_gather(w_up, "ctx", axis=1, tiled=True),
        lax.all_gather(w_down, "ctx", axis=1, tiled=True),
    )
    full_in, full_out, full_gate, full_up, full_down, small_full = (
        lax.all_gather(input_columns, "dp", axis=0, tiled=True),
        lax.all_gather(out_cols, "dp", axis=0, tiled=True),
        lax.all_gather(gate_cols, "dp", axis=0, tiled=True),
        lax.all_gather(up_cols, "dp", axis=0, tiled=True),
        lax.all_gather(down_cols, "dp", axis=0, tiled=True),
        lax.all_gather(small_params, "dp", axis=1, tiled=True),
    )
    small_float = small_full.astype(jnp.float32)
    first_gain = small_float[0]
    second_gain = small_float[1]
    taps = small_float[2:5]
    inputs = tokens.reshape(row_count, model_width).astype(jnp.float32)
    normed, scale_mix = norm_forward(inputs, first_gain)
    normed_low = normed.astype(jnp.bfloat16)
    projected = jnp.dot(normed_low, full_in, preferred_element_type=jnp.float32)
    gate_b = projected[:, :model_width]
    gate_c = projected[:, model_width : 2 * model_width]
    values = projected[:, 2 * model_width :]
    product = (gate_b * values).reshape(seq_count, piece_len, model_width)
    previous = passed_along(product[:, piece_len - 2 :].astype(jnp.bfloat16), "ctx", 1).astype(
        jnp.float32
    )
    padded = jnp.concatenate([previous, product], axis=1)
    convolved = taps[0] * padded[:, :-2] + taps[1] * padded[:, 1:-1] + taps[2] * padded[:, 2:]
    convolved = convolved.reshape(row_count, model_width)
    mixer_out = (gate_c * convolved).astype(jnp.bfloat16)
    residual = inputs + jnp.dot(mixer_out, full_out, preferred_element_type=jnp.float32)
    feedforward_normed, scale_ffn = norm_forward(residual, second_gain)
    nffn_low = feedforward_normed.astype(jnp.bfloat16)
    gate = jnp.dot(nffn_low, full_gate, preferred_element_type=jnp.float32)
    up_value = jnp.dot(nffn_low, full_up, preferred_element_type=jnp.float32)
    sigmoid_gate = jax.nn.sigmoid(gate)
    activated = gate * sigmoid_gate
    hidden = (activated * up_value).astype(jnp.bfloat16)
    result = residual + jnp.dot(hidden, full_down, preferred_element_type=jnp.float32)
    result = result.astype(jnp.bfloat16).reshape(seq_count, piece_len, model_width)
    back_in, output_backward, back_gate, back_up, back_down = (
        lax.all_gather(w_in, "ctx", axis=1, tiled=True),
        lax.all_gather(w_out, "ctx", axis=1, tiled=True),
        lax.all_gather(w_gate, "ctx", axis=1, tiled=True),
        lax.all_gather(w_up, "ctx", axis=1, tiled=True),
        lax.all_gather(w_down, "ctx", axis=1, tiled=True),
    )
    input_weight_used, use_out, use_gate, use_up, use_down = (
        lax.all_gather(back_in, "dp", axis=0, tiled=True),
        lax.all_gather(output_backward, "dp", axis=0, tiled=True),
        lax.all_gather(back_gate, "dp", axis=0, tiled=True),
        lax.all_gather(back_up, "dp", axis=0, tiled=True),
        lax.all_gather(back_down, "dp", axis=0, tiled=True),
    )
    grad_out = cotangent.reshape(row_count, model_width)
    grad_out_float = grad_out.astype(jnp.float32)
    grad_w_down = cross_rows(hidden, grad_out)
    grad_hidden = cross_cols(grad_out, use_down)
    grad_gate = (
        grad_hidden * up_value * sigmoid_gate * (1.0 + gate * (1.0 - sigmoid_gate))
    ).astype(jnp.bfloat16)
    grad_up = (grad_hidden * activated).astype(jnp.bfloat16)
    grad_w_gate = cross_rows(nffn_low, grad_gate)
    grad_w_up = cross_rows(nffn_low, grad_up)
    grad_nffn = cross_cols(grad_gate, use_gate) + cross_cols(grad_up, use_up)
    residual_norm_gradient, grad_gain_ffn = norm_backward(
        residual, scale_ffn, second_gain, grad_nffn
    )
    grad_residual = grad_out_float + residual_norm_gradient
    grad_branch = grad_residual.astype(jnp.bfloat16)
    grad_w_out = cross_rows(mixer_out, grad_branch)
    grad_mix = cross_cols(grad_branch, use_out)
    grad_c = grad_mix * convolved
    grad_conv = (grad_mix * gate_c).reshape(seq_count, piece_len, model_width)
    following = passed_along(grad_conv[:, :2].astype(jnp.bfloat16), "ctx", -1).astype(jnp.float32)
    extended = jnp.concatenate([grad_conv, following], axis=1)
    grad_product = (
        taps[2] * extended[:, :-2] + taps[1] * extended[:, 1:-1] + taps[0] * extended[:, 2:]
    )
    grad_kernel = jnp.stack(
        [
            jnp.sum(grad_conv * padded[:, shift_at : shift_at + piece_len], axis=(0, 1))
            for shift_at in range(3)
        ],
        axis=0,
    )
    grad_product = grad_product.reshape(row_count, model_width)
    grad_projected = jnp.concatenate(
        [grad_product * values, grad_c, grad_product * gate_b], axis=1
    ).astype(jnp.bfloat16)
    grad_w_in = cross_rows(normed_low, grad_projected)
    grad_normed = cross_cols(grad_projected, input_weight_used)
    grad_in_norm, grad_gain_mix = norm_backward(inputs, scale_mix, first_gain, grad_normed)
    grad_tokens = (grad_residual + grad_in_norm).reshape(seq_count, piece_len, model_width)
    small_grad = jnp.concatenate([grad_gain_mix[None], grad_gain_ffn[None], grad_kernel], axis=0)
    part_in, part_out, part_gate, part_up, part_down, small_part = (
        lax.psum_scatter(grad_w_in, "dp", scatter_dimension=0, tiled=True),
        lax.psum_scatter(grad_w_out, "dp", scatter_dimension=0, tiled=True),
        lax.psum_scatter(grad_w_gate, "dp", scatter_dimension=0, tiled=True),
        lax.psum_scatter(grad_w_up, "dp", scatter_dimension=0, tiled=True),
        lax.psum_scatter(grad_w_down, "dp", scatter_dimension=0, tiled=True),
        lax.psum_scatter(small_grad, "dp", scatter_dimension=1, tiled=True),
    )
    final_in, final_out, final_gate, final_up, final_down = (
        lax.psum_scatter(part_in, "ctx", scatter_dimension=1, tiled=True),
        lax.psum_scatter(part_out, "ctx", scatter_dimension=1, tiled=True),
        lax.psum_scatter(part_gate, "ctx", scatter_dimension=1, tiled=True),
        lax.psum_scatter(part_up, "ctx", scatter_dimension=1, tiled=True),
        lax.psum_scatter(part_down, "ctx", scatter_dimension=1, tiled=True),
    )
    small_total = lax.psum(small_part, "ctx")
    return (
        result,
        grad_tokens,
        final_in,
        final_out,
        final_gate,
        final_up,
        final_down,
        small_total[0],
        small_total[1],
        small_total[2:5],
    )


NT = (((1,), (1,)), ((), ()))
TN = (((0,), (0,)), ((), ()))


def swap(block):
    return lax.ppermute(block, "core", [(0, 1), (1, 0)])


def across(block, mask):
    count = lax.axis_size("chip") * lax.axis_size("ctx")
    return lax.ppermute(block, ("chip", "ctx"), [(i, i ^ mask) for i in range(count)])


def bit_masks():
    n_chip, n_ctx = lax.axis_size("chip"), lax.axis_size("ctx")
    ctx_bits = [1 << b for b in range(n_ctx.bit_length() - 1)]
    near = [n_ctx]
    far = [n_ctx << b for b in range(1, n_chip.bit_length() - 1)]
    return far, near + ctx_bits, ctx_bits + near


def after(value, *done):
    return lax.optimization_barrier((value, *done))[0]


def gather_plan(cut, total):
    far, first_order, second_order = bit_masks()
    plan = []
    for operand, order, row0, rows in ((0, first_order, 0, cut), (2, second_order, cut, total - cut)):
        masks = [0]
        for mask in far + order[:-1]:
            masks = masks + [m ^ mask for m in masks]
        for index, mask in enumerate(masks):
            plan.append((operand, index, mask, row0, rows))
            plan.append((operand + 1, index, mask ^ order[-1], row0, rows))
    return plan


def gather(block, cut):
    far, first_order, second_order = bit_masks()
    hold = block[None]
    for mask in far:
        hold = jnp.concatenate([hold, across(hold, mask)], axis=0)
    parts = []
    for order, half in ((first_order, hold[:, :cut]), (second_order, hold[:, cut:])):
        for mask in order[:-1]:
            half = jnp.concatenate([half, across(half, mask)], axis=0)
        parts += [half, across(half, order[-1])]
    return parts


def scatter_sum(parts, ties=()):
    far, first_order, second_order = bit_masks()
    ties = dict(enumerate(ties))

    def sent(block, mask, step):
        block = block.astype(bf16)
        if ties.get(step) is not None:
            block = after(block, ties[step])
        return across(block, mask).astype(f32)

    halves = []
    for order, keep, send in ((first_order, parts[0], parts[1]), (second_order, parts[2], parts[3])):
        keep = keep.astype(f32) + sent(send, order[-1], 0)
        for step, mask in enumerate(reversed(order[:-1])):
            mid = keep.shape[0] // 2
            keep = keep[:mid] + sent(keep[mid:], mask, step + 1)
        halves.append(keep)
    keep = jnp.concatenate(halves, axis=1)
    for step, mask in enumerate(reversed(far)):
        mid = keep.shape[0] // 2
        keep = keep[:mid] + sent(keep[mid:], mask, len(first_order) + step)
    return keep[0]


def slot_pairs(own, plan, refs, segments, n_ctx, targets):
    pairs = []
    for operand, index, mask, row0, nrows in plan:
        slot = index if mask is None else jnp.bitwise_xor(own, mask)
        y = lax.rem(slot, n_ctx)
        chip = lax.div(slot, n_ctx)
        src = refs[operand].at[index]
        for seg_row, seg_rows, lane0, lanes, target, row_step, row_add, lane_step, lane_add in segments:
            low, high = max(seg_row, row0), min(seg_row + seg_rows, row0 + nrows)
            if low >= high:
                continue
            row = pl.multiple_of(chip * row_step + row_add + (low - seg_row), 16)
            lane = pl.multiple_of(y * lane_step + lane_add, 128)
            pairs.append(
                (
                    src.at[pl.ds(low - row0, high - low), pl.ds(lane0, lanes)],
                    targets[target].at[pl.ds(row, high - low), pl.ds(lane, lanes)],
                )
            )
    return pairs


def copy_all(pairs, sems):
    copies = [pltpu.make_async_copy(a, b, sems.at[i]) for i, (a, b) in enumerate(pairs)]
    for copy in copies:
        copy.start()
    for copy in copies:
        copy.wait()


def part_count(plan):
    return 1 + max(entry[0] for entry in plan)


def part_shapes(plan, lanes):
    shapes = {}
    for operand, index, _, _, rows in plan:
        shapes[operand] = (max(index + 1, shapes.get(operand, (0,))[0]), rows, lanes)
    return [shapes[operand] for operand in sorted(shapes)]


def ffn_kernel(geometry, out_geometry, first, own_ref, n_ref, go_ref, *refs):
    plan, segments, n_ctx = geometry
    out_plan = out_geometry[0]
    count, out_count = part_count(plan), part_count(out_plan)
    weights, refs = refs[:count], refs[count:]
    if not first:
        res_in, gn_in = refs[:2]
        refs = refs[2:]
    res_ref, gn_ref = refs[:2]
    grads, refs = refs[2 : 2 + out_count], refs[2 + out_count :]
    gate_m, up_m, down_m, d_gate, d_up, d_down, h_m, gg_m, gu_m, sems = refs
    own = own_ref[0]
    targets = (gate_m, up_m, down_m)

    @pl.when(pl.program_id(0) == 0)
    def _():
        d_gate[...] = jnp.zeros_like(d_gate)
        d_up[...] = jnp.zeros_like(d_up)
        d_down[...] = jnp.zeros_like(d_down)
        copy_all(slot_pairs(own, plan, weights, segments, n_ctx, targets), sems)

    n = n_ref[...]
    go = go_ref[...]
    hidden_count = gate_m.shape[1]
    step = 256
    for start in range(0, hidden_count, step):
        cols = slice(start, start + step)
        g = jnp.dot(n, gate_m[:, cols], preferred_element_type=f32)
        u = jnp.dot(n, up_m[:, cols], preferred_element_type=f32)
        gh = lax.dot_general(go, down_m[cols, :], NT, preferred_element_type=f32)
        s = jax.nn.sigmoid(g)
        act = g * s
        h_m[:, cols] = (act * u).astype(bf16)
        gg_m[:, cols] = (gh * u * s * (1.0 + g * (1.0 - s))).astype(bf16)
        gu_m[:, cols] = (gh * act).astype(bf16)
    res = jnp.dot(h_m[...], down_m[...], preferred_element_type=f32)
    gn = lax.dot_general(gg_m[...], gate_m[...], NT, preferred_element_type=f32)
    gn = gn + lax.dot_general(gu_m[...], up_m[...], NT, preferred_element_type=f32)
    if not first:
        res = res_in[...] + res
        gn = gn_in[...] + gn
    res_ref[...] = res
    gn_ref[...] = gn
    d_gate[...] += lax.dot_general(n, gg_m[...], TN, preferred_element_type=f32)
    d_up[...] += lax.dot_general(n, gu_m[...], TN, preferred_element_type=f32)
    d_down[...] += lax.dot_general(h_m[...], go, TN, preferred_element_type=f32)

    @pl.when(pl.program_id(0) == pl.num_programs(0) - 1)
    def _():
        gate_m[...] = d_gate[...].astype(bf16)
        up_m[...] = d_up[...].astype(bf16)
        down_m[...] = d_down[...].astype(bf16)
        pairs = slot_pairs(own, out_plan, grads, segments, n_ctx, targets)
        copy_all([(b, a) for a, b in pairs], sems)


def ffn_chunk(own, nffn, go, weights, totals, geometry, out_geometry, hidden_count, rows=256):
    total, width = nffn.shape
    first = totals is None
    plan, segments, _ = geometry
    out_plan = out_geometry[0]
    count, out_count = part_count(plan), part_count(out_plan)
    lanes = weights[0].shape[-1]
    row_spec = pl.BlockSpec((rows, width), lambda i, o: (i, 0))
    any_spec = pl.BlockSpec(memory_space=pl.ANY)
    outs = pl.pallas_call(
        functools.partial(ffn_kernel, geometry, out_geometry, first),
        out_shape=[jax.ShapeDtypeStruct((total, width), f32)] * 2
        + [jax.ShapeDtypeStruct(s, bf16) for s in part_shapes(out_plan, lanes)],
        grid_spec=pltpu.PrefetchScalarGridSpec(
            num_scalar_prefetch=1,
            grid=(total // rows,),
            in_specs=[row_spec] * 2 + [any_spec] * count + [row_spec] * (0 if first else 2),
            out_specs=[row_spec] * 2 + [any_spec] * out_count,
            scratch_shapes=[
                pltpu.VMEM((width, hidden_count), bf16),
                pltpu.VMEM((width, hidden_count), bf16),
                pltpu.VMEM((hidden_count, width), bf16),
                pltpu.VMEM((width, hidden_count), f32),
                pltpu.VMEM((width, hidden_count), f32),
                pltpu.VMEM((hidden_count, width), f32),
                pltpu.VMEM((rows, hidden_count), bf16),
                pltpu.VMEM((rows, hidden_count), bf16),
                pltpu.VMEM((rows, hidden_count), bf16),
                pltpu.SemaphoreType.DMA((max(len(plan), len(out_plan)) * len(segments),)),
            ],
        ),
        input_output_aliases={} if first else {3 + count: 0, 4 + count: 1},
        compiler_params=pltpu.CompilerParams(
            vmem_limit_bytes=56 * 1024 * 1024, dimension_semantics=("arbitrary",)
        ),
        cost_estimate=pl.CostEstimate(
            flops=18 * total * width * hidden_count,
            bytes_accessed=20 * total * width,
            transcendentals=total * hidden_count,
        ),
    )(own, nffn, go, *weights, *(() if first else totals))
    return (outs[0], outs[1]), outs[2:]


def move_kernel(geometry, count, outward, own_ref, *refs):
    plan, segments, n_ctx = geometry
    sems = refs[-1]
    refs = refs[:-1]
    if outward:
        targets, parts = refs[: len(refs) - count], refs[len(refs) - count :]
    else:
        parts, targets = refs[:count], refs[count:]
    pairs = slot_pairs(own_ref[0], plan, parts, segments, n_ctx, targets)
    copy_all([(b, a) for a, b in pairs] if outward else pairs, sems)


def move(own, arrays, shapes, geometry, count, outward):
    plan, segments, _ = geometry
    any_spec = pl.BlockSpec(memory_space=pl.ANY)
    vmem_spec = pl.BlockSpec(memory_space=pltpu.VMEM)
    return pl.pallas_call(
        functools.partial(move_kernel, geometry, count, outward),
        out_shape=[jax.ShapeDtypeStruct(s, bf16) for s in shapes],
        in_specs=[pl.BlockSpec(memory_space=pltpu.SMEM)]
        + [vmem_spec if outward else any_spec] * len(arrays),
        out_specs=[any_spec if outward else vmem_spec] * len(shapes),
        scratch_shapes=[pltpu.SemaphoreType.DMA((len(plan) * len(segments),))],
        compiler_params=pltpu.CompilerParams(vmem_limit_bytes=24 * 1024 * 1024),
        cost_estimate=pl.CostEstimate(flops=0, bytes_accessed=1 << 24, transcendentals=0),
    )(own, *arrays)


def fits(tokens, w_in, w_out, w_gate, w_down, n_dp, n_ctx):
    width, hidden = w_gate.shape
    if n_dp % 2 or n_dp % (2 * n_ctx) or n_dp & (n_dp - 1) or n_ctx & (n_ctx - 1) or n_ctx < 2:
        return False
    depth = width // n_dp
    if width % n_dp or hidden % (n_dp * CHUNKS * 48) or w_in.shape[1] % (2 * n_ctx * 256):
        return False
    lanes = hidden // n_dp // CHUNKS * (n_dp // n_ctx // 2)
    wide = width // n_ctx
    return (
        lanes % 128 == 0
        and wide == lanes + 128
        and lanes == 384
        and wide % 256 == 0
        and depth % 16 == 0
        and 2 * depth <= 256
        and (w_in.shape[1] // n_ctx) % (2 * depth) == 0
        and width % (2 * depth) == 0
        and tokens.shape[1] % n_ctx == 0
    )


def fast_shards(tokens, w_in, w_out, w_gate, w_up, w_down, gain_mix, gain_ffn, kernel, cotangent):
    seqs, piece, width = tokens.shape
    rows = seqs * piece
    n_chip, n_ctx = lax.axis_size("chip"), lax.axis_size("ctx")
    slots = n_chip * n_ctx
    core = lax.axis_index("core")
    own_slot = lax.axis_index("chip") * n_ctx + lax.axis_index("ctx")
    own = own_slot.astype(jnp.int32)[None]
    depth = w_in.shape[0]
    groups = n_chip // n_ctx
    sub = w_down.shape[0] // CHUNKS
    lanes = groups * sub
    wide = w_out.shape[1]
    in_cols = w_in.shape[1] // 2
    in_parts, out_parts = in_cols // 256, wide // 256
    hidden_count = n_chip * sub
    channels = width // 2

    def mine_other(pair):
        return jnp.where(core == 0, pair[0], pair[1]), jnp.where(core == 0, pair[1], pair[0])

    def in_core_order(mine, other, axis):
        return jnp.where(
            core == 0,
            jnp.concatenate([mine, other], axis=axis),
            jnp.concatenate([other, mine], axis=axis),
        )

    small = jnp.concatenate([gain_mix[None], gain_ffn[None], kernel], axis=0)
    in_pair = w_in.reshape(depth, in_cols // depth, 2, depth).transpose(2, 0, 1, 3)
    in_pair = in_pair.reshape(2, depth, in_parts, 256).transpose(0, 2, 1, 3)
    in_mine, in_other = mine_other(in_pair)
    small_rows = jnp.pad(small, ((0, 11), (0, 256 - depth)))
    swapped = swap(jnp.concatenate([in_other.reshape(in_parts * depth, 256), small_rows], axis=0))
    in_got = swapped[: in_parts * depth].reshape(in_parts, depth, 256)
    in_block = in_core_order(in_mine, in_got, 1).reshape(in_parts * 2 * depth, 256)
    small_block = in_core_order(small, swapped[in_parts * depth :][:5, :depth], 1)
    small_block = jnp.pad(small_block, ((0, 11), (0, 256 - 2 * depth)))
    out_block = w_out.reshape(depth, out_parts, 256).transpose(1, 0, 2).reshape(-1, 256)
    mix_block = jnp.concatenate([in_block, out_block, small_block], axis=0)

    both = jnp.stack([w_gate, w_up]).reshape(2, depth, groups, 2, CHUNKS, sub)
    both = both.transpose(3, 4, 0, 1, 2, 5).reshape(2, CHUNKS, 2, depth, lanes)
    both_mine, both_other = mine_other(both)
    both_block = in_core_order(both_mine, swap(both_other), 2)
    both_block = both_block.reshape(CHUNKS, 4 * depth, lanes)
    down = w_down.reshape(CHUNKS, sub, wide)
    down_rest = down[:, :, lanes:].reshape(CHUNKS, 3, sub // 3, 128).transpose(0, 2, 1, 3)
    chunk_blocks = jnp.concatenate(
        [both_block, down[:, :, :lanes], down_rest.reshape(CHUNKS, sub // 3, lanes)], axis=1
    )

    mix_rows = mix_block.shape[0]
    mix_cut = 256
    in_rows = in_parts * 2 * depth
    mix_segments = [
        (k * 2 * depth, 2 * depth, 0, 256, 0, 2 * depth, 0, in_cols, 256 * k)
        for k in range(in_parts)
    ]
    mix_segments += [
        (in_rows + k * depth, depth, 0, 256, 1, depth, 0, wide, 256 * k) for k in range(out_parts)
    ]
    small_segment = (in_rows + out_parts * depth, 16, 0, 256, 2, 16, 0, 256, 0)
    mix_plan = gather_plan(mix_cut, mix_rows)
    chunk_rows = chunk_blocks.shape[1]
    chunk_cut = chunk_rows // 2
    chunk_segments = [
        (0, 2 * depth, 0, lanes, 0, 2 * depth, 0, lanes, 0),
        (2 * depth, 2 * depth, 0, lanes, 1, 2 * depth, 0, lanes, 0),
        (4 * depth, sub, 0, lanes, 2, sub, 0, wide, 0),
    ] + [
        (4 * depth + sub, sub // 3, 128 * k, 128, 2, sub, k * (sub // 3), wide, lanes)
        for k in range(3)
    ]
    whole_plan = [(0, i, None, 0, chunk_rows) for i in range(slots)]
    whole_geometry = (whole_plan, chunk_segments, n_ctx)
    step_geometry = (gather_plan(chunk_cut, chunk_rows), chunk_segments, n_ctx)

    mix_parts = gather(mix_block, mix_cut)
    chunk_weights = [[lax.all_gather(chunk_blocks[q], ("chip", "ctx"))] for q in range(CHUNKS)]
    in_half, out_half, small_all = move(
        own,
        mix_parts,
        [(width, n_ctx * in_cols), (channels, width), (n_chip * 16, n_ctx * 256)],
        (mix_plan, mix_segments + [small_segment], n_ctx),
        4,
        False,
    )
    small_all = small_all.reshape(n_chip, 16, n_ctx * 256)[:, :5, : 2 * depth].astype(f32)
    first_gain = small_all[:, 0].reshape(width)
    second_gain = small_all[:, 1].reshape(width)
    taps = small_all[:, 2:].reshape(n_chip, 3, 2, depth)
    taps = jnp.where(core == 0, taps[:, :, 0], taps[:, :, 1]).transpose(1, 0, 2)
    taps = taps.reshape(3, channels)

    token_rows = tokens.reshape(rows, width)
    inputs = jnp.concatenate([token_rows, swap(token_rows)], axis=0).astype(f32)
    go_rows = cotangent.reshape(rows, width)
    go = jnp.concatenate([go_rows, swap(go_rows)], axis=0)
    normed, scale_mix = norm_forward(inputs, first_gain)
    normed_low = normed.astype(bf16)
    projected = jnp.dot(normed_low, in_half, preferred_element_type=f32)
    gate_b = projected[:, :channels]
    gate_c = projected[:, channels : 2 * channels]
    values = projected[:, 2 * channels :]
    product = (gate_b * values).reshape(2 * seqs, piece, channels)
    previous = passed_along(product[:, piece - 2 :].astype(bf16), "ctx", 1).astype(f32)
    padded = jnp.concatenate([previous, product], axis=1)
    convolved = taps[0] * padded[:, :-2] + taps[1] * padded[:, 1:-1] + taps[2] * padded[:, 2:]
    convolved = convolved.reshape(2 * rows, channels)
    mixer_out = (gate_c * convolved).astype(bf16)
    branch = jnp.dot(mixer_out, out_half, preferred_element_type=f32)

    def swap_rows(block):
        got = swap(block.astype(bf16)).astype(f32)
        return jnp.concatenate([got[rows:], got[:rows]], axis=0)

    residual = inputs + (branch + swap_rows(branch))
    feedforward_normed, scale_ffn = norm_forward(residual, second_gain)
    nffn_low = feedforward_normed.astype(bf16)

    totals = None
    chunk_parts = []
    for q in range(CHUNKS):
        steps = q == CHUNKS - 1
        totals, parts = ffn_chunk(
            own, nffn_low, go, chunk_weights[q], totals, whole_geometry,
            step_geometry if steps else whole_geometry, hidden_count,
        )
        chunk_parts.append(parts)
    chunk_grads = [
        lax.psum_scatter(parts[0], ("chip", "ctx"), scatter_dimension=0).astype(f32)
        for parts in chunk_parts[:-1]
    ]
    ffn_out, grad_nffn = totals
    grad_nffn = grad_nffn + swap_rows(grad_nffn)
    result = residual[:rows] + (ffn_out[:rows] + swap(ffn_out[rows:].astype(bf16)).astype(f32))
    result = result.astype(bf16).reshape(seqs, piece, width)

    weighted = grad_nffn * second_gain
    grad_gain_ffn = jnp.sum((grad_nffn * residual * scale_ffn)[:rows], axis=0)
    inner = jnp.mean(weighted * residual, axis=-1, keepdims=True)
    grad_residual = go.astype(f32) + (
        scale_ffn * weighted - residual * (scale_ffn * scale_ffn * scale_ffn) * inner
    )
    grad_branch = grad_residual.astype(bf16)
    grad_w_out = cross_rows(mixer_out, grad_branch).astype(bf16)
    grad_mix = cross_cols(grad_branch, out_half)
    grad_c = grad_mix * convolved
    grad_conv = (grad_mix * gate_c).reshape(2 * seqs, piece, channels)
    following = passed_along(grad_conv[:, :2].astype(bf16), "ctx", -1).astype(f32)
    extended = jnp.concatenate([grad_conv, following], axis=1)
    grad_product = (
        taps[2] * extended[:, :-2] + taps[1] * extended[:, 1:-1] + taps[0] * extended[:, 2:]
    )
    grad_kernel = jnp.stack(
        [jnp.sum(grad_conv * padded[:, k : k + piece], axis=(0, 1)) for k in range(3)], axis=0
    )
    grad_product = grad_product.reshape(2 * rows, channels)
    grad_projected = jnp.concatenate(
        [grad_product * values, grad_c, grad_product * gate_b], axis=1
    ).astype(bf16)
    last_sum = scatter_sum(chunk_parts[-1], (None, grad_branch, grad_conv, grad_projected))
    grad_w_in = cross_rows(normed_low, grad_projected).astype(bf16)
    mix_grad_parts = move(
        own,
        [grad_w_in, grad_w_out],
        [(slots // 2, mix_cut, 256)] * 2 + [(slots // 2, in_rows + out_parts * depth - mix_cut, 256)] * 2,
        (gather_plan(mix_cut, in_rows + out_parts * depth), mix_segments, n_ctx),
        4,
        True,
    )
    mix_sum = scatter_sum(mix_grad_parts)
    grad_normed = cross_cols(grad_projected, in_half)
    grad_normed = grad_normed[:rows] + swap(grad_normed[rows:].astype(bf16)).astype(f32)
    grad_in_norm, grad_gain_mix = norm_backward(
        inputs[:rows], scale_mix[:rows], first_gain, grad_normed
    )
    grad_tokens = (grad_residual[:rows] + grad_in_norm).reshape(seqs, piece, width)

    chunk_sum = jnp.stack(chunk_grads + [last_sum])
    both_sum = chunk_sum[:, : 4 * depth].reshape(CHUNKS, 2, 2, depth, lanes).transpose(2, 0, 1, 3, 4)
    both_mine, both_other = mine_other(both_sum)
    both_got = swap(both_other)
    both_sum = in_core_order(both_mine[None], both_got[None], 0)
    both_sum = both_sum.reshape(2, CHUNKS, 2, depth, groups, sub).transpose(2, 3, 4, 0, 1, 5)
    both_sum = both_sum.reshape(2, depth, 2 * CHUNKS * lanes)
    down_rest = chunk_sum[:, 4 * depth + sub :].reshape(CHUNKS, sub // 3, 3, 128)
    down_rest = down_rest.transpose(0, 2, 1, 3).reshape(CHUNKS, sub, 128)
    final_down = jnp.concatenate([chunk_sum[:, 4 * depth : 4 * depth + sub], down_rest], axis=2)
    final_down = final_down.reshape(CHUNKS * sub, wide)

    in_sum = mix_sum[:in_rows].reshape(in_parts, 2, depth, 256).transpose(1, 0, 2, 3)
    in_mine, in_other = mine_other(in_sum)
    in_sum = in_core_order(in_mine[None], swap(in_other)[None], 0)
    in_sum = in_sum.transpose(0, 2, 1, 3).reshape(2, depth, in_cols // depth, depth)
    final_in = in_sum.transpose(1, 2, 0, 3).reshape(depth, 2 * in_cols)
    final_out = mix_sum[in_rows:].reshape(out_parts, depth, 256).transpose(1, 0, 2)
    final_out = final_out.reshape(depth, wide)

    grad_taps = grad_kernel.reshape(3, n_chip, 1, depth)
    grad_taps = jnp.where(
        jnp.arange(2).reshape(1, 1, 2, 1) == core, grad_taps, jnp.zeros_like(grad_taps)
    ).reshape(3, width)
    small_grad = jnp.concatenate([grad_gain_mix[None], grad_gain_ffn[None], grad_taps], axis=0)
    small_sum = lax.psum_scatter(small_grad, ("chip", "core"), scatter_dimension=1, tiled=True)
    for bit in range(n_ctx.bit_length() - 1):
        route = [(i, i ^ (1 << bit)) for i in range(n_ctx)]
        small_sum = small_sum + lax.ppermute(small_sum, "ctx", route)
    return (
        result,
        grad_tokens,
        final_in,
        final_out,
        both_sum[0],
        both_sum[1],
        final_down,
        small_sum[0],
        small_sum[1],
        small_sum[2:5],
    )


def solution(mesh):
    n_dp, n_ctx = mesh.shape["dp"], mesh.shape["ctx"]

    def placed(dp):
        whole, cut = P(dp, "ctx", None), P(dp, "ctx")
        ins = (whole, cut, cut, cut, cut, cut, P(dp), P(dp), P(None, dp), whole)
        outs = (whole, whole, cut, cut, cut, cut, cut, P(dp), P(dp), P(None, dp))
        return ins, outs

    def run(tokens, w_in, w_out, w_gate, w_up, w_down, gain_mix, gain_ffn, kernel, cotangent):
        if fits(tokens, w_in, w_out, w_gate, w_down, n_dp, n_ctx):
            cut_mesh = Mesh(mesh.devices.reshape(n_dp // 2, 2, n_ctx), ("chip", "core", "ctx"))
            body, on, (ins, outs) = fast_shards, cut_mesh, placed(("chip", "core"))
        else:
            body, on, (ins, outs) = plain_shards, mesh, placed("dp")
        call = jax.shard_map(body, mesh=on, in_specs=ins, out_specs=outs, check_vma=False)
        return call(
            tokens, w_in, w_out, w_gate, w_up, w_down, gain_mix, gain_ffn, kernel, cotangent
        )

    return run
```

```python
import functools
import jax
import jax.numpy as jnp
from jax import lax
from jax.experimental import pallas as pl
from jax.experimental.pallas import tpu as pltpu
from jax.sharding import Mesh
from jax.sharding import PartitionSpec as P

EPSILON = 1e-05
CHUNKS = 3
f32 = jnp.float32
bf16 = jnp.bfloat16


def passed_along(block, axis, distance):
    devices = range(lax.axis_size(axis))
    route = [(i - distance, i) for i in devices if i - distance in devices]
    return lax.ppermute(block, axis, route)


def cross_rows(left_operand, right_operand):
    return lax.dot_general(
        left_operand, right_operand, (((0,), (0,)), ((), ())), preferred_element_type=jnp.float32
    )


def cross_cols(left_operand, right_operand):
    return lax.dot_general(
        left_operand, right_operand, (((1,), (1,)), ((), ())), preferred_element_type=jnp.float32
    )


def norm_forward(values, gain):
    scale = lax.rsqrt(jnp.mean(values * values, axis=-1, keepdims=True) + EPSILON)
    return (values * scale * gain, scale)


def norm_backward(values, scale, gain, incoming):
    weighted = incoming * gain
    gain_grad = jnp.sum(incoming * values * scale, axis=0)
    inner = jnp.mean(weighted * values, axis=-1, keepdims=True)
    return (scale * weighted - values * (scale * scale * scale) * inner, gain_grad)


def plain_shards(tokens, w_in, w_out, w_gate, w_up, w_down, gain_mix, gain_ffn, kernel, cotangent):
    seq_count, piece_len, model_width = tokens.shape
    row_count = seq_count * piece_len
    small_params = jnp.concatenate([gain_mix[None], gain_ffn[None], kernel], axis=0)
    input_columns, out_cols, gate_cols, up_cols, down_cols = (
        lax.all_gather(w_in, "ctx", axis=1, tiled=True),
        lax.all_gather(w_out, "ctx", axis=1, tiled=True),
        lax.all_gather(w_gate, "ctx", axis=1, tiled=True),
        lax.all_gather(w_up, "ctx", axis=1, tiled=True),
        lax.all_gather(w_down, "ctx", axis=1, tiled=True),
    )
    full_in, full_out, full_gate, full_up, full_down, small_full = (
        lax.all_gather(input_columns, "dp", axis=0, tiled=True),
        lax.all_gather(out_cols, "dp", axis=0, tiled=True),
        lax.all_gather(gate_cols, "dp", axis=0, tiled=True),
        lax.all_gather(up_cols, "dp", axis=0, tiled=True),
        lax.all_gather(down_cols, "dp", axis=0, tiled=True),
        lax.all_gather(small_params, "dp", axis=1, tiled=True),
    )
    small_float = small_full.astype(jnp.float32)
    first_gain = small_float[0]
    second_gain = small_float[1]
    taps = small_float[2:5]
    inputs = tokens.reshape(row_count, model_width).astype(jnp.float32)
    normed, scale_mix = norm_forward(inputs, first_gain)
    normed_low = normed.astype(jnp.bfloat16)
    projected = jnp.dot(normed_low, full_in, preferred_element_type=jnp.float32)
    gate_b = projected[:, :model_width]
    gate_c = projected[:, model_width : 2 * model_width]
    values = projected[:, 2 * model_width :]
    product = (gate_b * values).reshape(seq_count, piece_len, model_width)
    previous = passed_along(product[:, piece_len - 2 :].astype(jnp.bfloat16), "ctx", 1).astype(
        jnp.float32
    )
    padded = jnp.concatenate([previous, product], axis=1)
    convolved = taps[0] * padded[:, :-2] + taps[1] * padded[:, 1:-1] + taps[2] * padded[:, 2:]
    convolved = convolved.reshape(row_count, model_width)
    mixer_out = (gate_c * convolved).astype(jnp.bfloat16)
    residual = inputs + jnp.dot(mixer_out, full_out, preferred_element_type=jnp.float32)
    feedforward_normed, scale_ffn = norm_forward(residual, second_gain)
    nffn_low = feedforward_normed.astype(jnp.bfloat16)
    gate = jnp.dot(nffn_low, full_gate, preferred_element_type=jnp.float32)
    up_value = jnp.dot(nffn_low, full_up, preferred_element_type=jnp.float32)
    sigmoid_gate = jax.nn.sigmoid(gate)
    activated = gate * sigmoid_gate
    hidden = (activated * up_value).astype(jnp.bfloat16)
    result = residual + jnp.dot(hidden, full_down, preferred_element_type=jnp.float32)
    result = result.astype(jnp.bfloat16).reshape(seq_count, piece_len, model_width)
    back_in, output_backward, back_gate, back_up, back_down = (
        lax.all_gather(w_in, "ctx", axis=1, tiled=True),
        lax.all_gather(w_out, "ctx", axis=1, tiled=True),
        lax.all_gather(w_gate, "ctx", axis=1, tiled=True),
        lax.all_gather(w_up, "ctx", axis=1, tiled=True),
        lax.all_gather(w_down, "ctx", axis=1, tiled=True),
    )
    input_weight_used, use_out, use_gate, use_up, use_down = (
        lax.all_gather(back_in, "dp", axis=0, tiled=True),
        lax.all_gather(output_backward, "dp", axis=0, tiled=True),
        lax.all_gather(back_gate, "dp", axis=0, tiled=True),
        lax.all_gather(back_up, "dp", axis=0, tiled=True),
        lax.all_gather(back_down, "dp", axis=0, tiled=True),
    )
    grad_out = cotangent.reshape(row_count, model_width)
    grad_out_float = grad_out.astype(jnp.float32)
    grad_w_down = cross_rows(hidden, grad_out)
    grad_hidden = cross_cols(grad_out, use_down)
    grad_gate = (
        grad_hidden * up_value * sigmoid_gate * (1.0 + gate * (1.0 - sigmoid_gate))
    ).astype(jnp.bfloat16)
    grad_up = (grad_hidden * activated).astype(jnp.bfloat16)
    grad_w_gate = cross_rows(nffn_low, grad_gate)
    grad_w_up = cross_rows(nffn_low, grad_up)
    grad_nffn = cross_cols(grad_gate, use_gate) + cross_cols(grad_up, use_up)
    residual_norm_gradient, grad_gain_ffn = norm_backward(
        residual, scale_ffn, second_gain, grad_nffn
    )
    grad_residual = grad_out_float + residual_norm_gradient
    grad_branch = grad_residual.astype(jnp.bfloat16)
    grad_w_out = cross_rows(mixer_out, grad_branch)
    grad_mix = cross_cols(grad_branch, use_out)
    grad_c = grad_mix * convolved
    grad_conv = (grad_mix * gate_c).reshape(seq_count, piece_len, model_width)
    following = passed_along(grad_conv[:, :2].astype(jnp.bfloat16), "ctx", -1).astype(jnp.float32)
    extended = jnp.concatenate([grad_conv, following], axis=1)
    grad_product = (
        taps[2] * extended[:, :-2] + taps[1] * extended[:, 1:-1] + taps[0] * extended[:, 2:]
    )
    grad_kernel = jnp.stack(
        [
            jnp.sum(grad_conv * padded[:, shift_at : shift_at + piece_len], axis=(0, 1))
            for shift_at in range(3)
        ],
        axis=0,
    )
    grad_product = grad_product.reshape(row_count, model_width)
    grad_projected = jnp.concatenate(
        [grad_product * values, grad_c, grad_product * gate_b], axis=1
    ).astype(jnp.bfloat16)
    grad_w_in = cross_rows(normed_low, grad_projected)
    grad_normed = cross_cols(grad_projected, input_weight_used)
    grad_in_norm, grad_gain_mix = norm_backward(inputs, scale_mix, first_gain, grad_normed)
    grad_tokens = (grad_residual + grad_in_norm).reshape(seq_count, piece_len, model_width)
    small_grad = jnp.concatenate([grad_gain_mix[None], grad_gain_ffn[None], grad_kernel], axis=0)
    part_in, part_out, part_gate, part_up, part_down, small_part = (
        lax.psum_scatter(grad_w_in, "dp", scatter_dimension=0, tiled=True),
        lax.psum_scatter(grad_w_out, "dp", scatter_dimension=0, tiled=True),
        lax.psum_scatter(grad_w_gate, "dp", scatter_dimension=0, tiled=True),
        lax.psum_scatter(grad_w_up, "dp", scatter_dimension=0, tiled=True),
        lax.psum_scatter(grad_w_down, "dp", scatter_dimension=0, tiled=True),
        lax.psum_scatter(small_grad, "dp", scatter_dimension=1, tiled=True),
    )
    final_in, final_out, final_gate, final_up, final_down = (
        lax.psum_scatter(part_in, "ctx", scatter_dimension=1, tiled=True),
        lax.psum_scatter(part_out, "ctx", scatter_dimension=1, tiled=True),
        lax.psum_scatter(part_gate, "ctx", scatter_dimension=1, tiled=True),
        lax.psum_scatter(part_up, "ctx", scatter_dimension=1, tiled=True),
        lax.psum_scatter(part_down, "ctx", scatter_dimension=1, tiled=True),
    )
    small_total = lax.psum(small_part, "ctx")
    return (
        result,
        grad_tokens,
        final_in,
        final_out,
        final_gate,
        final_up,
        final_down,
        small_total[0],
        small_total[1],
        small_total[2:5],
    )


NT = (((1,), (1,)), ((), ()))
TN = (((0,), (0,)), ((), ()))


def swap(block):
    return lax.ppermute(block, "core", [(0, 1), (1, 0)])


def across(block, mask):
    count = lax.axis_size("chip") * lax.axis_size("ctx")
    return lax.ppermute(block, ("chip", "ctx"), [(i, i ^ mask) for i in range(count)])


def bit_masks():
    n_chip, n_ctx = lax.axis_size("chip"), lax.axis_size("ctx")
    ctx_bits = [1 << b for b in range(n_ctx.bit_length() - 1)]
    near = [n_ctx]
    far = [n_ctx << b for b in range(1, n_chip.bit_length() - 1)]
    return far, near + ctx_bits, ctx_bits + near


def after(value, *done):
    return lax.optimization_barrier((value, *done))[0]


def gather_plan(cut, total):
    far, first_order, second_order = bit_masks()
    plan = []
    for operand, order, row0, rows in ((0, first_order, 0, cut), (2, second_order, cut, total - cut)):
        masks = [0]
        for mask in far + order[:-1]:
            masks = masks + [m ^ mask for m in masks]
        for index, mask in enumerate(masks):
            plan.append((operand, index, mask, row0, rows))
            plan.append((operand + 1, index, mask ^ order[-1], row0, rows))
    return plan


def gather(block, cut):
    far, first_order, second_order = bit_masks()
    hold = block[None]
    for mask in far:
        hold = jnp.concatenate([hold, across(hold, mask)], axis=0)
    parts = []
    for order, half in ((first_order, hold[:, :cut]), (second_order, hold[:, cut:])):
        for mask in order[:-1]:
            half = jnp.concatenate([half, across(half, mask)], axis=0)
        parts += [half, across(half, order[-1])]
    return parts


def scatter_sum(parts, ties=()):
    far, first_order, second_order = bit_masks()
    ties = dict(enumerate(ties))

    def sent(block, mask, step):
        block = block.astype(bf16)
        if ties.get(step) is not None:
            block = after(block, ties[step])
        return across(block, mask).astype(f32)

    halves = []
    for order, keep, send in ((first_order, parts[0], parts[1]), (second_order, parts[2], parts[3])):
        keep = keep.astype(f32) + sent(send, order[-1], 0)
        for step, mask in enumerate(reversed(order[:-1])):
            mid = keep.shape[0] // 2
            keep = keep[:mid] + sent(keep[mid:], mask, step + 1)
        halves.append(keep)
    keep = jnp.concatenate(halves, axis=1)
    for step, mask in enumerate(reversed(far)):
        mid = keep.shape[0] // 2
        keep = keep[:mid] + sent(keep[mid:], mask, len(first_order) + step)
    return keep[0]


def slot_pairs(own, plan, refs, segments, n_ctx, targets):
    pairs = []
    for operand, index, mask, row0, nrows in plan:
        slot = index if mask is None else jnp.bitwise_xor(own, mask)
        y = lax.rem(slot, n_ctx)
        chip = lax.div(slot, n_ctx)
        src = refs[operand].at[index]
        for seg_row, seg_rows, lane0, lanes, target, row_step, row_add, lane_step, lane_add in segments:
            low, high = max(seg_row, row0), min(seg_row + seg_rows, row0 + nrows)
            if low >= high:
                continue
            row = pl.multiple_of(chip * row_step + row_add + (low - seg_row), 16)
            lane = pl.multiple_of(y * lane_step + lane_add, 128)
            pairs.append(
                (
                    src.at[pl.ds(low - row0, high - low), pl.ds(lane0, lanes)],
                    targets[target].at[pl.ds(row, high - low), pl.ds(lane, lanes)],
                )
            )
    return pairs


def copy_all(pairs, sems):
    copies = [pltpu.make_async_copy(a, b, sems.at[i]) for i, (a, b) in enumerate(pairs)]
    for copy in copies:
        copy.start()
    for copy in copies:
        copy.wait()


def part_count(plan):
    return 1 + max(entry[0] for entry in plan)


def part_shapes(plan, lanes):
    shapes = {}
    for operand, index, _, _, rows in plan:
        shapes[operand] = (max(index + 1, shapes.get(operand, (0,))[0]), rows, lanes)
    return [shapes[operand] for operand in sorted(shapes)]


def ffn_kernel(geometry, out_geometry, first, own_ref, n_ref, go_ref, *refs):
    plan, segments, n_ctx = geometry
    out_plan = out_geometry[0]
    count, out_count = part_count(plan), part_count(out_plan)
    weights, refs = refs[:count], refs[count:]
    if not first:
        res_in, gn_in = refs[:2]
        refs = refs[2:]
    res_ref, gn_ref = refs[:2]
    grads, refs = refs[2 : 2 + out_count], refs[2 + out_count :]
    gate_m, up_m, down_m, d_gate, d_up, d_down, h_m, gg_m, gu_m, sems = refs
    own = own_ref[0]
    targets = (gate_m, up_m, down_m)

    @pl.when(pl.program_id(0) == 0)
    def _():
        d_gate[...] = jnp.zeros_like(d_gate)
        d_up[...] = jnp.zeros_like(d_up)
        d_down[...] = jnp.zeros_like(d_down)
        copy_all(slot_pairs(own, plan, weights, segments, n_ctx, targets), sems)

    n = n_ref[...]
    go = go_ref[...]
    hidden_count = gate_m.shape[1]
    step = 256
    for start in range(0, hidden_count, step):
        cols = slice(start, start + step)
        g = jnp.dot(n, gate_m[:, cols], preferred_element_type=f32)
        u = jnp.dot(n, up_m[:, cols], preferred_element_type=f32)
        gh = lax.dot_general(go, down_m[cols, :], NT, preferred_element_type=f32)
        s = jax.nn.sigmoid(g)
        act = g * s
        h_m[:, cols] = (act * u).astype(bf16)
        gg_m[:, cols] = (gh * u * s * (1.0 + g * (1.0 - s))).astype(bf16)
        gu_m[:, cols] = (gh * act).astype(bf16)
    res = jnp.dot(h_m[...], down_m[...], preferred_element_type=f32)
    gn = lax.dot_general(gg_m[...], gate_m[...], NT, preferred_element_type=f32)
    gn = gn + lax.dot_general(gu_m[...], up_m[...], NT, preferred_element_type=f32)
    if not first:
        res = res_in[...] + res
        gn = gn_in[...] + gn
    res_ref[...] = res
    gn_ref[...] = gn
    d_gate[...] += lax.dot_general(n, gg_m[...], TN, preferred_element_type=f32)
    d_up[...] += lax.dot_general(n, gu_m[...], TN, preferred_element_type=f32)
    d_down[...] += lax.dot_general(h_m[...], go, TN, preferred_element_type=f32)

    @pl.when(pl.program_id(0) == pl.num_programs(0) - 1)
    def _():
        gate_m[...] = d_gate[...].astype(bf16)
        up_m[...] = d_up[...].astype(bf16)
        down_m[...] = d_down[...].astype(bf16)
        pairs = slot_pairs(own, out_plan, grads, segments, n_ctx, targets)
        copy_all([(b, a) for a, b in pairs], sems)


def ffn_chunk(own, nffn, go, weights, totals, geometry, out_geometry, hidden_count, rows=256):
    total, width = nffn.shape
    first = totals is None
    plan, segments, _ = geometry
    out_plan = out_geometry[0]
    count, out_count = part_count(plan), part_count(out_plan)
    lanes = weights[0].shape[-1]
    row_spec = pl.BlockSpec((rows, width), lambda i, o: (i, 0))
    any_spec = pl.BlockSpec(memory_space=pl.ANY)
    outs = pl.pallas_call(
        functools.partial(ffn_kernel, geometry, out_geometry, first),
        out_shape=[jax.ShapeDtypeStruct((total, width), f32)] * 2
        + [jax.ShapeDtypeStruct(s, bf16) for s in part_shapes(out_plan, lanes)],
        grid_spec=pltpu.PrefetchScalarGridSpec(
            num_scalar_prefetch=1,
            grid=(total // rows,),
            in_specs=[row_spec] * 2 + [any_spec] * count + [row_spec] * (0 if first else 2),
            out_specs=[row_spec] * 2 + [any_spec] * out_count,
            scratch_shapes=[
                pltpu.VMEM((width, hidden_count), bf16),
                pltpu.VMEM((width, hidden_count), bf16),
                pltpu.VMEM((hidden_count, width), bf16),
                pltpu.VMEM((width, hidden_count), f32),
                pltpu.VMEM((width, hidden_count), f32),
                pltpu.VMEM((hidden_count, width), f32),
                pltpu.VMEM((rows, hidden_count), bf16),
                pltpu.VMEM((rows, hidden_count), bf16),
                pltpu.VMEM((rows, hidden_count), bf16),
                pltpu.SemaphoreType.DMA((max(len(plan), len(out_plan)) * len(segments),)),
            ],
        ),
        input_output_aliases={} if first else {3 + count: 0, 4 + count: 1},
        compiler_params=pltpu.CompilerParams(
            vmem_limit_bytes=56 * 1024 * 1024, dimension_semantics=("arbitrary",)
        ),
        cost_estimate=pl.CostEstimate(
            flops=18 * total * width * hidden_count,
            bytes_accessed=20 * total * width,
            transcendentals=total * hidden_count,
        ),
    )(own, nffn, go, *weights, *(() if first else totals))
    return (outs[0], outs[1]), outs[2:]


def move_kernel(geometry, count, outward, own_ref, *refs):
    plan, segments, n_ctx = geometry
    sems = refs[-1]
    refs = refs[:-1]
    if outward:
        targets, parts = refs[: len(refs) - count], refs[len(refs) - count :]
    else:
        parts, targets = refs[:count], refs[count:]
    pairs = slot_pairs(own_ref[0], plan, parts, segments, n_ctx, targets)
    copy_all([(b, a) for a, b in pairs] if outward else pairs, sems)


def move(own, arrays, shapes, geometry, count, outward):
    plan, segments, _ = geometry
    any_spec = pl.BlockSpec(memory_space=pl.ANY)
    vmem_spec = pl.BlockSpec(memory_space=pltpu.VMEM)
    return pl.pallas_call(
        functools.partial(move_kernel, geometry, count, outward),
        out_shape=[jax.ShapeDtypeStruct(s, bf16) for s in shapes],
        in_specs=[pl.BlockSpec(memory_space=pltpu.SMEM)]
        + [vmem_spec if outward else any_spec] * len(arrays),
        out_specs=[any_spec if outward else vmem_spec] * len(shapes),
        scratch_shapes=[pltpu.SemaphoreType.DMA((len(plan) * len(segments),))],
        compiler_params=pltpu.CompilerParams(vmem_limit_bytes=24 * 1024 * 1024),
        cost_estimate=pl.CostEstimate(flops=0, bytes_accessed=1 << 24, transcendentals=0),
    )(own, *arrays)


def shifted_down(block, before):
    row = lax.broadcasted_iota(jnp.int32, block.shape, 0)
    one = jnp.where(row == 0, before[1:2], pltpu.roll(block, 1, 0))
    two = jnp.where(row == 0, before[0:1], pltpu.roll(block, 2, 0))
    return one, jnp.where(row == 1, before[1:2], two)


def shifted_up(block, behind):
    count = block.shape[0]
    row = lax.broadcasted_iota(jnp.int32, block.shape, 0)
    one = jnp.where(row == count - 1, behind[0:1], pltpu.roll(block, count - 1, 0))
    two = jnp.where(row == count - 2, behind[0:1], pltpu.roll(block, count - 2, 0))
    return one, jnp.where(row == count - 1, behind[1:2], two)


def in_kernel(x_ref, gain_ref, w_ref, normed_ref, projected_ref):
    x = x_ref[...].astype(f32)
    scale = lax.rsqrt(jnp.mean(x * x, axis=-1, keepdims=True) + EPSILON)
    normed = (x * scale * gain_ref[...]).astype(bf16)
    normed_ref[...] = normed
    projected_ref[...] = jnp.dot(normed, w_ref[...], preferred_element_type=f32)


def conv_kernel(projected_ref, before_ref, taps_ref, w_ref, mixer_ref, conv_ref, branch_ref):
    channels = conv_ref.shape[1]
    product = projected_ref[:, :channels] * projected_ref[:, 2 * channels :]
    one, two = shifted_down(product, before_ref[0].astype(f32))
    conv = taps_ref[0:1] * two + taps_ref[1:2] * one + taps_ref[2:3] * product
    conv_ref[...] = conv
    mixer = (projected_ref[:, channels : 2 * channels] * conv).astype(bf16)
    mixer_ref[...] = mixer
    branch_ref[...] = jnp.dot(mixer, w_ref[...], preferred_element_type=f32).astype(bf16)


def norm_kernel(x_ref, branch_ref, got_ref, gain_ref, residual_ref, normed_ref):
    residual = x_ref[...].astype(f32) + (branch_ref[...].astype(f32) + got_ref[...].astype(f32))
    residual_ref[...] = residual
    scale = lax.rsqrt(jnp.mean(residual * residual, axis=-1, keepdims=True) + EPSILON)
    normed_ref[...] = (residual * scale * gain_ref[...]).astype(bf16)


def branch_grad_kernel(
    own_first, gn_ref, got_ref, residual_ref, go_ref, gain_ref, mixer_ref, conv_ref, gate_c_ref,
    w_ref, grad_residual_ref, grad_conv_ref, grad_c_ref, grad_w_ref, grad_gain_ref, total_ref,
):
    step = pl.program_id(0)

    @pl.when(step == 0)
    def _():
        total_ref[...] = jnp.zeros_like(total_ref)
        grad_gain_ref[...] = jnp.zeros_like(grad_gain_ref)

    incoming = gn_ref[...] + got_ref[...].astype(f32)
    residual = residual_ref[...]
    scale = lax.rsqrt(jnp.mean(residual * residual, axis=-1, keepdims=True) + EPSILON)
    weighted = incoming * gain_ref[...]

    @pl.when(step >= own_first)
    def _():
        grad_gain_ref[...] += jnp.sum(incoming * residual * scale, axis=0, keepdims=True)

    inner = jnp.mean(weighted * residual, axis=-1, keepdims=True)
    grad_residual = go_ref[...].astype(f32) + (
        scale * weighted - residual * (scale * scale * scale) * inner
    )
    grad_residual_ref[...] = grad_residual
    grad_branch = grad_residual.astype(bf16)
    grad_mix = lax.dot_general(grad_branch, w_ref[...], NT, preferred_element_type=f32)
    grad_c_ref[...] = (grad_mix * conv_ref[...]).astype(bf16)
    grad_conv_ref[...] = grad_mix * gate_c_ref[...]
    total_ref[...] += lax.dot_general(mixer_ref[...], grad_branch, TN, preferred_element_type=f32)

    @pl.when(step == pl.num_programs(0) - 1)
    def _():
        grad_w_ref[...] = total_ref[...].astype(bf16)


def in_grad_kernel(
    geometry, count, own_ref, grad_conv_ref, behind_ref, before_ref, projected_ref, grad_c_ref,
    normed_ref, taps_ref, grad_out_ref, grad_projected_ref, grad_taps_ref, *refs
):
    parts, (total_ref, low_ref, sems) = refs[:count], refs[count:]
    plan, segments, n_ctx = geometry
    step = pl.program_id(0)

    @pl.when(step == 0)
    def _():
        total_ref[...] = jnp.zeros_like(total_ref)
        grad_taps_ref[...] = jnp.zeros_like(grad_taps_ref)

    channels = grad_c_ref.shape[1]
    grad_conv = grad_conv_ref[...]
    gate_b = projected_ref[:, :channels]
    values = projected_ref[:, 2 * channels :]
    product = gate_b * values
    one, two = shifted_down(product, before_ref[0].astype(f32))
    for k, shifted in enumerate((two, one, product)):
        grad_taps_ref[k : k + 1] += jnp.sum(grad_conv * shifted, axis=0, keepdims=True)
    one, two = shifted_up(grad_conv, behind_ref[0].astype(f32))
    grad_product = taps_ref[2:3] * grad_conv + taps_ref[1:2] * one + taps_ref[0:1] * two
    grad_projected_ref[:, :channels] = (grad_product * values).astype(bf16)
    grad_projected_ref[:, channels : 2 * channels] = grad_c_ref[...]
    grad_projected_ref[:, 2 * channels :] = (grad_product * gate_b).astype(bf16)
    total_ref[...] += lax.dot_general(
        normed_ref[...], grad_projected_ref[...], TN, preferred_element_type=f32
    )

    @pl.when(step == pl.num_programs(0) - 1)
    def _():
        low_ref[...] = total_ref[...].astype(bf16)
        pairs = slot_pairs(own_ref[0], plan, parts, segments, n_ctx, (low_ref, grad_out_ref))
        copy_all([(b, a) for a, b in pairs], sems)


def row_call(body, steps, ins, outs, scratch=(), flops=0, limit=48):
    return pl.pallas_call(
        body,
        grid=(steps,),
        in_specs=[
            pl.BlockSpec(memory_space=pltpu.SMEM) if block is None else pl.BlockSpec(block, place)
            for _, block, place in ins
        ],
        out_specs=[
            pl.BlockSpec(memory_space=pl.ANY) if block is None else pl.BlockSpec(block, place)
            for _, _, block, place in outs
        ],
        out_shape=[jax.ShapeDtypeStruct(shape, dtype) for shape, dtype, _, _ in outs],
        scratch_shapes=list(scratch),
        compiler_params=pltpu.CompilerParams(
            vmem_limit_bytes=limit * 1024 * 1024, dimension_semantics=("arbitrary",)
        ),
        cost_estimate=pl.CostEstimate(
            flops=flops,
            bytes_accessed=sum(a.size * a.dtype.itemsize for a, _, _ in ins),
            transcendentals=0,
        ),
    )(*[a for a, _, _ in ins])


def fits(tokens, w_in, w_out, w_gate, w_down, n_dp, n_ctx):
    width, hidden = w_gate.shape
    if n_dp % 2 or n_dp % (2 * n_ctx) or n_dp & (n_dp - 1) or n_ctx & (n_ctx - 1) or n_ctx < 2:
        return False
    depth = width // n_dp
    if width % n_dp or hidden % (n_dp * CHUNKS * 48) or w_in.shape[1] % (2 * n_ctx * 256):
        return False
    lanes = hidden // n_dp // CHUNKS * (n_dp // n_ctx // 2)
    wide = width // n_ctx
    return (
        lanes % 128 == 0
        and wide == lanes + 128
        and lanes == 384
        and wide % 256 == 0
        and depth % 16 == 0
        and 2 * depth <= 256
        and (w_in.shape[1] // n_ctx) % (2 * depth) == 0
        and width % (2 * depth) == 0
        and tokens.shape[1] % n_ctx == 0
    )


def fast_shards(tokens, w_in, w_out, w_gate, w_up, w_down, gain_mix, gain_ffn, kernel, cotangent):
    seqs, piece, width = tokens.shape
    rows = seqs * piece
    n_chip, n_ctx = lax.axis_size("chip"), lax.axis_size("ctx")
    slots = n_chip * n_ctx
    core = lax.axis_index("core")
    own_slot = lax.axis_index("chip") * n_ctx + lax.axis_index("ctx")
    own = own_slot.astype(jnp.int32)[None]
    depth = w_in.shape[0]
    groups = n_chip // n_ctx
    sub = w_down.shape[0] // CHUNKS
    lanes = groups * sub
    wide = w_out.shape[1]
    in_cols = w_in.shape[1] // 2
    in_parts, out_parts = in_cols // 256, wide // 256
    hidden_count = n_chip * sub
    channels = width // 2

    def mine_other(pair):
        return jnp.where(core == 0, pair[0], pair[1]), jnp.where(core == 0, pair[1], pair[0])

    def in_core_order(mine, other, axis):
        return jnp.where(
            core == 0,
            jnp.concatenate([mine, other], axis=axis),
            jnp.concatenate([other, mine], axis=axis),
        )

    small = jnp.concatenate([gain_mix[None], gain_ffn[None], kernel], axis=0)
    in_pair = w_in.reshape(depth, in_cols // depth, 2, depth).transpose(2, 0, 1, 3)
    in_pair = in_pair.reshape(2, depth, in_parts, 256).transpose(0, 2, 1, 3)
    in_mine, in_other = mine_other(in_pair)
    small_rows = jnp.pad(small, ((0, 11), (0, 256 - depth)))
    swapped = swap(jnp.concatenate([in_other.reshape(in_parts * depth, 256), small_rows], axis=0))
    in_got = swapped[: in_parts * depth].reshape(in_parts, depth, 256)
    in_block = in_core_order(in_mine, in_got, 1).reshape(in_parts * 2 * depth, 256)
    small_block = in_core_order(small, swapped[in_parts * depth :][:5, :depth], 1)
    small_block = jnp.pad(small_block, ((0, 11), (0, 256 - 2 * depth)))
    out_block = w_out.reshape(depth, out_parts, 256).transpose(1, 0, 2).reshape(-1, 256)
    mix_block = jnp.concatenate([in_block, small_block], axis=0)

    both = jnp.stack([w_gate, w_up]).reshape(2, depth, groups, 2, CHUNKS, sub)
    both = both.transpose(3, 4, 0, 1, 2, 5).reshape(2, CHUNKS, 2, depth, lanes)
    both_mine, both_other = mine_other(both)
    both_block = in_core_order(both_mine, swap(both_other), 2)
    both_block = both_block.reshape(CHUNKS, 4 * depth, lanes)
    down = w_down.reshape(CHUNKS, sub, wide)
    down_rest = down[:, :, lanes:].reshape(CHUNKS, 3, sub // 3, 128).transpose(0, 2, 1, 3)
    chunk_blocks = jnp.concatenate(
        [both_block, down[:, :, :lanes], down_rest.reshape(CHUNKS, sub // 3, lanes)], axis=1
    )

    mix_rows = mix_block.shape[0]
    mix_cut = in_parts * depth
    in_rows = in_parts * 2 * depth
    mix_segments = [
        (k * 2 * depth, 2 * depth, 0, 256, 0, 2 * depth, 0, in_cols, 256 * k)
        for k in range(in_parts)
    ]
    out_segments = [
        (in_rows + k * depth, depth, 0, 256, 1, depth, 0, wide, 256 * k) for k in range(out_parts)
    ]
    small_segment = (in_rows, 16, 0, 256, 1, 16, 0, 256, 0)
    mix_plan = gather_plan(mix_cut, mix_rows)
    chunk_rows = chunk_blocks.shape[1]
    chunk_cut = chunk_rows // 2
    chunk_segments = [
        (0, 2 * depth, 0, lanes, 0, 2 * depth, 0, lanes, 0),
        (2 * depth, 2 * depth, 0, lanes, 1, 2 * depth, 0, lanes, 0),
        (4 * depth, sub, 0, lanes, 2, sub, 0, wide, 0),
    ] + [
        (4 * depth + sub, sub // 3, 128 * k, 128, 2, sub, k * (sub // 3), wide, lanes)
        for k in range(3)
    ]
    whole_plan = [(0, i, None, 0, chunk_rows) for i in range(slots)]
    whole_geometry = (whole_plan, chunk_segments, n_ctx)
    step_geometry = (gather_plan(chunk_cut, chunk_rows), chunk_segments, n_ctx)

    first_block = jnp.concatenate(
        [chunk_blocks[0], jnp.pad(out_block, ((0, 0), (0, lanes - 256)))], axis=0
    )
    first_all = lax.all_gather(first_block, ("chip", "ctx"))
    last_all = lax.all_gather(chunk_blocks[2], ("chip", "ctx"))

    far, first_order, second_order = bit_masks()

    def doubled(hold, got):
        return jnp.concatenate([hold, got], axis=0)

    hold = mix_block[None]
    for mask in far:
        hold = doubled(hold, across(hold, mask))
    mix_halves = [hold[:, :mix_cut], hold[:, mix_cut:]]
    next_hold = after(chunk_blocks[1][None], hold)
    far_left = list(far)
    mix_parts = []
    for step in range(len(first_order)):
        got = [across(h, order[step]) for h, order in zip(mix_halves, (first_order, second_order))]
        if far_left:
            next_got = across(next_hold, far_left.pop(0))
            next_hold = doubled(next_hold, next_got)
            if step + 1 < len(first_order):
                got = [after(g, next_got) for g in got]
        if step + 1 < len(first_order):
            mix_halves = [doubled(h, g) for h, g in zip(mix_halves, got)]
            next_hold = after(next_hold, *got)
        else:
            mix_parts = [mix_halves[0], got[0], mix_halves[1], got[1]]
    for mask in far_left:
        next_hold = doubled(next_hold, across(next_hold, mask))
    in_half, small_all = move(
        own,
        mix_parts,
        [(width, n_ctx * in_cols), (n_chip * 16, n_ctx * 256)],
        (mix_plan, mix_segments + [small_segment], n_ctx),
        4,
        False,
    )
    (out_half,) = move(
        own,
        [first_all],
        [(channels, width)],
        (
            [(0, i, None, 0, chunk_rows + out_parts * depth) for i in range(slots)],
            [
                (chunk_rows + k * depth, depth, 0, 256, 0, depth, 0, wide, 256 * k)
                for k in range(out_parts)
            ],
            n_ctx,
        ),
        1,
        False,
    )
    next_halves = [next_hold[:, :chunk_cut], next_hold[:, chunk_cut:]]
    next_orders = (first_order, second_order)

    def next_step(step, *done):
        got = [across(after(h, *done), o[step]) for h, o in zip(next_halves, next_orders)]
        return got

    small_all = small_all.reshape(n_chip, 16, n_ctx * 256)[:, :5, : 2 * depth].astype(f32)
    first_gain = small_all[:, 0].reshape(width)
    second_gain = small_all[:, 1].reshape(width)
    taps = small_all[:, 2:].reshape(n_chip, 3, 2, depth)
    taps = jnp.where(core == 0, taps[:, :, 0], taps[:, :, 1]).transpose(1, 0, 2)
    taps = taps.reshape(3, channels)

    token_rows = tokens.reshape(rows, width)
    inputs = jnp.concatenate([token_rows, swap(token_rows)], axis=0)
    go_rows = cotangent.reshape(rows, width)
    go = jnp.concatenate([go_rows, swap(go_rows)], axis=0)
    blocks = 2 * seqs

    def at(i):
        return (i, 0)

    def still(i):
        return (0, 0)

    def other(i):
        return ((i + seqs) % blocks, 0)

    wide_rows, thin_rows = (piece, width), (piece, channels)
    taps = jnp.pad(taps, ((0, 5), (0, 0)))
    next_got = next_step(0, in_half)
    normed_low, projected = row_call(
        in_kernel,
        blocks,
        [
            (inputs, wide_rows, at),
            (first_gain[None], (1, width), still),
            (in_half, in_half.shape, still),
        ],
        [
            ((2 * rows, width), bf16, wide_rows, at),
            ((2 * rows, 3 * channels), f32, (piece, 3 * channels), at),
        ],
        flops=12 * rows * width * channels,
    )
    tail = projected.reshape(blocks, piece, 3 * channels)[:, piece - 2 :]
    tail = (tail[:, :, :channels] * tail[:, :, 2 * channels :]).astype(bf16)
    before = passed_along(tail, "ctx", 1)
    halo = (1, 2, channels)

    def halo_at(i):
        return (i, 0, 0)

    mixer_out, convolved, branch = row_call(
        conv_kernel,
        blocks,
        [
            (projected, (piece, 3 * channels), at),
            (before, halo, halo_at),
            (taps, taps.shape, still),
            (out_half, out_half.shape, still),
        ],
        [
            ((2 * rows, channels), bf16, thin_rows, at),
            ((2 * rows, channels), f32, thin_rows, at),
            ((2 * rows, width), bf16, wide_rows, at),
        ],
        flops=4 * rows * width * channels,
    )
    branch = after(branch, *next_got)
    for step in range(1, len(first_order)):
        next_halves = [doubled(h, g) for h, g in zip(next_halves, next_got)]
        next_got = next_step(step, branch)
    next_parts = [next_halves[0], next_got[0], next_halves[1], next_got[1]]
    residual, nffn_low = row_call(
        norm_kernel,
        blocks,
        [
            (inputs, wide_rows, at),
            (branch, wide_rows, at),
            (swap(branch), wide_rows, other),
            (second_gain[None], (1, width), still),
        ],
        [((2 * rows, width), f32, wide_rows, at), ((2 * rows, width), bf16, wide_rows, at)],
    )

    totals, first_grads = ffn_chunk(
        own, nffn_low, go, [first_all], None, whole_geometry, step_geometry, hidden_count
    )
    first_total = totals[1]
    totals, next_grads = ffn_chunk(
        own, nffn_low, go, next_parts, totals, step_geometry, step_geometry, hidden_count
    )
    next_total = totals[1]
    totals, last_grads = ffn_chunk(
        own, nffn_low, go, [last_all], totals, whole_geometry, step_geometry, hidden_count
    )
    ffn_out, grad_nffn = totals
    grad_got = swap(grad_nffn.astype(bf16))
    ffn_got = swap(ffn_out[rows:].astype(bf16))

    def turned(i):
        return ((i + seqs) % blocks, 0)

    def turned_back(i):
        return (i, 0)

    def own_place(i):
        return (jnp.maximum(i - seqs, 0), 0)

    def gate_c_place(i):
        return ((i + seqs) % blocks, 1)

    grad_residual, grad_conv, grad_c, grad_w_out, grad_gain_ffn = row_call(
        functools.partial(branch_grad_kernel, seqs),
        blocks,
        [
            (grad_nffn, wide_rows, turned),
            (grad_got, wide_rows, turned_back),
            (residual, wide_rows, turned),
            (go, wide_rows, turned),
            (second_gain[None], (1, width), still),
            (mixer_out, thin_rows, turned),
            (convolved, thin_rows, turned),
            (projected, thin_rows, gate_c_place),
            (out_half, out_half.shape, still),
        ],
        [
            ((rows, width), f32, wide_rows, own_place),
            ((2 * rows, channels), f32, thin_rows, turned),
            ((2 * rows, channels), bf16, thin_rows, turned),
            ((channels, width), bf16, (channels, width), still),
            ((1, width), f32, (1, width), still),
        ],
        scratch=[pltpu.VMEM((channels, width), f32)],
        flops=8 * rows * width * channels,
    )
    grad_gain_ffn = grad_gain_ffn[0]
    head = grad_conv.reshape(blocks, piece, channels)[:, :2].astype(bf16)
    behind = passed_along(head, "ctx", -1)
    sum_rows = in_rows + out_parts * depth
    sum_cut = sum_rows // 2
    sum_plan = gather_plan(sum_cut, sum_rows)
    sum_segments = mix_segments + out_segments
    grad_projected, grad_kernel, *mix_grad_parts = row_call(
        functools.partial(in_grad_kernel, (sum_plan, sum_segments, n_ctx), 4),
        blocks,
        [
            (own, None, None),
            (grad_conv, thin_rows, at),
            (behind, halo, halo_at),
            (before, halo, halo_at),
            (projected, (piece, 3 * channels), at),
            (grad_c, thin_rows, at),
            (normed_low, wide_rows, at),
            (taps, taps.shape, still),
            (grad_w_out, grad_w_out.shape, still),
        ],
        [
            ((2 * rows, 3 * channels), bf16, (piece, 3 * channels), at),
            ((8, channels), f32, (8, channels), still),
        ]
        + [(shape, bf16, None, None) for shape in part_shapes(sum_plan, 256)],
        scratch=[
            pltpu.VMEM((width, 3 * channels), f32),
            pltpu.VMEM((width, 3 * channels), bf16),
            pltpu.SemaphoreType.DMA((len(sum_plan) * len(sum_segments),)),
        ],
        flops=12 * rows * width * channels,
    )
    grad_kernel = grad_kernel[:3]
    first_sum = scatter_sum(first_grads, (None, next_total, grad_got, grad_c))
    next_sum = scatter_sum(next_grads, (None, grad_got, grad_c, grad_projected))
    last_sum = scatter_sum(last_grads, (None, grad_c, grad_projected, grad_projected))
    mix_sum = scatter_sum(mix_grad_parts)
    late_projected = after(grad_projected, mix_grad_parts[1])
    grad_normed = cross_cols(late_projected[rows:], in_half).astype(bf16)
    grad_normed = cross_cols(late_projected[:rows], in_half) + swap(grad_normed).astype(f32)
    result = residual[:rows] + (ffn_out[:rows] + ffn_got.astype(f32))
    result = result.astype(bf16).reshape(seqs, piece, width)
    own_inputs = token_rows.astype(f32)
    scale_mix = lax.rsqrt(jnp.mean(own_inputs * own_inputs, axis=-1, keepdims=True) + EPSILON)
    grad_in_norm, grad_gain_mix = norm_backward(own_inputs, scale_mix, first_gain, grad_normed)
    grad_tokens = (grad_residual + grad_in_norm).reshape(seqs, piece, width)

    chunk_sum = jnp.stack([first_sum, next_sum, last_sum])
    both_sum = chunk_sum[:, : 4 * depth].reshape(CHUNKS, 2, 2, depth, lanes).transpose(2, 0, 1, 3, 4)
    both_mine, both_other = mine_other(both_sum)
    both_got = swap(both_other)
    both_sum = in_core_order(both_mine[None], both_got[None], 0)
    both_sum = both_sum.reshape(2, CHUNKS, 2, depth, groups, sub).transpose(2, 3, 4, 0, 1, 5)
    both_sum = both_sum.reshape(2, depth, 2 * CHUNKS * lanes)
    down_rest = chunk_sum[:, 4 * depth + sub :].reshape(CHUNKS, sub // 3, 3, 128)
    down_rest = down_rest.transpose(0, 2, 1, 3).reshape(CHUNKS, sub, 128)
    final_down = jnp.concatenate([chunk_sum[:, 4 * depth : 4 * depth + sub], down_rest], axis=2)
    final_down = final_down.reshape(CHUNKS * sub, wide)

    in_sum = mix_sum[:in_rows].reshape(in_parts, 2, depth, 256).transpose(1, 0, 2, 3)
    in_mine, in_other = mine_other(in_sum)
    in_sum = in_core_order(in_mine[None], swap(in_other)[None], 0)
    in_sum = in_sum.transpose(0, 2, 1, 3).reshape(2, depth, in_cols // depth, depth)
    final_in = in_sum.transpose(1, 2, 0, 3).reshape(depth, 2 * in_cols)
    final_out = mix_sum[in_rows:].reshape(out_parts, depth, 256).transpose(1, 0, 2)
    final_out = final_out.reshape(depth, wide)

    grad_taps = grad_kernel.reshape(3, n_chip, 1, depth)
    grad_taps = jnp.where(
        jnp.arange(2).reshape(1, 1, 2, 1) == core, grad_taps, jnp.zeros_like(grad_taps)
    ).reshape(3, width)
    small_grad = jnp.concatenate([grad_gain_mix[None], grad_gain_ffn[None], grad_taps], axis=0)
    small_sum = small_grad.reshape(5, n_chip, 2 * depth).transpose(1, 0, 2)
    for bit in range(n_ctx.bit_length() - 1):
        small_sum = small_sum + across(small_sum, 1 << bit)
    for bit in range(n_chip.bit_length() - 1):
        mask = n_chip >> (bit + 1)
        low, high = small_sum[: small_sum.shape[0] // 2], small_sum[small_sum.shape[0] // 2 :]
        upper = jnp.bitwise_and(lax.axis_index("chip"), mask) != 0
        small_sum = jnp.where(upper, high, low) + across(jnp.where(upper, low, high), mask * n_ctx)
    small_mine, small_other = mine_other(small_sum[0].reshape(5, 2, depth).transpose(1, 0, 2))
    small_sum = small_mine + swap(small_other)
    return (
        result,
        grad_tokens,
        final_in,
        final_out,
        both_sum[0],
        both_sum[1],
        final_down,
        small_sum[0],
        small_sum[1],
        small_sum[2:5],
    )


def solution(mesh):
    n_dp, n_ctx = mesh.shape["dp"], mesh.shape["ctx"]

    def placed(dp):
        whole, cut = P(dp, "ctx", None), P(dp, "ctx")
        ins = (whole, cut, cut, cut, cut, cut, P(dp), P(dp), P(None, dp), whole)
        outs = (whole, whole, cut, cut, cut, cut, cut, P(dp), P(dp), P(None, dp))
        return ins, outs

    def run(tokens, w_in, w_out, w_gate, w_up, w_down, gain_mix, gain_ffn, kernel, cotangent):
        if fits(tokens, w_in, w_out, w_gate, w_down, n_dp, n_ctx):
            cut_mesh = Mesh(mesh.devices.reshape(n_dp // 2, 2, n_ctx), ("chip", "core", "ctx"))
            body, on, (ins, outs) = fast_shards, cut_mesh, placed(("chip", "core"))
        else:
            body, on, (ins, outs) = plain_shards, mesh, placed("dp")
        call = jax.shard_map(body, mesh=on, in_specs=ins, out_specs=outs, check_vma=False)
        return call(
            tokens, w_in, w_out, w_gate, w_up, w_down, gain_mix, gain_ffn, kernel, cotangent
        )

    return run
```

```python
import functools
import jax
import jax.numpy as jnp
from jax import lax
from jax.experimental import pallas as pl
from jax.experimental.pallas import tpu as pltpu
from jax.sharding import Mesh
from jax.sharding import PartitionSpec as P

EPSILON = 1e-05
CHUNKS = 3
f32 = jnp.float32
bf16 = jnp.bfloat16


def passed_along(block, axis, distance):
    devices = range(lax.axis_size(axis))
    route = [(i - distance, i) for i in devices if i - distance in devices]
    return lax.ppermute(block, axis, route)


def cross_rows(left_operand, right_operand):
    return lax.dot_general(
        left_operand, right_operand, (((0,), (0,)), ((), ())), preferred_element_type=jnp.float32
    )


def cross_cols(left_operand, right_operand):
    return lax.dot_general(
        left_operand, right_operand, (((1,), (1,)), ((), ())), preferred_element_type=jnp.float32
    )


def norm_forward(values, gain):
    scale = lax.rsqrt(jnp.mean(values * values, axis=-1, keepdims=True) + EPSILON)
    return (values * scale * gain, scale)


def norm_backward(values, scale, gain, incoming):
    weighted = incoming * gain
    gain_grad = jnp.sum(incoming * values * scale, axis=0)
    inner = jnp.mean(weighted * values, axis=-1, keepdims=True)
    return (scale * weighted - values * (scale * scale * scale) * inner, gain_grad)


def plain_shards(tokens, w_in, w_out, w_gate, w_up, w_down, gain_mix, gain_ffn, kernel, cotangent):
    seq_count, piece_len, model_width = tokens.shape
    row_count = seq_count * piece_len
    small_params = jnp.concatenate([gain_mix[None], gain_ffn[None], kernel], axis=0)
    input_columns, out_cols, gate_cols, up_cols, down_cols = (
        lax.all_gather(w_in, "ctx", axis=1, tiled=True),
        lax.all_gather(w_out, "ctx", axis=1, tiled=True),
        lax.all_gather(w_gate, "ctx", axis=1, tiled=True),
        lax.all_gather(w_up, "ctx", axis=1, tiled=True),
        lax.all_gather(w_down, "ctx", axis=1, tiled=True),
    )
    full_in, full_out, full_gate, full_up, full_down, small_full = (
        lax.all_gather(input_columns, "dp", axis=0, tiled=True),
        lax.all_gather(out_cols, "dp", axis=0, tiled=True),
        lax.all_gather(gate_cols, "dp", axis=0, tiled=True),
        lax.all_gather(up_cols, "dp", axis=0, tiled=True),
        lax.all_gather(down_cols, "dp", axis=0, tiled=True),
        lax.all_gather(small_params, "dp", axis=1, tiled=True),
    )
    small_float = small_full.astype(jnp.float32)
    first_gain = small_float[0]
    second_gain = small_float[1]
    taps = small_float[2:5]
    inputs = tokens.reshape(row_count, model_width).astype(jnp.float32)
    normed, scale_mix = norm_forward(inputs, first_gain)
    normed_low = normed.astype(jnp.bfloat16)
    projected = jnp.dot(normed_low, full_in, preferred_element_type=jnp.float32)
    gate_b = projected[:, :model_width]
    gate_c = projected[:, model_width : 2 * model_width]
    values = projected[:, 2 * model_width :]
    product = (gate_b * values).reshape(seq_count, piece_len, model_width)
    previous = passed_along(product[:, piece_len - 2 :].astype(jnp.bfloat16), "ctx", 1).astype(
        jnp.float32
    )
    padded = jnp.concatenate([previous, product], axis=1)
    convolved = taps[0] * padded[:, :-2] + taps[1] * padded[:, 1:-1] + taps[2] * padded[:, 2:]
    convolved = convolved.reshape(row_count, model_width)
    mixer_out = (gate_c * convolved).astype(jnp.bfloat16)
    residual = inputs + jnp.dot(mixer_out, full_out, preferred_element_type=jnp.float32)
    feedforward_normed, scale_ffn = norm_forward(residual, second_gain)
    nffn_low = feedforward_normed.astype(jnp.bfloat16)
    gate = jnp.dot(nffn_low, full_gate, preferred_element_type=jnp.float32)
    up_value = jnp.dot(nffn_low, full_up, preferred_element_type=jnp.float32)
    sigmoid_gate = jax.nn.sigmoid(gate)
    activated = gate * sigmoid_gate
    hidden = (activated * up_value).astype(jnp.bfloat16)
    result = residual + jnp.dot(hidden, full_down, preferred_element_type=jnp.float32)
    result = result.astype(jnp.bfloat16).reshape(seq_count, piece_len, model_width)
    back_in, output_backward, back_gate, back_up, back_down = (
        lax.all_gather(w_in, "ctx", axis=1, tiled=True),
        lax.all_gather(w_out, "ctx", axis=1, tiled=True),
        lax.all_gather(w_gate, "ctx", axis=1, tiled=True),
        lax.all_gather(w_up, "ctx", axis=1, tiled=True),
        lax.all_gather(w_down, "ctx", axis=1, tiled=True),
    )
    input_weight_used, use_out, use_gate, use_up, use_down = (
        lax.all_gather(back_in, "dp", axis=0, tiled=True),
        lax.all_gather(output_backward, "dp", axis=0, tiled=True),
        lax.all_gather(back_gate, "dp", axis=0, tiled=True),
        lax.all_gather(back_up, "dp", axis=0, tiled=True),
        lax.all_gather(back_down, "dp", axis=0, tiled=True),
    )
    grad_out = cotangent.reshape(row_count, model_width)
    grad_out_float = grad_out.astype(jnp.float32)
    grad_w_down = cross_rows(hidden, grad_out)
    grad_hidden = cross_cols(grad_out, use_down)
    grad_gate = (
        grad_hidden * up_value * sigmoid_gate * (1.0 + gate * (1.0 - sigmoid_gate))
    ).astype(jnp.bfloat16)
    grad_up = (grad_hidden * activated).astype(jnp.bfloat16)
    grad_w_gate = cross_rows(nffn_low, grad_gate)
    grad_w_up = cross_rows(nffn_low, grad_up)
    grad_nffn = cross_cols(grad_gate, use_gate) + cross_cols(grad_up, use_up)
    residual_norm_gradient, grad_gain_ffn = norm_backward(
        residual, scale_ffn, second_gain, grad_nffn
    )
    grad_residual = grad_out_float + residual_norm_gradient
    grad_branch = grad_residual.astype(jnp.bfloat16)
    grad_w_out = cross_rows(mixer_out, grad_branch)
    grad_mix = cross_cols(grad_branch, use_out)
    grad_c = grad_mix * convolved
    grad_conv = (grad_mix * gate_c).reshape(seq_count, piece_len, model_width)
    following = passed_along(grad_conv[:, :2].astype(jnp.bfloat16), "ctx", -1).astype(jnp.float32)
    extended = jnp.concatenate([grad_conv, following], axis=1)
    grad_product = (
        taps[2] * extended[:, :-2] + taps[1] * extended[:, 1:-1] + taps[0] * extended[:, 2:]
    )
    grad_kernel = jnp.stack(
        [
            jnp.sum(grad_conv * padded[:, shift_at : shift_at + piece_len], axis=(0, 1))
            for shift_at in range(3)
        ],
        axis=0,
    )
    grad_product = grad_product.reshape(row_count, model_width)
    grad_projected = jnp.concatenate(
        [grad_product * values, grad_c, grad_product * gate_b], axis=1
    ).astype(jnp.bfloat16)
    grad_w_in = cross_rows(normed_low, grad_projected)
    grad_normed = cross_cols(grad_projected, input_weight_used)
    grad_in_norm, grad_gain_mix = norm_backward(inputs, scale_mix, first_gain, grad_normed)
    grad_tokens = (grad_residual + grad_in_norm).reshape(seq_count, piece_len, model_width)
    small_grad = jnp.concatenate([grad_gain_mix[None], grad_gain_ffn[None], grad_kernel], axis=0)
    part_in, part_out, part_gate, part_up, part_down, small_part = (
        lax.psum_scatter(grad_w_in, "dp", scatter_dimension=0, tiled=True),
        lax.psum_scatter(grad_w_out, "dp", scatter_dimension=0, tiled=True),
        lax.psum_scatter(grad_w_gate, "dp", scatter_dimension=0, tiled=True),
        lax.psum_scatter(grad_w_up, "dp", scatter_dimension=0, tiled=True),
        lax.psum_scatter(grad_w_down, "dp", scatter_dimension=0, tiled=True),
        lax.psum_scatter(small_grad, "dp", scatter_dimension=1, tiled=True),
    )
    final_in, final_out, final_gate, final_up, final_down = (
        lax.psum_scatter(part_in, "ctx", scatter_dimension=1, tiled=True),
        lax.psum_scatter(part_out, "ctx", scatter_dimension=1, tiled=True),
        lax.psum_scatter(part_gate, "ctx", scatter_dimension=1, tiled=True),
        lax.psum_scatter(part_up, "ctx", scatter_dimension=1, tiled=True),
        lax.psum_scatter(part_down, "ctx", scatter_dimension=1, tiled=True),
    )
    small_total = lax.psum(small_part, "ctx")
    return (
        result,
        grad_tokens,
        final_in,
        final_out,
        final_gate,
        final_up,
        final_down,
        small_total[0],
        small_total[1],
        small_total[2:5],
    )


SMALL_COST = pl.CostEstimate(flops=1 << 16, bytes_accessed=1 << 16, transcendentals=0)
VMEM_LIMIT = 60 * 1024 * 1024
NT = (((1,), (1,)), ((), ()))
TN = (((0,), (0,)), ((), ()))


def swap(block):
    return lax.ppermute(block, "core", [(0, 1), (1, 0)])


def across(block, mask):
    count = lax.axis_size("chip") * lax.axis_size("ctx")
    return lax.ppermute(block, ("chip", "ctx"), [(i, i ^ mask) for i in range(count)])


def bit_masks():
    n_chip, n_ctx = lax.axis_size("chip"), lax.axis_size("ctx")
    ctx_bits = [1 << b for b in range(n_ctx.bit_length() - 1)]
    near = [n_ctx]
    far = [n_ctx << b for b in range(1, n_chip.bit_length() - 1)]
    return far, near + ctx_bits, ctx_bits + near


def after(value, *done):
    return lax.optimization_barrier((value, *done))[0]


def gather_plan(cut, total):
    far, first_order, second_order = bit_masks()
    plan = []
    for operand, order, row0, rows in ((0, first_order, 0, cut), (2, second_order, cut, total - cut)):
        masks = [0]
        for mask in far + order[:-1]:
            masks = masks + [m ^ mask for m in masks]
        for index, mask in enumerate(masks):
            plan.append((operand, index, mask, row0, rows))
            plan.append((operand + 1, index, mask ^ order[-1], row0, rows))
    return plan


def gather(block, cut):
    far, first_order, second_order = bit_masks()
    hold = block[None]
    for mask in far:
        hold = jnp.concatenate([hold, across(hold, mask)], axis=0)
    parts = []
    for order, half in ((first_order, hold[:, :cut]), (second_order, hold[:, cut:])):
        for mask in order[:-1]:
            half = jnp.concatenate([half, across(half, mask)], axis=0)
        parts += [half, across(half, order[-1])]
    return parts


def scatter_sum(parts, ties=()):
    far, first_order, second_order = bit_masks()
    n_slots = lax.axis_size("chip") * lax.axis_size("ctx")
    ties = dict(enumerate(ties))

    def got(block, mask, step, senders=range(n_slots)):
        block = lax.ppermute(block.astype(bf16), ("chip", "ctx"), [(i, i ^ mask) for i in senders])
        if ties.get(step) is not None:
            block = after(block, ties[step])
        return block.astype(f32)

    halves = []
    for order, keep, send in ((first_order, parts[0], parts[1]), (second_order, parts[2], parts[3])):
        keep = keep.astype(f32) + got(send, order[-1], 0)
        for step, mask in enumerate(reversed(order[:-1])):
            mid = keep.shape[0] // 2
            keep = keep[:mid] + got(keep[mid:], mask, step + 1)
        halves.append(keep)
    keep = jnp.concatenate(halves, axis=1)
    step = len(first_order)
    if len(far) == 2:
        low, high = far
        outer = [i for i in range(n_slots) if (i & low == 0) == (i & high == 0)]
        inner = [i for i in range(n_slots) if i not in outer]
        distant = keep[2:] + got(keep[2:], low, step, outer)[::-1]
        keep = keep[:2] + got(distant, low | high, step + 1, inner)[::-1]
        return keep[0] + got(keep[1:], low, step + 2)[0]
    for mask in reversed(far):
        mid = keep.shape[0] // 2
        keep = keep[:mid] + got(keep[mid:], mask, step)
        step += 1
    return keep[0]


def slot_pairs(own, plan, refs, segments, n_ctx, targets):
    pairs = []
    for operand, index, mask, row0, nrows in plan:
        slot = index if mask is None else jnp.bitwise_xor(own, mask)
        y = lax.rem(slot, n_ctx)
        chip = lax.div(slot, n_ctx)
        src = refs[operand].at[index]
        for seg_row, seg_rows, lane0, lanes, target, row_step, row_add, lane_step, lane_add in segments:
            low, high = max(seg_row, row0), min(seg_row + seg_rows, row0 + nrows)
            if low >= high:
                continue
            row = pl.multiple_of(chip * row_step + row_add + (low - seg_row), 16)
            lane = pl.multiple_of(y * lane_step + lane_add, 128)
            pairs.append(
                (
                    src.at[pl.ds(low - row0, high - low), pl.ds(lane0, lanes)],
                    targets[target].at[pl.ds(row, high - low), pl.ds(lane, lanes)],
                )
            )
    return pairs


def copy_all(pairs, sems):
    copies = [pltpu.make_async_copy(a, b, sems.at[i]) for i, (a, b) in enumerate(pairs)]
    for copy in copies:
        copy.start()
    for copy in copies:
        copy.wait()


def part_count(plan):
    return 1 + max(entry[0] for entry in plan)


def part_shapes(plan, lanes):
    shapes = {}
    for operand, index, _, _, rows in plan:
        shapes[operand] = (max(index + 1, shapes.get(operand, (0,))[0]), rows, lanes)
    return [shapes[operand] for operand in sorted(shapes)]


def ffn_kernel(geometry, out_geometry, first, own_ref, n_ref, go_ref, *refs):
    plan, segments, n_ctx = geometry
    out_plan = out_geometry[0]
    count, out_count = part_count(plan), part_count(out_plan)
    weights, refs = refs[:count], refs[count:]
    if not first:
        res_in, gn_in = refs[:2]
        refs = refs[2:]
    res_ref, gn_ref = refs[:2]
    grads, refs = refs[2 : 2 + out_count], refs[2 + out_count :]
    gate_m, up_m, down_m, d_gate, d_up, d_down, h_m, gg_m, gu_m, sems = refs
    own = own_ref[0]
    targets = (gate_m, up_m, down_m)

    @pl.when(pl.program_id(0) == 0)
    def _():
        d_gate[...] = jnp.zeros_like(d_gate)
        d_up[...] = jnp.zeros_like(d_up)
        d_down[...] = jnp.zeros_like(d_down)
        copy_all(slot_pairs(own, plan, weights, segments, n_ctx, targets), sems)

    n = n_ref[...]
    go = go_ref[...]
    hidden_count = gate_m.shape[1]
    step = 256
    for start in range(0, hidden_count, step):
        cols = slice(start, start + step)
        g = jnp.dot(n, gate_m[:, cols], preferred_element_type=f32)
        u = jnp.dot(n, up_m[:, cols], preferred_element_type=f32)
        gh = lax.dot_general(go, down_m[cols, :], NT, preferred_element_type=f32)
        s = jax.nn.sigmoid(g)
        act = g * s
        h_m[:, cols] = (act * u).astype(bf16)
        gg_m[:, cols] = (gh * u * s * (1.0 + g * (1.0 - s))).astype(bf16)
        gu_m[:, cols] = (gh * act).astype(bf16)
    res = jnp.dot(h_m[...], down_m[...], preferred_element_type=f32)
    gn = lax.dot_general(gg_m[...], gate_m[...], NT, preferred_element_type=f32)
    gn = gn + lax.dot_general(gu_m[...], up_m[...], NT, preferred_element_type=f32)
    if not first:
        res = res_in[...] + res
        gn = gn_in[...] + gn
    res_ref[...] = res
    gn_ref[...] = gn
    d_gate[...] += lax.dot_general(n, gg_m[...], TN, preferred_element_type=f32)
    d_up[...] += lax.dot_general(n, gu_m[...], TN, preferred_element_type=f32)
    d_down[...] += lax.dot_general(h_m[...], go, TN, preferred_element_type=f32)

    @pl.when(pl.program_id(0) == pl.num_programs(0) - 1)
    def _():
        gate_m[...] = d_gate[...].astype(bf16)
        up_m[...] = d_up[...].astype(bf16)
        down_m[...] = d_down[...].astype(bf16)
        pairs = slot_pairs(own, out_plan, grads, segments, n_ctx, targets)
        copy_all([(b, a) for a, b in pairs], sems)


def ffn_chunk(own, nffn, go, weights, totals, geometry, out_geometry, hidden_count, rows=256):
    total, width = nffn.shape
    first = totals is None
    plan, segments, _ = geometry
    out_plan = out_geometry[0]
    count, out_count = part_count(plan), part_count(out_plan)
    lanes = weights[0].shape[-1]
    row_spec = pl.BlockSpec((rows, width), lambda i, o: (i, 0))
    any_spec = pl.BlockSpec(memory_space=pl.ANY)
    outs = pl.pallas_call(
        functools.partial(ffn_kernel, geometry, out_geometry, first),
        out_shape=[jax.ShapeDtypeStruct((total, width), f32)] * 2
        + [jax.ShapeDtypeStruct(s, bf16) for s in part_shapes(out_plan, lanes)],
        grid_spec=pltpu.PrefetchScalarGridSpec(
            num_scalar_prefetch=1,
            grid=(total // rows,),
            in_specs=[row_spec] * 2 + [any_spec] * count + [row_spec] * (0 if first else 2),
            out_specs=[row_spec] * 2 + [any_spec] * out_count,
            scratch_shapes=[
                pltpu.VMEM((width, hidden_count), bf16),
                pltpu.VMEM((width, hidden_count), bf16),
                pltpu.VMEM((hidden_count, width), bf16),
                pltpu.VMEM((width, hidden_count), f32),
                pltpu.VMEM((width, hidden_count), f32),
                pltpu.VMEM((hidden_count, width), f32),
                pltpu.VMEM((rows, hidden_count), bf16),
                pltpu.VMEM((rows, hidden_count), bf16),
                pltpu.VMEM((rows, hidden_count), bf16),
                pltpu.SemaphoreType.DMA((max(len(plan), len(out_plan)) * len(segments),)),
            ],
        ),
        input_output_aliases={} if first else {3 + count: 0, 4 + count: 1},
        compiler_params=pltpu.CompilerParams(
            vmem_limit_bytes=VMEM_LIMIT, dimension_semantics=("arbitrary",)
        ),
        cost_estimate=SMALL_COST,
    )(own, nffn, go, *weights, *(() if first else totals))
    return (outs[0], outs[1]), outs[2:]


def move_kernel(geometry, count, outward, own_ref, *refs):
    plan, segments, n_ctx = geometry
    sems = refs[-1]
    refs = refs[:-1]
    if outward:
        targets, parts = refs[: len(refs) - count], refs[len(refs) - count :]
    else:
        parts, targets = refs[:count], refs[count:]
    pairs = slot_pairs(own_ref[0], plan, parts, segments, n_ctx, targets)
    copy_all([(b, a) for a, b in pairs] if outward else pairs, sems)


def move(own, arrays, shapes, geometry, count, outward):
    plan, segments, _ = geometry
    any_spec = pl.BlockSpec(memory_space=pl.ANY)
    vmem_spec = pl.BlockSpec(memory_space=pltpu.VMEM)
    return pl.pallas_call(
        functools.partial(move_kernel, geometry, count, outward),
        out_shape=[jax.ShapeDtypeStruct(s, bf16) for s in shapes],
        in_specs=[pl.BlockSpec(memory_space=pltpu.SMEM)]
        + [vmem_spec if outward else any_spec] * len(arrays),
        out_specs=[any_spec if outward else vmem_spec] * len(shapes),
        scratch_shapes=[pltpu.SemaphoreType.DMA((len(plan) * len(segments),))],
        compiler_params=pltpu.CompilerParams(vmem_limit_bytes=VMEM_LIMIT),
        cost_estimate=SMALL_COST,
    )(own, *arrays)


def shifted_down(block, before):
    row = lax.broadcasted_iota(jnp.int32, block.shape, 0)
    one = jnp.where(row == 0, before[1:2], pltpu.roll(block, 1, 0))
    two = jnp.where(row == 0, before[0:1], pltpu.roll(block, 2, 0))
    return one, jnp.where(row == 1, before[1:2], two)


def shifted_up(block, behind):
    count = block.shape[0]
    row = lax.broadcasted_iota(jnp.int32, block.shape, 0)
    one = jnp.where(row == count - 1, behind[0:1], pltpu.roll(block, count - 1, 0))
    two = jnp.where(row == count - 2, behind[0:1], pltpu.roll(block, count - 2, 0))
    return one, jnp.where(row == count - 1, behind[1:2], two)


def in_kernel(x_ref, gain_ref, w_ref, normed_ref, projected_ref):
    x = x_ref[...].astype(f32)
    scale = lax.rsqrt(jnp.mean(x * x, axis=-1, keepdims=True) + EPSILON)
    normed = (x * scale * gain_ref[...]).astype(bf16)
    normed_ref[...] = normed
    projected_ref[...] = jnp.dot(normed, w_ref[...], preferred_element_type=f32)


def conv_kernel(projected_ref, before_ref, taps_ref, w_ref, mixer_ref, conv_ref, branch_ref):
    channels = conv_ref.shape[1]
    product = projected_ref[:, :channels] * projected_ref[:, 2 * channels :]
    one, two = shifted_down(product, before_ref[0].astype(f32))
    conv = taps_ref[0:1] * two + taps_ref[1:2] * one + taps_ref[2:3] * product
    conv_ref[...] = conv
    mixer = (projected_ref[:, channels : 2 * channels] * conv).astype(bf16)
    mixer_ref[...] = mixer
    branch_ref[...] = jnp.dot(mixer, w_ref[...], preferred_element_type=f32).astype(bf16)


def norm_kernel(x_ref, branch_ref, got_ref, gain_ref, residual_ref, normed_ref):
    residual = x_ref[...].astype(f32) + (branch_ref[...].astype(f32) + got_ref[...].astype(f32))
    residual_ref[...] = residual
    scale = lax.rsqrt(jnp.mean(residual * residual, axis=-1, keepdims=True) + EPSILON)
    normed_ref[...] = (residual * scale * gain_ref[...]).astype(bf16)


def branch_grad_kernel(
    own_first, gn_ref, got_ref, residual_ref, go_ref, gain_ref, mixer_ref, conv_ref, gate_c_ref,
    w_ref, grad_residual_ref, grad_conv_ref, grad_c_ref, grad_w_ref, grad_gain_ref, total_ref,
):
    step = pl.program_id(0)

    @pl.when(step == 0)
    def _():
        total_ref[...] = jnp.zeros_like(total_ref)
        grad_gain_ref[...] = jnp.zeros_like(grad_gain_ref)

    incoming = gn_ref[...] + got_ref[...].astype(f32)
    residual = residual_ref[...]
    scale = lax.rsqrt(jnp.mean(residual * residual, axis=-1, keepdims=True) + EPSILON)
    weighted = incoming * gain_ref[...]

    @pl.when(step >= own_first)
    def _():
        grad_gain_ref[...] += jnp.sum(incoming * residual * scale, axis=0, keepdims=True)

    inner = jnp.mean(weighted * residual, axis=-1, keepdims=True)
    grad_residual = go_ref[...].astype(f32) + (
        scale * weighted - residual * (scale * scale * scale) * inner
    )
    grad_residual_ref[...] = grad_residual
    grad_branch = grad_residual.astype(bf16)
    grad_mix = lax.dot_general(grad_branch, w_ref[...], NT, preferred_element_type=f32)
    grad_c_ref[...] = (grad_mix * conv_ref[...]).astype(bf16)
    grad_conv_ref[...] = grad_mix * gate_c_ref[...]
    total_ref[...] += lax.dot_general(mixer_ref[...], grad_branch, TN, preferred_element_type=f32)

    @pl.when(step == pl.num_programs(0) - 1)
    def _():
        grad_w_ref[...] = total_ref[...].astype(bf16)


def in_grad_kernel(
    geometry, count, own_ref, grad_conv_ref, behind_ref, before_ref, projected_ref, grad_c_ref,
    normed_ref, taps_ref, grad_projected_ref, grad_taps_ref, *refs
):
    parts, (total_ref, low_ref, sems) = refs[:count], refs[count:]
    plan, segments, n_ctx = geometry
    step = pl.program_id(0)

    @pl.when(step == 0)
    def _():
        total_ref[...] = jnp.zeros_like(total_ref)
        grad_taps_ref[...] = jnp.zeros_like(grad_taps_ref)

    channels = grad_c_ref.shape[1]
    grad_conv = grad_conv_ref[...]
    gate_b = projected_ref[:, :channels]
    values = projected_ref[:, 2 * channels :]
    product = gate_b * values
    one, two = shifted_down(product, before_ref[0].astype(f32))
    for k, shifted in enumerate((two, one, product)):
        grad_taps_ref[k : k + 1] += jnp.sum(grad_conv * shifted, axis=0, keepdims=True)
    one, two = shifted_up(grad_conv, behind_ref[0].astype(f32))
    grad_product = taps_ref[2:3] * grad_conv + taps_ref[1:2] * one + taps_ref[0:1] * two
    grad_projected_ref[:, :channels] = (grad_product * values).astype(bf16)
    grad_projected_ref[:, channels : 2 * channels] = grad_c_ref[...]
    grad_projected_ref[:, 2 * channels :] = (grad_product * gate_b).astype(bf16)
    total_ref[...] += lax.dot_general(
        normed_ref[...], grad_projected_ref[...], TN, preferred_element_type=f32
    )

    @pl.when(step == pl.num_programs(0) - 1)
    def _():
        low_ref[...] = total_ref[...].astype(bf16)
        pairs = slot_pairs(own_ref[0], plan, parts, segments, n_ctx, (low_ref,))
        copy_all([(b, a) for a, b in pairs], sems)


def row_call(body, steps, ins, outs, scratch=()):
    return pl.pallas_call(
        body,
        grid=(steps,),
        in_specs=[
            pl.BlockSpec(memory_space=pltpu.SMEM) if block is None else pl.BlockSpec(block, place)
            for _, block, place in ins
        ],
        out_specs=[
            pl.BlockSpec(memory_space=pl.ANY) if block is None else pl.BlockSpec(block, place)
            for _, _, block, place in outs
        ],
        out_shape=[jax.ShapeDtypeStruct(shape, dtype) for shape, dtype, _, _ in outs],
        scratch_shapes=list(scratch),
        compiler_params=pltpu.CompilerParams(
            vmem_limit_bytes=VMEM_LIMIT, dimension_semantics=("arbitrary",)
        ),
        cost_estimate=SMALL_COST,
    )(*[a for a, _, _ in ins])


def fits(tokens, w_in, w_out, w_gate, w_down, n_dp, n_ctx):
    width, hidden = w_gate.shape
    if n_dp % 2 or n_dp % (2 * n_ctx) or n_dp & (n_dp - 1) or n_ctx & (n_ctx - 1) or n_ctx < 2:
        return False
    depth = width // n_dp
    if width % n_dp or hidden % (n_dp * CHUNKS * 48) or w_in.shape[1] % (2 * n_ctx * 256):
        return False
    lanes = hidden // n_dp // CHUNKS * (n_dp // n_ctx // 2)
    wide = width // n_ctx
    return (
        lanes % 128 == 0
        and wide == lanes + 128
        and lanes == 384
        and wide % 256 == 0
        and depth % 16 == 0
        and 2 * depth <= 256
        and (w_in.shape[1] // n_ctx) % (2 * depth) == 0
        and width % (2 * depth) == 0
        and tokens.shape[1] % n_ctx == 0
    )


def fast_shards(tokens, w_in, w_out, w_gate, w_up, w_down, gain_mix, gain_ffn, kernel, cotangent):
    seqs, piece, width = tokens.shape
    rows = seqs * piece
    n_chip, n_ctx = lax.axis_size("chip"), lax.axis_size("ctx")
    slots = n_chip * n_ctx
    core = lax.axis_index("core")
    own_slot = lax.axis_index("chip") * n_ctx + lax.axis_index("ctx")
    own = own_slot.astype(jnp.int32)[None]
    depth = w_in.shape[0]
    groups = n_chip // n_ctx
    sub = w_down.shape[0] // CHUNKS
    lanes = groups * sub
    wide = w_out.shape[1]
    in_cols = w_in.shape[1] // 2
    in_parts, out_parts = in_cols // 256, wide // 256
    hidden_count = n_chip * sub
    channels = width // 2

    def mine_other(pair):
        return jnp.where(core == 0, pair[0], pair[1]), jnp.where(core == 0, pair[1], pair[0])

    def in_core_order(mine, other, axis):
        return jnp.where(
            core == 0,
            jnp.concatenate([mine, other], axis=axis),
            jnp.concatenate([other, mine], axis=axis),
        )

    small = jnp.concatenate([gain_mix[None], gain_ffn[None], kernel], axis=0)
    in_pair = w_in.reshape(depth, in_cols // depth, 2, depth).transpose(2, 0, 1, 3)
    in_pair = in_pair.reshape(2, depth, in_parts, 256).transpose(0, 2, 1, 3)
    in_mine, in_other = mine_other(in_pair)
    small_rows = jnp.pad(small, ((0, 11), (0, 256 - depth)))
    swapped = swap(jnp.concatenate([in_other.reshape(in_parts * depth, 256), small_rows], axis=0))
    in_got = swapped[: in_parts * depth].reshape(in_parts, depth, 256)
    in_block = in_core_order(in_mine, in_got, 1).reshape(in_parts * 2 * depth, 256)
    small_block = in_core_order(small, swapped[in_parts * depth :][:5, :depth], 1)
    small_block = jnp.pad(small_block, ((0, 11), (0, 256 - 2 * depth)))
    out_block = w_out.reshape(depth, out_parts, 256).transpose(1, 0, 2).reshape(-1, 256)
    mix_block = jnp.concatenate([in_block, small_block], axis=0)

    both = jnp.stack([w_gate, w_up]).reshape(2, depth, groups, 2, CHUNKS, sub)
    both = both.transpose(3, 4, 0, 1, 2, 5).reshape(2, CHUNKS, 2, depth, lanes)
    both_mine, both_other = mine_other(both)
    both_block = in_core_order(both_mine, swap(both_other), 2)
    both_block = both_block.reshape(CHUNKS, 4 * depth, lanes)
    down = w_down.reshape(CHUNKS, sub, wide)
    down_rest = down[:, :, lanes:].reshape(CHUNKS, 3, sub // 3, 128).transpose(0, 2, 1, 3)
    chunk_blocks = jnp.concatenate(
        [both_block, down[:, :, :lanes], down_rest.reshape(CHUNKS, sub // 3, lanes)], axis=1
    )

    mix_rows = mix_block.shape[0]
    mix_cut = in_parts * depth
    in_rows = in_parts * 2 * depth
    mix_segments = [
        (k * 2 * depth, 2 * depth, 0, 256, 0, 2 * depth, 0, in_cols, 256 * k)
        for k in range(in_parts)
    ]
    out_segments = [
        (k * depth, depth, 0, 256, 0, depth, 0, wide, 256 * k) for k in range(out_parts)
    ]
    small_segment = (in_rows, 16, 0, 256, 1, 16, 0, 256, 0)
    mix_plan = gather_plan(mix_cut, mix_rows)
    chunk_rows = chunk_blocks.shape[1]
    chunk_cut = chunk_rows // 2
    chunk_segments = [
        (0, 2 * depth, 0, lanes, 0, 2 * depth, 0, lanes, 0),
        (2 * depth, 2 * depth, 0, lanes, 1, 2 * depth, 0, lanes, 0),
        (4 * depth, sub, 0, lanes, 2, sub, 0, wide, 0),
    ] + [
        (4 * depth + sub, sub // 3, 128 * k, 128, 2, sub, k * (sub // 3), wide, lanes)
        for k in range(3)
    ]
    whole_plan = [(0, i, None, 0, chunk_rows) for i in range(slots)]
    whole_geometry = (whole_plan, chunk_segments, n_ctx)
    step_geometry = (gather_plan(chunk_cut, chunk_rows), chunk_segments, n_ctx)

    out_all = lax.all_gather(out_block, ("chip", "ctx"))

    far, first_order, second_order = bit_masks()

    def doubled(hold, got):
        return jnp.concatenate([hold, got], axis=0)

    hold = mix_block[None]
    for mask in far:
        hold = doubled(hold, across(hold, mask))
    mix_halves = [hold[:, :mix_cut], hold[:, mix_cut:]]
    next_hold = after(chunk_blocks[0][None], hold)
    chunk_all = [
        lax.all_gather(after(block, hold), ("chip", "ctx")) for block in chunk_blocks[1:]
    ]
    far_left = list(far)
    mix_parts = []
    for step in range(len(first_order)):
        got = [across(h, order[step]) for h, order in zip(mix_halves, (first_order, second_order))]
        if far_left:
            next_got = across(next_hold, far_left.pop(0))
            next_hold = doubled(next_hold, next_got)
            if step + 1 < len(first_order):
                got = [after(g, next_got) for g in got]
        if step + 1 < len(first_order):
            mix_halves = [doubled(h, g) for h, g in zip(mix_halves, got)]
            next_hold = after(next_hold, *got)
        else:
            mix_parts = [mix_halves[0], got[0], mix_halves[1], got[1]]
    for mask in far_left:
        next_hold = doubled(next_hold, across(next_hold, mask))
    in_half, small_all = move(
        own,
        mix_parts,
        [(width, n_ctx * in_cols), (n_chip * 16, n_ctx * 256)],
        (mix_plan, mix_segments + [small_segment], n_ctx),
        4,
        False,
    )
    (out_half,) = move(
        own,
        [out_all],
        [(channels, width)],
        ([(0, i, None, 0, out_parts * depth) for i in range(slots)], out_segments, n_ctx),
        1,
        False,
    )
    next_halves = [next_hold[:, :chunk_cut], next_hold[:, chunk_cut:]]
    next_orders = (first_order, second_order)

    def next_step(step, done):
        got = [across(h, o[step]) for h, o in zip(next_halves, next_orders)]
        return [after(g, done) for g in got]

    small_all = small_all.reshape(n_chip, 16, n_ctx * 256)[:, :5, : 2 * depth].astype(f32)
    first_gain = small_all[:, 0].reshape(width)
    second_gain = small_all[:, 1].reshape(width)
    taps = small_all[:, 2:].reshape(n_chip, 3, 2, depth)
    taps = jnp.where(core == 0, taps[:, :, 0], taps[:, :, 1]).transpose(1, 0, 2)
    taps = taps.reshape(3, channels)

    token_rows = tokens.reshape(rows, width)
    inputs = jnp.concatenate([token_rows, swap(token_rows)], axis=0)
    go_rows = cotangent.reshape(rows, width)
    go = jnp.concatenate([go_rows, swap(go_rows)], axis=0)
    blocks = 2 * seqs

    def at(i):
        return (i, 0)

    def still(i):
        return (0, 0)

    def other(i):
        return ((i + seqs) % blocks, 0)

    wide_rows, thin_rows = (piece, width), (piece, channels)
    taps = jnp.pad(taps, ((0, 5), (0, 0)))
    normed_low, projected = row_call(
        in_kernel,
        blocks,
        [
            (inputs, wide_rows, at),
            (first_gain[None], (1, width), still),
            (in_half, in_half.shape, still),
        ],
        [
            ((2 * rows, width), bf16, wide_rows, at),
            ((2 * rows, 3 * channels), f32, (piece, 3 * channels), at),
        ],
    )
    next_got = next_step(0, projected)
    tail = projected.reshape(blocks, piece, 3 * channels)[:, piece - 2 :]
    tail = (tail[:, :, :channels] * tail[:, :, 2 * channels :]).astype(bf16)
    before = passed_along(tail, "ctx", 1)
    halo = (1, 2, channels)

    def halo_at(i):
        return (i, 0, 0)

    mixer_out, convolved, branch = row_call(
        conv_kernel,
        blocks,
        [
            (projected, (piece, 3 * channels), at),
            (before, halo, halo_at),
            (taps, taps.shape, still),
            (out_half, out_half.shape, still),
        ],
        [
            ((2 * rows, channels), bf16, thin_rows, at),
            ((2 * rows, channels), f32, thin_rows, at),
            ((2 * rows, width), bf16, wide_rows, at),
        ],
    )
    residual, nffn_low = row_call(
        norm_kernel,
        blocks,
        [
            (inputs, wide_rows, at),
            (branch, wide_rows, at),
            (swap(branch), wide_rows, other),
            (second_gain[None], (1, width), still),
        ],
        [((2 * rows, width), f32, wide_rows, at), ((2 * rows, width), bf16, wide_rows, at)],
    )

    for step in range(1, len(first_order)):
        next_halves = [doubled(h, g) for h, g in zip(next_halves, next_got)]
        next_got = next_step(step, nffn_low)
    next_parts = [next_halves[0], next_got[0], next_halves[1], next_got[1]]
    totals, first_grads = ffn_chunk(
        own, nffn_low, go, next_parts, None, step_geometry, step_geometry, hidden_count
    )
    totals, second_grads = ffn_chunk(
        own, nffn_low, go, [chunk_all[0]], totals, whole_geometry, step_geometry, hidden_count
    )
    second_total = totals[1]
    totals, last_grads = ffn_chunk(
        own, nffn_low, go, [chunk_all[1]], totals, whole_geometry, step_geometry, hidden_count
    )
    ffn_out, grad_nffn = totals
    grad_got = swap(grad_nffn.astype(bf16))
    ffn_got = swap(ffn_out[rows:].astype(bf16))

    def turned(i):
        return ((i + seqs) % blocks, 0)

    def turned_back(i):
        return (i, 0)

    def own_place(i):
        return (jnp.maximum(i - seqs, 0), 0)

    def gate_c_place(i):
        return ((i + seqs) % blocks, 1)

    grad_residual, grad_conv, grad_c, grad_w_out, grad_gain_ffn = row_call(
        functools.partial(branch_grad_kernel, seqs),
        blocks,
        [
            (grad_nffn, wide_rows, turned),
            (grad_got, wide_rows, turned_back),
            (residual, wide_rows, turned),
            (go, wide_rows, turned),
            (second_gain[None], (1, width), still),
            (mixer_out, thin_rows, turned),
            (convolved, thin_rows, turned),
            (projected, thin_rows, gate_c_place),
            (out_half, out_half.shape, still),
        ],
        [
            ((rows, width), f32, wide_rows, own_place),
            ((2 * rows, channels), f32, thin_rows, turned),
            ((2 * rows, channels), bf16, thin_rows, turned),
            ((channels, width), bf16, (channels, width), still),
            ((1, width), f32, (1, width), still),
        ],
        scratch=[pltpu.VMEM((channels, width), f32)],
    )
    grad_gain_ffn = grad_gain_ffn[0]
    head = grad_conv.reshape(blocks, piece, channels)[:, :2].astype(bf16)
    behind = passed_along(head, "ctx", -1)
    grad_out_slots = grad_w_out.reshape(n_chip, depth, n_ctx, out_parts, 256)
    grad_out_slots = grad_out_slots.transpose(0, 2, 3, 1, 4).reshape(slots, out_parts * depth, 256)
    out_sum = lax.psum_scatter(grad_out_slots, ("chip", "ctx"), scatter_dimension=0).astype(f32)
    sum_plan = gather_plan(mix_cut, in_rows)
    grad_projected, grad_kernel, *mix_grad_parts = row_call(
        functools.partial(in_grad_kernel, (sum_plan, mix_segments, n_ctx), 4),
        blocks,
        [
            (own, None, None),
            (grad_conv, thin_rows, at),
            (behind, halo, halo_at),
            (before, halo, halo_at),
            (projected, (piece, 3 * channels), at),
            (grad_c, thin_rows, at),
            (normed_low, wide_rows, at),
            (taps, taps.shape, still),
        ],
        [
            ((2 * rows, 3 * channels), bf16, (piece, 3 * channels), at),
            ((8, channels), f32, (8, channels), still),
        ]
        + [(shape, bf16, None, None) for shape in part_shapes(sum_plan, 256)],
        scratch=[
            pltpu.VMEM((width, 3 * channels), f32),
            pltpu.VMEM((width, 3 * channels), bf16),
            pltpu.SemaphoreType.DMA((len(sum_plan) * len(mix_segments),)),
        ],
    )
    grad_kernel = grad_kernel[:3]
    first_sum = scatter_sum(
        first_grads, (second_total, grad_nffn, grad_c, grad_projected, grad_projected)
    )
    second_sum = scatter_sum(second_grads, (grad_nffn, grad_c, grad_projected))
    last_sum = scatter_sum(last_grads, (grad_c, grad_projected))
    mix_sum = scatter_sum(mix_grad_parts)
    late_projected = after(grad_projected, mix_grad_parts[1])
    grad_normed = cross_cols(late_projected[rows:], in_half).astype(bf16)
    grad_normed = cross_cols(late_projected[:rows], in_half) + swap(grad_normed).astype(f32)
    result = residual[:rows] + (ffn_out[:rows] + ffn_got.astype(f32))
    result = result.astype(bf16).reshape(seqs, piece, width)
    own_inputs = token_rows.astype(f32)
    scale_mix = lax.rsqrt(jnp.mean(own_inputs * own_inputs, axis=-1, keepdims=True) + EPSILON)
    grad_in_norm, grad_gain_mix = norm_backward(own_inputs, scale_mix, first_gain, grad_normed)
    grad_tokens = (grad_residual + grad_in_norm).reshape(seqs, piece, width)

    chunk_sum = jnp.stack([first_sum, second_sum, last_sum])
    both_sum = chunk_sum[:, : 4 * depth].reshape(CHUNKS, 2, 2, depth, lanes).transpose(2, 0, 1, 3, 4)
    both_mine, both_other = mine_other(both_sum)
    both_got = swap(both_other)
    both_sum = in_core_order(both_mine[None], both_got[None], 0)
    both_sum = both_sum.reshape(2, CHUNKS, 2, depth, groups, sub).transpose(2, 3, 4, 0, 1, 5)
    both_sum = both_sum.reshape(2, depth, 2 * CHUNKS * lanes)
    down_rest = chunk_sum[:, 4 * depth + sub :].reshape(CHUNKS, sub // 3, 3, 128)
    down_rest = down_rest.transpose(0, 2, 1, 3).reshape(CHUNKS, sub, 128)
    final_down = jnp.concatenate([chunk_sum[:, 4 * depth : 4 * depth + sub], down_rest], axis=2)
    final_down = final_down.reshape(CHUNKS * sub, wide)

    in_sum = mix_sum.reshape(in_parts, 2, depth, 256).transpose(1, 0, 2, 3)
    in_mine, in_other = mine_other(in_sum)
    in_sum = in_core_order(in_mine[None], swap(in_other)[None], 0)
    in_sum = in_sum.transpose(0, 2, 1, 3).reshape(2, depth, in_cols // depth, depth)
    final_in = in_sum.transpose(1, 2, 0, 3).reshape(depth, 2 * in_cols)
    final_out = out_sum.reshape(out_parts, depth, 256).transpose(1, 0, 2)
    final_out = final_out.reshape(depth, wide)

    grad_taps = grad_kernel.reshape(3, n_chip, 1, depth)
    grad_taps = jnp.where(
        jnp.arange(2).reshape(1, 1, 2, 1) == core, grad_taps, jnp.zeros_like(grad_taps)
    ).reshape(3, width)
    small_grad = jnp.concatenate([grad_gain_mix[None], grad_gain_ffn[None], grad_taps], axis=0)
    small_sum = small_grad.reshape(5, n_chip, 2 * depth).transpose(1, 0, 2)
    for bit in range(n_ctx.bit_length() - 1):
        small_sum = small_sum + across(small_sum, 1 << bit)
    for bit in range(n_chip.bit_length() - 1):
        mask = n_chip >> (bit + 1)
        low, high = small_sum[: small_sum.shape[0] // 2], small_sum[small_sum.shape[0] // 2 :]
        upper = jnp.bitwise_and(lax.axis_index("chip"), mask) != 0
        small_sum = jnp.where(upper, high, low) + across(jnp.where(upper, low, high), mask * n_ctx)
    small_mine, small_other = mine_other(small_sum[0].reshape(5, 2, depth).transpose(1, 0, 2))
    small_sum = small_mine + swap(small_other)
    return (
        result,
        grad_tokens,
        final_in,
        final_out,
        both_sum[0],
        both_sum[1],
        final_down,
        small_sum[0],
        small_sum[1],
        small_sum[2:5],
    )


def solution(mesh):
    n_dp, n_ctx = mesh.shape["dp"], mesh.shape["ctx"]

    def placed(dp):
        whole, cut = P(dp, "ctx", None), P(dp, "ctx")
        ins = (whole, cut, cut, cut, cut, cut, P(dp), P(dp), P(None, dp), whole)
        outs = (whole, whole, cut, cut, cut, cut, cut, P(dp), P(dp), P(None, dp))
        return ins, outs

    def run(tokens, w_in, w_out, w_gate, w_up, w_down, gain_mix, gain_ffn, kernel, cotangent):
        if fits(tokens, w_in, w_out, w_gate, w_down, n_dp, n_ctx):
            cut_mesh = Mesh(mesh.devices.reshape(n_dp // 2, 2, n_ctx), ("chip", "core", "ctx"))
            body, on, (ins, outs) = fast_shards, cut_mesh, placed(("chip", "core"))
        else:
            body, on, (ins, outs) = plain_shards, mesh, placed("dp")
        call = jax.shard_map(body, mesh=on, in_specs=ins, out_specs=outs, check_vma=False)
        return call(
            tokens, w_in, w_out, w_gate, w_up, w_down, gain_mix, gain_ffn, kernel, cotangent
        )

    return run
```

```python
import functools
import jax
import jax.numpy as jnp
from jax import lax
from jax.experimental import pallas as pl
from jax.experimental.pallas import tpu as pltpu
from jax.sharding import Mesh
from jax.sharding import PartitionSpec as P

EPSILON = 1e-05
CHUNKS = 3
f32 = jnp.float32
bf16 = jnp.bfloat16


def passed_along(block, axis, distance):
    devices = range(lax.axis_size(axis))
    route = [(i - distance, i) for i in devices if i - distance in devices]
    return lax.ppermute(block, axis, route)


def cross_rows(left_operand, right_operand):
    return lax.dot_general(
        left_operand, right_operand, (((0,), (0,)), ((), ())), preferred_element_type=jnp.float32
    )


def cross_cols(left_operand, right_operand):
    return lax.dot_general(
        left_operand, right_operand, (((1,), (1,)), ((), ())), preferred_element_type=jnp.float32
    )


def norm_forward(values, gain):
    scale = lax.rsqrt(jnp.mean(values * values, axis=-1, keepdims=True) + EPSILON)
    return (values * scale * gain, scale)


def norm_backward(values, scale, gain, incoming):
    weighted = incoming * gain
    gain_grad = jnp.sum(incoming * values * scale, axis=0)
    inner = jnp.mean(weighted * values, axis=-1, keepdims=True)
    return (scale * weighted - values * (scale * scale * scale) * inner, gain_grad)


def plain_shards(tokens, w_in, w_out, w_gate, w_up, w_down, gain_mix, gain_ffn, kernel, cotangent):
    seq_count, piece_len, model_width = tokens.shape
    row_count = seq_count * piece_len
    small_params = jnp.concatenate([gain_mix[None], gain_ffn[None], kernel], axis=0)
    input_columns, out_cols, gate_cols, up_cols, down_cols = (
        lax.all_gather(w_in, "ctx", axis=1, tiled=True),
        lax.all_gather(w_out, "ctx", axis=1, tiled=True),
        lax.all_gather(w_gate, "ctx", axis=1, tiled=True),
        lax.all_gather(w_up, "ctx", axis=1, tiled=True),
        lax.all_gather(w_down, "ctx", axis=1, tiled=True),
    )
    full_in, full_out, full_gate, full_up, full_down, small_full = (
        lax.all_gather(input_columns, "dp", axis=0, tiled=True),
        lax.all_gather(out_cols, "dp", axis=0, tiled=True),
        lax.all_gather(gate_cols, "dp", axis=0, tiled=True),
        lax.all_gather(up_cols, "dp", axis=0, tiled=True),
        lax.all_gather(down_cols, "dp", axis=0, tiled=True),
        lax.all_gather(small_params, "dp", axis=1, tiled=True),
    )
    small_float = small_full.astype(jnp.float32)
    first_gain = small_float[0]
    second_gain = small_float[1]
    taps = small_float[2:5]
    inputs = tokens.reshape(row_count, model_width).astype(jnp.float32)
    normed, scale_mix = norm_forward(inputs, first_gain)
    normed_low = normed.astype(jnp.bfloat16)
    projected = jnp.dot(normed_low, full_in, preferred_element_type=jnp.float32)
    gate_b = projected[:, :model_width]
    gate_c = projected[:, model_width : 2 * model_width]
    values = projected[:, 2 * model_width :]
    product = (gate_b * values).reshape(seq_count, piece_len, model_width)
    previous = passed_along(product[:, piece_len - 2 :].astype(jnp.bfloat16), "ctx", 1).astype(
        jnp.float32
    )
    padded = jnp.concatenate([previous, product], axis=1)
    convolved = taps[0] * padded[:, :-2] + taps[1] * padded[:, 1:-1] + taps[2] * padded[:, 2:]
    convolved = convolved.reshape(row_count, model_width)
    mixer_out = (gate_c * convolved).astype(jnp.bfloat16)
    residual = inputs + jnp.dot(mixer_out, full_out, preferred_element_type=jnp.float32)
    feedforward_normed, scale_ffn = norm_forward(residual, second_gain)
    nffn_low = feedforward_normed.astype(jnp.bfloat16)
    gate = jnp.dot(nffn_low, full_gate, preferred_element_type=jnp.float32)
    up_value = jnp.dot(nffn_low, full_up, preferred_element_type=jnp.float32)
    sigmoid_gate = jax.nn.sigmoid(gate)
    activated = gate * sigmoid_gate
    hidden = (activated * up_value).astype(jnp.bfloat16)
    result = residual + jnp.dot(hidden, full_down, preferred_element_type=jnp.float32)
    result = result.astype(jnp.bfloat16).reshape(seq_count, piece_len, model_width)
    back_in, output_backward, back_gate, back_up, back_down = (
        lax.all_gather(w_in, "ctx", axis=1, tiled=True),
        lax.all_gather(w_out, "ctx", axis=1, tiled=True),
        lax.all_gather(w_gate, "ctx", axis=1, tiled=True),
        lax.all_gather(w_up, "ctx", axis=1, tiled=True),
        lax.all_gather(w_down, "ctx", axis=1, tiled=True),
    )
    input_weight_used, use_out, use_gate, use_up, use_down = (
        lax.all_gather(back_in, "dp", axis=0, tiled=True),
        lax.all_gather(output_backward, "dp", axis=0, tiled=True),
        lax.all_gather(back_gate, "dp", axis=0, tiled=True),
        lax.all_gather(back_up, "dp", axis=0, tiled=True),
        lax.all_gather(back_down, "dp", axis=0, tiled=True),
    )
    grad_out = cotangent.reshape(row_count, model_width)
    grad_out_float = grad_out.astype(jnp.float32)
    grad_w_down = cross_rows(hidden, grad_out)
    grad_hidden = cross_cols(grad_out, use_down)
    grad_gate = (
        grad_hidden * up_value * sigmoid_gate * (1.0 + gate * (1.0 - sigmoid_gate))
    ).astype(jnp.bfloat16)
    grad_up = (grad_hidden * activated).astype(jnp.bfloat16)
    grad_w_gate = cross_rows(nffn_low, grad_gate)
    grad_w_up = cross_rows(nffn_low, grad_up)
    grad_nffn = cross_cols(grad_gate, use_gate) + cross_cols(grad_up, use_up)
    residual_norm_gradient, grad_gain_ffn = norm_backward(
        residual, scale_ffn, second_gain, grad_nffn
    )
    grad_residual = grad_out_float + residual_norm_gradient
    grad_branch = grad_residual.astype(jnp.bfloat16)
    grad_w_out = cross_rows(mixer_out, grad_branch)
    grad_mix = cross_cols(grad_branch, use_out)
    grad_c = grad_mix * convolved
    grad_conv = (grad_mix * gate_c).reshape(seq_count, piece_len, model_width)
    following = passed_along(grad_conv[:, :2].astype(jnp.bfloat16), "ctx", -1).astype(jnp.float32)
    extended = jnp.concatenate([grad_conv, following], axis=1)
    grad_product = (
        taps[2] * extended[:, :-2] + taps[1] * extended[:, 1:-1] + taps[0] * extended[:, 2:]
    )
    grad_kernel = jnp.stack(
        [
            jnp.sum(grad_conv * padded[:, shift_at : shift_at + piece_len], axis=(0, 1))
            for shift_at in range(3)
        ],
        axis=0,
    )
    grad_product = grad_product.reshape(row_count, model_width)
    grad_projected = jnp.concatenate(
        [grad_product * values, grad_c, grad_product * gate_b], axis=1
    ).astype(jnp.bfloat16)
    grad_w_in = cross_rows(normed_low, grad_projected)
    grad_normed = cross_cols(grad_projected, input_weight_used)
    grad_in_norm, grad_gain_mix = norm_backward(inputs, scale_mix, first_gain, grad_normed)
    grad_tokens = (grad_residual + grad_in_norm).reshape(seq_count, piece_len, model_width)
    small_grad = jnp.concatenate([grad_gain_mix[None], grad_gain_ffn[None], grad_kernel], axis=0)
    part_in, part_out, part_gate, part_up, part_down, small_part = (
        lax.psum_scatter(grad_w_in, "dp", scatter_dimension=0, tiled=True),
        lax.psum_scatter(grad_w_out, "dp", scatter_dimension=0, tiled=True),
        lax.psum_scatter(grad_w_gate, "dp", scatter_dimension=0, tiled=True),
        lax.psum_scatter(grad_w_up, "dp", scatter_dimension=0, tiled=True),
        lax.psum_scatter(grad_w_down, "dp", scatter_dimension=0, tiled=True),
        lax.psum_scatter(small_grad, "dp", scatter_dimension=1, tiled=True),
    )
    final_in, final_out, final_gate, final_up, final_down = (
        lax.psum_scatter(part_in, "ctx", scatter_dimension=1, tiled=True),
        lax.psum_scatter(part_out, "ctx", scatter_dimension=1, tiled=True),
        lax.psum_scatter(part_gate, "ctx", scatter_dimension=1, tiled=True),
        lax.psum_scatter(part_up, "ctx", scatter_dimension=1, tiled=True),
        lax.psum_scatter(part_down, "ctx", scatter_dimension=1, tiled=True),
    )
    small_total = lax.psum(small_part, "ctx")
    return (
        result,
        grad_tokens,
        final_in,
        final_out,
        final_gate,
        final_up,
        final_down,
        small_total[0],
        small_total[1],
        small_total[2:5],
    )


SMALL_COST = pl.CostEstimate(flops=1 << 16, bytes_accessed=1 << 16, transcendentals=0)
VMEM_LIMIT = 60 * 1024 * 1024
NT = (((1,), (1,)), ((), ()))
TN = (((0,), (0,)), ((), ()))


def swap(block):
    return lax.ppermute(block, "core", [(0, 1), (1, 0)])


def across(block, mask):
    count = lax.axis_size("chip") * lax.axis_size("ctx")
    return lax.ppermute(block, ("chip", "ctx"), [(i, i ^ mask) for i in range(count)])


def bit_masks():
    n_chip, n_ctx = lax.axis_size("chip"), lax.axis_size("ctx")
    ctx_bits = [1 << b for b in range(n_ctx.bit_length() - 1)]
    near = [n_ctx]
    far = [n_ctx << b for b in range(1, n_chip.bit_length() - 1)]
    return far, near + ctx_bits, ctx_bits + near


def after(value, *done):
    return lax.optimization_barrier((value, *done))[0]


def gather_plan(cut, total):
    far, first_order, second_order = bit_masks()
    plan = []
    for operand, order, row0, rows in ((0, first_order, 0, cut), (2, second_order, cut, total - cut)):
        masks = [0]
        for mask in far + order[:-1]:
            masks = masks + [m ^ mask for m in masks]
        for index, mask in enumerate(masks):
            plan.append((operand, index, mask, row0, rows))
            plan.append((operand + 1, index, mask ^ order[-1], row0, rows))
    return plan


def gather(block, cut):
    far, first_order, second_order = bit_masks()
    hold = block[None]
    for mask in far:
        hold = jnp.concatenate([hold, across(hold, mask)], axis=0)
    parts = []
    for order, half in ((first_order, hold[:, :cut]), (second_order, hold[:, cut:])):
        for mask in order[:-1]:
            half = jnp.concatenate([half, across(half, mask)], axis=0)
        parts += [half, across(half, order[-1])]
    return parts


def scatter_steps(parts):
    far, first_order, second_order = bit_masks()
    n_slots = lax.axis_size("chip") * lax.axis_size("ctx")

    def send(block, mask, senders=range(n_slots)):
        route = [(i, i ^ mask) for i in senders]
        return lax.ppermute(block.astype(bf16), ("chip", "ctx"), route)

    orders = (first_order, second_order)
    got = yield [send(parts[1], first_order[-1]), send(parts[3], second_order[-1])]
    keeps = [k.astype(f32) + g.astype(f32) for k, g in zip((parts[0], parts[2]), got)]
    for step in range(len(first_order) - 2, -1, -1):
        mid = keeps[0].shape[0] // 2
        got = yield [send(k[mid:], order[step]) for k, order in zip(keeps, orders)]
        keeps = [k[:mid] + g.astype(f32) for k, g in zip(keeps, got)]
    keep = jnp.concatenate(keeps, axis=1)
    if len(far) == 2:
        low, high = far
        outer = [i for i in range(n_slots) if (i & low == 0) == (i & high == 0)]
        inner = [i for i in range(n_slots) if i not in outer]
        (got,) = yield [send(keep[2:], low, outer)]
        distant = keep[2:] + got.astype(f32)[::-1]
        (got,) = yield [send(distant, low | high, inner)]
        keep = keep[:2] + got.astype(f32)[::-1]
        far = far[:1]
    for mask in reversed(far):
        mid = keep.shape[0] // 2
        (got,) = yield [send(keep[mid:], mask)]
        keep = keep[:mid] + got.astype(f32)
    return keep[0]


class Stages:
    def __init__(self, parts):
        self.steps = scatter_steps(parts)
        self.got = next(self.steps)
        self.total = None

    def advance(self, *done):
        try:
            self.got = self.steps.send([after(g, *done) for g in self.got])
        except StopIteration as end:
            self.got, self.total = [], end.value


def slot_pairs(own, plan, refs, segments, n_ctx, targets):
    pairs = []
    for operand, index, mask, row0, nrows in plan:
        slot = index if mask is None else jnp.bitwise_xor(own, mask)
        y = lax.rem(slot, n_ctx)
        chip = lax.div(slot, n_ctx)
        src = refs[operand].at[index]
        for seg_row, seg_rows, lane0, lanes, target, row_step, row_add, lane_step, lane_add in segments:
            low, high = max(seg_row, row0), min(seg_row + seg_rows, row0 + nrows)
            if low >= high:
                continue
            row = pl.multiple_of(chip * row_step + row_add + (low - seg_row), 16)
            lane = pl.multiple_of(y * lane_step + lane_add, 128)
            pairs.append(
                (
                    src.at[pl.ds(low - row0, high - low), pl.ds(lane0, lanes)],
                    targets[target].at[pl.ds(row, high - low), pl.ds(lane, lanes)],
                )
            )
    return pairs


def copy_all(pairs, sems):
    copies = [pltpu.make_async_copy(a, b, sems.at[i]) for i, (a, b) in enumerate(pairs)]
    for copy in copies:
        copy.start()
    for copy in copies:
        copy.wait()


def part_count(plan):
    return 1 + max(entry[0] for entry in plan)


def part_shapes(plan, lanes):
    shapes = {}
    for operand, index, _, _, rows in plan:
        shapes[operand] = (max(index + 1, shapes.get(operand, (0,))[0]), rows, lanes)
    return [shapes[operand] for operand in sorted(shapes)]


def ffn_kernel(geometry, out_geometry, first, last, own_ref, n_ref, go_ref, *refs):
    plan, segments, n_ctx = geometry
    out_plan = out_geometry[0]
    count, out_count = part_count(plan), part_count(out_plan)
    weights, refs = refs[:count], refs[count:]
    if not first:
        res_in, gn_in = refs[:2]
        refs = refs[2:]
    res_ref, gn_ref = refs[:2]
    refs = refs[2:]
    if last:
        res_low_ref, gn_low_ref = refs[:2]
        refs = refs[2:]
    grads, refs = refs[:out_count], refs[out_count:]
    gate_m, up_m, down_m, d_gate, d_up, d_down, h_m, gg_m, gu_m, sems = refs
    own = own_ref[0]
    targets = (gate_m, up_m, down_m)

    @pl.when(pl.program_id(0) == 0)
    def _():
        d_gate[...] = jnp.zeros_like(d_gate)
        d_up[...] = jnp.zeros_like(d_up)
        d_down[...] = jnp.zeros_like(d_down)
        copy_all(slot_pairs(own, plan, weights, segments, n_ctx, targets), sems)

    n = n_ref[...]
    go = go_ref[...]
    hidden_count = gate_m.shape[1]
    step = 256
    for start in range(0, hidden_count, step):
        cols = slice(start, start + step)
        g = jnp.dot(n, gate_m[:, cols], preferred_element_type=f32)
        u = jnp.dot(n, up_m[:, cols], preferred_element_type=f32)
        gh = lax.dot_general(go, down_m[cols, :], NT, preferred_element_type=f32)
        s = jax.nn.sigmoid(g)
        act = g * s
        h_m[:, cols] = (act * u).astype(bf16)
        gg_m[:, cols] = (gh * u * s * (1.0 + g * (1.0 - s))).astype(bf16)
        gu_m[:, cols] = (gh * act).astype(bf16)
    res = jnp.dot(h_m[...], down_m[...], preferred_element_type=f32)
    gn = lax.dot_general(gg_m[...], gate_m[...], NT, preferred_element_type=f32)
    gn = gn + lax.dot_general(gu_m[...], up_m[...], NT, preferred_element_type=f32)
    if not first:
        res = res_in[...] + res
        gn = gn_in[...] + gn
    res_ref[...] = res
    gn_ref[...] = gn
    if last:
        res_low_ref[...] = res.astype(bf16)
        gn_low_ref[...] = gn.astype(bf16)
    d_gate[...] += lax.dot_general(n, gg_m[...], TN, preferred_element_type=f32)
    d_up[...] += lax.dot_general(n, gu_m[...], TN, preferred_element_type=f32)
    d_down[...] += lax.dot_general(h_m[...], go, TN, preferred_element_type=f32)

    @pl.when(pl.program_id(0) == pl.num_programs(0) - 1)
    def _():
        gate_m[...] = d_gate[...].astype(bf16)
        up_m[...] = d_up[...].astype(bf16)
        down_m[...] = d_down[...].astype(bf16)
        pairs = slot_pairs(own, out_plan, grads, segments, n_ctx, targets)
        copy_all([(b, a) for a, b in pairs], sems)


def ffn_chunk(
    own, nffn, go, weights, totals, geometry, out_geometry, hidden_count, last=False, rows=256
):
    total, width = nffn.shape
    first = totals is None
    plan, segments, _ = geometry
    out_plan = out_geometry[0]
    count, out_count = part_count(plan), part_count(out_plan)
    lanes = weights[0].shape[-1]
    row_spec = pl.BlockSpec((rows, width), lambda i, o: (i, 0))
    any_spec = pl.BlockSpec(memory_space=pl.ANY)
    outs = pl.pallas_call(
        functools.partial(ffn_kernel, geometry, out_geometry, first, last),
        out_shape=[jax.ShapeDtypeStruct((total, width), f32)] * 2
        + [jax.ShapeDtypeStruct((total, width), bf16)] * (2 if last else 0)
        + [jax.ShapeDtypeStruct(s, bf16) for s in part_shapes(out_plan, lanes)],
        grid_spec=pltpu.PrefetchScalarGridSpec(
            num_scalar_prefetch=1,
            grid=(total // rows,),
            in_specs=[row_spec] * 2 + [any_spec] * count + [row_spec] * (0 if first else 2),
            out_specs=[row_spec] * (4 if last else 2) + [any_spec] * out_count,
            scratch_shapes=[
                pltpu.VMEM((width, hidden_count), bf16),
                pltpu.VMEM((width, hidden_count), bf16),
                pltpu.VMEM((hidden_count, width), bf16),
                pltpu.VMEM((width, hidden_count), f32),
                pltpu.VMEM((width, hidden_count), f32),
                pltpu.VMEM((hidden_count, width), f32),
                pltpu.VMEM((rows, hidden_count), bf16),
                pltpu.VMEM((rows, hidden_count), bf16),
                pltpu.VMEM((rows, hidden_count), bf16),
                pltpu.SemaphoreType.DMA((max(len(plan), len(out_plan)) * len(segments),)),
            ],
        ),
        input_output_aliases={} if first else {3 + count: 0, 4 + count: 1},
        compiler_params=pltpu.CompilerParams(
            vmem_limit_bytes=VMEM_LIMIT, dimension_semantics=("arbitrary",)
        ),
        cost_estimate=SMALL_COST,
    )(own, nffn, go, *weights, *(() if first else totals))
    if last:
        return outs[:4], outs[4:]
    return outs[:2], outs[2:]


def move_kernel(geometry, count, outward, own_ref, *refs):
    plan, segments, n_ctx = geometry
    sems = refs[-1]
    refs = refs[:-1]
    if outward:
        targets, parts = refs[: len(refs) - count], refs[len(refs) - count :]
    else:
        parts, targets = refs[:count], refs[count:]
    pairs = slot_pairs(own_ref[0], plan, parts, segments, n_ctx, targets)
    copy_all([(b, a) for a, b in pairs] if outward else pairs, sems)


def move(own, arrays, shapes, geometry, count, outward):
    plan, segments, _ = geometry
    any_spec = pl.BlockSpec(memory_space=pl.ANY)
    vmem_spec = pl.BlockSpec(memory_space=pltpu.VMEM)
    return pl.pallas_call(
        functools.partial(move_kernel, geometry, count, outward),
        out_shape=[jax.ShapeDtypeStruct(s, bf16) for s in shapes],
        in_specs=[pl.BlockSpec(memory_space=pltpu.SMEM)]
        + [vmem_spec if outward else any_spec] * len(arrays),
        out_specs=[any_spec if outward else vmem_spec] * len(shapes),
        scratch_shapes=[pltpu.SemaphoreType.DMA((len(plan) * len(segments),))],
        compiler_params=pltpu.CompilerParams(vmem_limit_bytes=VMEM_LIMIT),
        cost_estimate=SMALL_COST,
    )(own, *arrays)


def shifted_down(block, before):
    row = lax.broadcasted_iota(jnp.int32, block.shape, 0)
    one = jnp.where(row == 0, before[1:2], pltpu.roll(block, 1, 0))
    two = jnp.where(row == 0, before[0:1], pltpu.roll(block, 2, 0))
    return one, jnp.where(row == 1, before[1:2], two)


def shifted_up(block, behind):
    count = block.shape[0]
    row = lax.broadcasted_iota(jnp.int32, block.shape, 0)
    one = jnp.where(row == count - 1, behind[0:1], pltpu.roll(block, count - 1, 0))
    two = jnp.where(row == count - 2, behind[0:1], pltpu.roll(block, count - 2, 0))
    return one, jnp.where(row == count - 1, behind[1:2], two)


def in_kernel(x_ref, gain_ref, w_ref, normed_ref, projected_ref):
    x = x_ref[...].astype(f32)
    scale = lax.rsqrt(jnp.mean(x * x, axis=-1, keepdims=True) + EPSILON)
    normed = (x * scale * gain_ref[...]).astype(bf16)
    normed_ref[...] = normed
    projected_ref[...] = jnp.dot(normed, w_ref[...], preferred_element_type=f32)


def conv_kernel(projected_ref, before_ref, taps_ref, w_ref, mixer_ref, conv_ref, branch_ref):
    channels = conv_ref.shape[1]
    product = projected_ref[:, :channels] * projected_ref[:, 2 * channels :]
    one, two = shifted_down(product, before_ref[0].astype(f32))
    conv = taps_ref[0:1] * two + taps_ref[1:2] * one + taps_ref[2:3] * product
    conv_ref[...] = conv
    mixer = (projected_ref[:, channels : 2 * channels] * conv).astype(bf16)
    mixer_ref[...] = mixer
    branch_ref[...] = jnp.dot(mixer, w_ref[...], preferred_element_type=f32).astype(bf16)


def norm_kernel(x_ref, branch_ref, got_ref, gain_ref, residual_ref, normed_ref):
    residual = x_ref[...].astype(f32) + (branch_ref[...].astype(f32) + got_ref[...].astype(f32))
    residual_ref[...] = residual
    scale = lax.rsqrt(jnp.mean(residual * residual, axis=-1, keepdims=True) + EPSILON)
    normed_ref[...] = (residual * scale * gain_ref[...]).astype(bf16)


def branch_grad_kernel(
    own_first, gn_ref, got_ref, residual_ref, go_ref, gain_ref, mixer_ref, conv_ref, gate_c_ref,
    w_ref, grad_residual_ref, grad_conv_ref, grad_c_ref, grad_w_ref, grad_gain_ref, total_ref,
):
    step = pl.program_id(0)

    @pl.when(step == 0)
    def _():
        total_ref[...] = jnp.zeros_like(total_ref)
        grad_gain_ref[...] = jnp.zeros_like(grad_gain_ref)

    incoming = gn_ref[...] + got_ref[...].astype(f32)
    residual = residual_ref[...]
    scale = lax.rsqrt(jnp.mean(residual * residual, axis=-1, keepdims=True) + EPSILON)
    weighted = incoming * gain_ref[...]

    @pl.when(step >= own_first)
    def _():
        grad_gain_ref[...] += jnp.sum(incoming * residual * scale, axis=0, keepdims=True)

    inner = jnp.mean(weighted * residual, axis=-1, keepdims=True)
    grad_residual = go_ref[...].astype(f32) + (
        scale * weighted - residual * (scale * scale * scale) * inner
    )
    grad_residual_ref[...] = grad_residual
    grad_branch = grad_residual.astype(bf16)
    grad_mix = lax.dot_general(grad_branch, w_ref[...], NT, preferred_element_type=f32)
    grad_c_ref[...] = (grad_mix * conv_ref[...]).astype(bf16)
    grad_conv_ref[...] = grad_mix * gate_c_ref[...]
    total_ref[...] += lax.dot_general(mixer_ref[...], grad_branch, TN, preferred_element_type=f32)

    @pl.when(step == pl.num_programs(0) - 1)
    def _():
        grad_w_ref[...] = total_ref[...].astype(bf16)


def in_grad_kernel(
    geometry, count, own_ref, grad_conv_ref, behind_ref, before_ref, projected_ref, grad_c_ref,
    normed_ref, taps_ref, grad_projected_ref, grad_taps_ref, *refs
):
    parts, (total_ref, low_ref, sems) = refs[:count], refs[count:]
    plan, segments, n_ctx = geometry
    step = pl.program_id(0)

    @pl.when(step == 0)
    def _():
        total_ref[...] = jnp.zeros_like(total_ref)
        grad_taps_ref[...] = jnp.zeros_like(grad_taps_ref)

    channels = grad_c_ref.shape[1]
    grad_conv = grad_conv_ref[...]
    gate_b = projected_ref[:, :channels]
    values = projected_ref[:, 2 * channels :]
    product = gate_b * values
    one, two = shifted_down(product, before_ref[0].astype(f32))
    for k, shifted in enumerate((two, one, product)):
        grad_taps_ref[k : k + 1] += jnp.sum(grad_conv * shifted, axis=0, keepdims=True)
    one, two = shifted_up(grad_conv, behind_ref[0].astype(f32))
    grad_product = taps_ref[2:3] * grad_conv + taps_ref[1:2] * one + taps_ref[0:1] * two
    grad_projected_ref[:, :channels] = (grad_product * values).astype(bf16)
    grad_projected_ref[:, channels : 2 * channels] = grad_c_ref[...]
    grad_projected_ref[:, 2 * channels :] = (grad_product * gate_b).astype(bf16)
    total_ref[...] += lax.dot_general(
        normed_ref[...], grad_projected_ref[...], TN, preferred_element_type=f32
    )

    @pl.when(step == pl.num_programs(0) - 1)
    def _():
        low_ref[...] = total_ref[...].astype(bf16)
        pairs = slot_pairs(own_ref[0], plan, parts, segments, n_ctx, (low_ref,))
        copy_all([(b, a) for a, b in pairs], sems)


def row_call(body, steps, ins, outs, scratch=()):
    return pl.pallas_call(
        body,
        grid=(steps,),
        in_specs=[
            pl.BlockSpec(memory_space=pltpu.SMEM) if block is None else pl.BlockSpec(block, place)
            for _, block, place in ins
        ],
        out_specs=[
            pl.BlockSpec(memory_space=pl.ANY) if block is None else pl.BlockSpec(block, place)
            for _, _, block, place in outs
        ],
        out_shape=[jax.ShapeDtypeStruct(shape, dtype) for shape, dtype, _, _ in outs],
        scratch_shapes=list(scratch),
        compiler_params=pltpu.CompilerParams(
            vmem_limit_bytes=VMEM_LIMIT, dimension_semantics=("arbitrary",)
        ),
        cost_estimate=SMALL_COST,
    )(*[a for a, _, _ in ins])


def fits(tokens, w_in, w_out, w_gate, w_down, n_dp, n_ctx):
    width, hidden = w_gate.shape
    if n_dp % 2 or n_dp % (2 * n_ctx) or n_dp & (n_dp - 1) or n_ctx & (n_ctx - 1) or n_ctx < 2:
        return False
    depth = width // n_dp
    if width % n_dp or hidden % (n_dp * CHUNKS * 48) or w_in.shape[1] % (2 * n_ctx * 256):
        return False
    lanes = hidden // n_dp // CHUNKS * (n_dp // n_ctx // 2)
    wide = width // n_ctx
    return (
        lanes % 128 == 0
        and wide == lanes + 128
        and lanes == 384
        and wide % 256 == 0
        and depth % 16 == 0
        and 2 * depth <= 256
        and (w_in.shape[1] // n_ctx) % (2 * depth) == 0
        and width % (2 * depth) == 0
        and tokens.shape[1] % n_ctx == 0
        and n_ctx == 2
        and n_dp >= 16
    )


def fast_shards(tokens, w_in, w_out, w_gate, w_up, w_down, gain_mix, gain_ffn, kernel, cotangent):
    seqs, piece, width = tokens.shape
    rows = seqs * piece
    n_chip, n_ctx = lax.axis_size("chip"), lax.axis_size("ctx")
    slots = n_chip * n_ctx
    core = lax.axis_index("core")
    own_slot = lax.axis_index("chip") * n_ctx + lax.axis_index("ctx")
    own = own_slot.astype(jnp.int32)[None]
    depth = w_in.shape[0]
    groups = n_chip // n_ctx
    sub = w_down.shape[0] // CHUNKS
    lanes = groups * sub
    wide = w_out.shape[1]
    in_cols = w_in.shape[1] // 2
    in_parts, out_parts = in_cols // 256, wide // 256
    hidden_count = n_chip * sub
    channels = width // 2

    def mine_other(pair):
        return jnp.where(core == 0, pair[0], pair[1]), jnp.where(core == 0, pair[1], pair[0])

    def in_core_order(mine, other, axis):
        return jnp.where(
            core == 0,
            jnp.concatenate([mine, other], axis=axis),
            jnp.concatenate([other, mine], axis=axis),
        )

    small = jnp.concatenate([gain_mix[None], gain_ffn[None], kernel], axis=0)
    in_pair = w_in.reshape(depth, in_cols // depth, 2, depth).transpose(2, 0, 1, 3)
    in_pair = in_pair.reshape(2, depth, in_parts, 256).transpose(0, 2, 1, 3)
    in_mine, in_other = mine_other(in_pair)
    small_rows = jnp.pad(small, ((0, 11), (0, 256 - depth)))
    swapped = swap(jnp.concatenate([in_other.reshape(in_parts * depth, 256), small_rows], axis=0))
    in_got = swapped[: in_parts * depth].reshape(in_parts, depth, 256)
    in_block = in_core_order(in_mine, in_got, 1).reshape(in_parts * 2 * depth, 256)
    small_block = in_core_order(small, swapped[in_parts * depth :][:5, :depth], 1)
    small_block = jnp.pad(small_block, ((0, 11), (0, 256 - 2 * depth)))
    out_block = w_out.reshape(depth, out_parts, 256).transpose(1, 0, 2).reshape(-1, 256)
    mix_block = jnp.concatenate([in_block, small_block], axis=0)

    both = jnp.stack([w_gate, w_up]).reshape(2, depth, groups, 2, CHUNKS, sub)
    both = both.transpose(3, 4, 0, 1, 2, 5).reshape(2, CHUNKS, 2, depth, lanes)
    both_mine, both_other = mine_other(both)
    both_block = in_core_order(both_mine, swap(both_other), 2)
    both_block = both_block.reshape(CHUNKS, 4 * depth, lanes)
    down = w_down.reshape(CHUNKS, sub, wide)
    down_rest = down[:, :, lanes:].reshape(CHUNKS, 3, sub // 3, 128).transpose(0, 2, 1, 3)
    chunk_blocks = jnp.concatenate(
        [both_block, down[:, :, :lanes], down_rest.reshape(CHUNKS, sub // 3, lanes)], axis=1
    )

    mix_rows = mix_block.shape[0]
    mix_cut = in_parts * depth
    in_rows = in_parts * 2 * depth
    mix_segments = [
        (k * 2 * depth, 2 * depth, 0, 256, 0, 2 * depth, 0, in_cols, 256 * k)
        for k in range(in_parts)
    ]
    out_segments = [
        (k * depth, depth, 0, 256, 0, depth, 0, wide, 256 * k) for k in range(out_parts)
    ]
    small_segment = (in_rows, 16, 0, 256, 1, 16, 0, 256, 0)
    mix_plan = gather_plan(mix_cut, mix_rows)
    chunk_rows = chunk_blocks.shape[1]
    chunk_cut = chunk_rows // 2
    chunk_segments = [
        (0, 2 * depth, 0, lanes, 0, 2 * depth, 0, lanes, 0),
        (2 * depth, 2 * depth, 0, lanes, 1, 2 * depth, 0, lanes, 0),
        (4 * depth, sub, 0, lanes, 2, sub, 0, wide, 0),
    ] + [
        (4 * depth + sub, sub // 3, 128 * k, 128, 2, sub, k * (sub // 3), wide, lanes)
        for k in range(3)
    ]
    whole_plan = [(0, i, None, 0, chunk_rows) for i in range(slots)]
    whole_geometry = (whole_plan, chunk_segments, n_ctx)
    step_geometry = (gather_plan(chunk_cut, chunk_rows), chunk_segments, n_ctx)

    out_all = lax.all_gather(out_block, ("chip", "ctx"))

    token_rows = tokens.reshape(rows, width)
    inputs = jnp.concatenate([token_rows, swap(token_rows)], axis=0)
    go_rows = cotangent.reshape(rows, width)
    go = jnp.concatenate([go_rows, swap(go_rows)], axis=0)

    far, first_order, second_order = bit_masks()
    orders = (first_order, second_order)

    def doubled(hold, got):
        return jnp.concatenate([hold, got], axis=0)

    hold = mix_block[None]
    for mask in far:
        hold = doubled(hold, across(hold, mask))
    chunk_all = lax.all_gather(after(chunk_blocks[1], hold), ("chip", "ctx"))
    mix_halves = [hold[:, :mix_cut], hold[:, mix_cut:]]
    next_hold = after(chunk_blocks[0][None], hold)
    far_left = list(far)
    early = [inputs, go]
    for step in range(len(first_order)):
        got = [across(h, order[step]) for h, order in zip(mix_halves, orders)]
        if far_left:
            next_got = across(next_hold, far_left.pop(0))
            next_hold = doubled(next_hold, next_got)
        if early:
            got = [after(g, early[0]) for g in got]
            early = early[1:]
        if step + 1 < len(first_order):
            got = [after(g, next_got) for g in got]
            mix_halves = [doubled(h, g) for h, g in zip(mix_halves, got)]
            next_hold = after(next_hold, *got)
    mix_parts = [mix_halves[0], got[0], mix_halves[1], got[1]]
    for mask in far_left:
        next_got = across(next_hold, mask)
        next_hold = doubled(next_hold, next_got)
    in_half, small_all = move(
        own,
        mix_parts,
        [(width, n_ctx * in_cols), (n_chip * 16, n_ctx * 256)],
        (mix_plan, mix_segments + [small_segment], n_ctx),
        4,
        False,
    )
    in_half = after(in_half, next_got)
    next_halves = [next_hold[:, :chunk_cut], next_hold[:, chunk_cut:]]
    last_hold = after(chunk_blocks[2][None], next_got)

    def step_of(halves, step):
        return [across(h, order[step]) for h, order in zip(halves, orders)]

    def all_after(blocks, *done):
        return [after(block, *done) for block in blocks]

    small_all = small_all.reshape(n_chip, 16, n_ctx * 256)[:, :5, : 2 * depth].astype(f32)
    first_gain = small_all[:, 0].reshape(width)
    second_gain = small_all[:, 1].reshape(width)
    taps = small_all[:, 2:].reshape(n_chip, 3, 2, depth)
    taps = jnp.where(core == 0, taps[:, :, 0], taps[:, :, 1]).transpose(1, 0, 2)
    taps = taps.reshape(3, channels)

    blocks = 2 * seqs

    def at(i):
        return (i, 0)

    def still(i):
        return (0, 0)

    def other(i):
        return ((i + seqs) % blocks, 0)

    wide_rows, thin_rows = (piece, width), (piece, channels)
    taps = jnp.pad(taps, ((0, 5), (0, 0)))
    next_got = step_of(next_halves, 0)
    last_got = across(last_hold, far[0])
    normed_low, projected = row_call(
        in_kernel,
        blocks,
        [
            (inputs, wide_rows, at),
            (first_gain[None], (1, width), still),
            (in_half, in_half.shape, still),
        ],
        [
            ((2 * rows, width), bf16, wide_rows, at),
            ((2 * rows, 3 * channels), f32, (piece, 3 * channels), at),
        ],
    )
    (out_half,) = move(
        own,
        [after(out_all, projected)],
        [(channels, width)],
        ([(0, i, None, 0, out_parts * depth) for i in range(slots)], out_segments, n_ctx),
        1,
        False,
    )
    tail = projected.reshape(blocks, piece, 3 * channels)[:, piece - 2 :]
    tail = (tail[:, :, :channels] * tail[:, :, 2 * channels :]).astype(bf16)
    before = passed_along(tail, "ctx", 1)
    halo = (1, 2, channels)

    def halo_at(i):
        return (i, 0, 0)

    conv_taps = after(taps, last_got, *next_got)
    next_halves = [
        doubled(h, g) for h, g in zip(next_halves, all_after(next_got, projected))
    ]
    last_hold = doubled(last_hold, after(last_got, projected))
    next_got = step_of(next_halves, 1)
    last_got = across(last_hold, far[1])
    mixer_out, convolved, branch = row_call(
        conv_kernel,
        blocks,
        [
            (projected, (piece, 3 * channels), at),
            (before, halo, halo_at),
            (conv_taps, taps.shape, still),
            (out_half, out_half.shape, still),
        ],
        [
            ((2 * rows, channels), bf16, thin_rows, at),
            ((2 * rows, channels), f32, thin_rows, at),
            ((2 * rows, width), bf16, wide_rows, at),
        ],
    )
    residual, nffn_low = row_call(
        norm_kernel,
        blocks,
        [
            (inputs, wide_rows, at),
            (branch, wide_rows, at),
            (swap(branch), wide_rows, other),
            (second_gain[None], (1, width), still),
        ],
        [((2 * rows, width), f32, wide_rows, at), ((2 * rows, width), bf16, wide_rows, at)],
    )

    next_parts = [next_halves[0], next_got[0], next_halves[1], next_got[1]]
    next_parts = all_after(next_parts, nffn_low)
    last_hold = doubled(last_hold, after(last_got, nffn_low))
    last_halves = [last_hold[:, :chunk_cut], last_hold[:, chunk_cut:]]
    last_got_halves = step_of(last_halves, 0)

    totals, first_grads = ffn_chunk(
        own, nffn_low, after(go, last_got), next_parts, None, step_geometry, step_geometry,
        hidden_count,
    )
    first_stages = Stages(first_grads)
    nffn_then = after(nffn_low, *last_got_halves)
    last_halves = [
        doubled(h, g) for h, g in zip(last_halves, all_after(last_got_halves, totals[1]))
    ]
    last_got_halves = step_of(last_halves, 1)
    totals, second_grads = ffn_chunk(
        own, nffn_then, go, [chunk_all], totals, whole_geometry, step_geometry, hidden_count
    )
    second_stages = Stages(second_grads)
    nffn_then = after(nffn_low, *first_stages.got)
    first_stages.advance(totals[1])
    last_got_halves = all_after(last_got_halves, totals[1])
    last_parts = [last_halves[0], last_got_halves[0], last_halves[1], last_got_halves[1]]
    totals, last_grads = ffn_chunk(
        own, nffn_then, go, last_parts, totals, step_geometry, step_geometry, hidden_count, last=True
    )
    ffn_out, grad_nffn, ffn_low, grad_low = totals
    last_stages = Stages(last_grads)
    grad_got = swap(after(grad_low, *first_stages.got, *second_stages.got))
    first_stages.advance(grad_low)
    second_stages.advance(grad_low)

    def turned(i):
        return ((i + seqs) % blocks, 0)

    def turned_back(i):
        return (i, 0)

    def own_place(i):
        return (jnp.maximum(i - seqs, 0), 0)

    def gate_c_place(i):
        return ((i + seqs) % blocks, 1)

    grad_residual, grad_conv, grad_c, grad_w_out, grad_gain_ffn = row_call(
        functools.partial(branch_grad_kernel, seqs),
        blocks,
        [
            (grad_nffn, wide_rows, turned),
            (grad_got, wide_rows, turned_back),
            (residual, wide_rows, turned),
            (go, wide_rows, turned),
            (second_gain[None], (1, width), still),
            (mixer_out, thin_rows, turned),
            (convolved, thin_rows, turned),
            (projected, thin_rows, gate_c_place),
            (out_half, out_half.shape, still),
        ],
        [
            ((rows, width), f32, wide_rows, own_place),
            ((2 * rows, channels), f32, thin_rows, turned),
            ((2 * rows, channels), bf16, thin_rows, turned),
            ((channels, width), bf16, (channels, width), still),
            ((1, width), f32, (1, width), still),
        ],
        scratch=[pltpu.VMEM((channels, width), f32)],
    )
    grad_gain_ffn = grad_gain_ffn[0]
    stages = (first_stages, second_stages, last_stages)
    grad_c_then = after(grad_c, *(g for s in stages for g in s.got))
    for s in stages:
        s.advance(grad_c)
    head = grad_conv.reshape(blocks, piece, channels)[:, :2].astype(bf16)
    behind = passed_along(head, "ctx", -1)
    grad_out_slots = grad_w_out.reshape(n_chip, depth, n_ctx, out_parts, 256)
    grad_out_slots = grad_out_slots.transpose(0, 2, 3, 1, 4).reshape(slots, out_parts * depth, 256)
    out_sum = lax.psum_scatter(grad_out_slots, ("chip", "ctx"), scatter_dimension=0).astype(f32)
    sum_plan = gather_plan(mix_cut, in_rows)
    grad_projected, grad_kernel, *mix_grad_parts = row_call(
        functools.partial(in_grad_kernel, (sum_plan, mix_segments, n_ctx), 4),
        blocks,
        [
            (own, None, None),
            (grad_conv, thin_rows, at),
            (behind, halo, halo_at),
            (before, halo, halo_at),
            (projected, (piece, 3 * channels), at),
            (grad_c_then, thin_rows, at),
            (normed_low, wide_rows, at),
            (taps, taps.shape, still),
        ],
        [
            ((2 * rows, 3 * channels), bf16, (piece, 3 * channels), at),
            ((8, channels), f32, (8, channels), still),
        ]
        + [(shape, bf16, None, None) for shape in part_shapes(sum_plan, 256)],
        scratch=[
            pltpu.VMEM((width, 3 * channels), f32),
            pltpu.VMEM((width, 3 * channels), bf16),
            pltpu.SemaphoreType.DMA((len(sum_plan) * len(mix_segments),)),
        ],
    )
    grad_kernel = grad_kernel[:3]
    mix_stages = Stages(mix_grad_parts)
    for s in stages:
        s.advance(grad_projected)
    grad_other = cross_cols(grad_projected[rows:], in_half).astype(bf16)
    for s in (mix_stages, *stages):
        s.advance(grad_other)
    other_got = swap(grad_other)
    grad_mine = cross_cols(after(grad_projected[:rows], other_got), in_half)
    for s in (mix_stages, second_stages, last_stages):
        s.advance(grad_mine)
    grad_normed = grad_mine + other_got.astype(f32)
    ffn_got = swap(after(ffn_low[rows:], grad_other))
    result = residual[:rows] + (after(ffn_out[:rows], grad_mine) + ffn_got.astype(f32))
    result = result.astype(bf16).reshape(seqs, piece, width)
    own_inputs = token_rows.astype(f32)
    scale_mix = lax.rsqrt(jnp.mean(own_inputs * own_inputs, axis=-1, keepdims=True) + EPSILON)
    grad_in_norm, grad_gain_mix = norm_backward(own_inputs, scale_mix, first_gain, grad_normed)
    grad_tokens = (grad_residual + grad_in_norm).reshape(seqs, piece, width)

    mix_stages.advance(grad_tokens)
    last_stages.advance(grad_tokens)
    while mix_stages.total is None:
        mix_stages.advance()

    chunk_sum = jnp.stack([s.total for s in stages])
    both_sum = chunk_sum[:, : 4 * depth].reshape(CHUNKS, 2, 2, depth, lanes).transpose(2, 0, 1, 3, 4)
    both_mine, both_other = mine_other(both_sum)
    both_got = swap(both_other)
    both_sum = in_core_order(both_mine[None], both_got[None], 0)
    both_sum = both_sum.reshape(2, CHUNKS, 2, depth, groups, sub).transpose(2, 3, 4, 0, 1, 5)
    both_sum = both_sum.reshape(2, depth, 2 * CHUNKS * lanes)
    down_rest = chunk_sum[:, 4 * depth + sub :].reshape(CHUNKS, sub // 3, 3, 128)
    down_rest = down_rest.transpose(0, 2, 1, 3).reshape(CHUNKS, sub, 128)
    final_down = jnp.concatenate([chunk_sum[:, 4 * depth : 4 * depth + sub], down_rest], axis=2)
    final_down = final_down.reshape(CHUNKS * sub, wide)

    in_sum = mix_stages.total.reshape(in_parts, 2, depth, 256).transpose(1, 0, 2, 3)
    in_mine, in_other = mine_other(in_sum)
    in_sum = in_core_order(in_mine[None], swap(in_other)[None], 0)
    in_sum = in_sum.transpose(0, 2, 1, 3).reshape(2, depth, in_cols // depth, depth)
    final_in = in_sum.transpose(1, 2, 0, 3).reshape(depth, 2 * in_cols)
    final_out = out_sum.reshape(out_parts, depth, 256).transpose(1, 0, 2)
    final_out = final_out.reshape(depth, wide)

    grad_taps = grad_kernel.reshape(3, n_chip, 1, depth)
    grad_taps = jnp.where(
        jnp.arange(2).reshape(1, 1, 2, 1) == core, grad_taps, jnp.zeros_like(grad_taps)
    ).reshape(3, width)
    small_grad = jnp.concatenate([grad_gain_mix[None], grad_gain_ffn[None], grad_taps], axis=0)
    small_sum = small_grad.reshape(5, n_chip, 2 * depth).transpose(1, 0, 2)
    for bit in range(n_ctx.bit_length() - 1):
        small_sum = small_sum + across(small_sum, 1 << bit)
    for bit in range(n_chip.bit_length() - 1):
        mask = n_chip >> (bit + 1)
        low, high = small_sum[: small_sum.shape[0] // 2], small_sum[small_sum.shape[0] // 2 :]
        upper = jnp.bitwise_and(lax.axis_index("chip"), mask) != 0
        small_sum = jnp.where(upper, high, low) + across(jnp.where(upper, low, high), mask * n_ctx)
    small_mine, small_other = mine_other(small_sum[0].reshape(5, 2, depth).transpose(1, 0, 2))
    small_sum = small_mine + swap(small_other)
    return (
        result,
        grad_tokens,
        final_in,
        final_out,
        both_sum[0],
        both_sum[1],
        final_down,
        small_sum[0],
        small_sum[1],
        small_sum[2:5],
    )


def solution(mesh):
    n_dp, n_ctx = mesh.shape["dp"], mesh.shape["ctx"]

    def placed(dp):
        whole, cut = P(dp, "ctx", None), P(dp, "ctx")
        ins = (whole, cut, cut, cut, cut, cut, P(dp), P(dp), P(None, dp), whole)
        outs = (whole, whole, cut, cut, cut, cut, cut, P(dp), P(dp), P(None, dp))
        return ins, outs

    def run(tokens, w_in, w_out, w_gate, w_up, w_down, gain_mix, gain_ffn, kernel, cotangent):
        if fits(tokens, w_in, w_out, w_gate, w_down, n_dp, n_ctx):
            cut_mesh = Mesh(mesh.devices.reshape(n_dp // 2, 2, n_ctx), ("chip", "core", "ctx"))
            body, on, (ins, outs) = fast_shards, cut_mesh, placed(("chip", "core"))
        else:
            body, on, (ins, outs) = plain_shards, mesh, placed("dp")
        call = jax.shard_map(body, mesh=on, in_specs=ins, out_specs=outs, check_vma=False)
        return call(
            tokens, w_in, w_out, w_gate, w_up, w_down, gain_mix, gain_ffn, kernel, cotangent
        )

    return run
```

```python
import functools
import jax
import jax.numpy as jnp
from jax import lax
from jax.experimental import pallas as pl
from jax.experimental.pallas import tpu as pltpu
from jax.sharding import Mesh
from jax.sharding import PartitionSpec as P

EPSILON = 1e-05
CHUNKS = 3
f32 = jnp.float32
bf16 = jnp.bfloat16


def passed_along(block, axis, distance):
    devices = range(lax.axis_size(axis))
    route = [(i - distance, i) for i in devices if i - distance in devices]
    return lax.ppermute(block, axis, route)


def cross_rows(left_operand, right_operand):
    return lax.dot_general(
        left_operand, right_operand, (((0,), (0,)), ((), ())), preferred_element_type=jnp.float32
    )


def cross_cols(left_operand, right_operand):
    return lax.dot_general(
        left_operand, right_operand, (((1,), (1,)), ((), ())), preferred_element_type=jnp.float32
    )


def norm_forward(values, gain):
    scale = lax.rsqrt(jnp.mean(values * values, axis=-1, keepdims=True) + EPSILON)
    return (values * scale * gain, scale)


def norm_backward(values, scale, gain, incoming):
    weighted = incoming * gain
    gain_grad = jnp.sum(incoming * values * scale, axis=0)
    inner = jnp.mean(weighted * values, axis=-1, keepdims=True)
    return (scale * weighted - values * (scale * scale * scale) * inner, gain_grad)


def plain_shards(tokens, w_in, w_out, w_gate, w_up, w_down, gain_mix, gain_ffn, kernel, cotangent):
    seq_count, piece_len, model_width = tokens.shape
    row_count = seq_count * piece_len
    small_params = jnp.concatenate([gain_mix[None], gain_ffn[None], kernel], axis=0)
    input_columns, out_cols, gate_cols, up_cols, down_cols = (
        lax.all_gather(w_in, "ctx", axis=1, tiled=True),
        lax.all_gather(w_out, "ctx", axis=1, tiled=True),
        lax.all_gather(w_gate, "ctx", axis=1, tiled=True),
        lax.all_gather(w_up, "ctx", axis=1, tiled=True),
        lax.all_gather(w_down, "ctx", axis=1, tiled=True),
    )
    full_in, full_out, full_gate, full_up, full_down, small_full = (
        lax.all_gather(input_columns, "dp", axis=0, tiled=True),
        lax.all_gather(out_cols, "dp", axis=0, tiled=True),
        lax.all_gather(gate_cols, "dp", axis=0, tiled=True),
        lax.all_gather(up_cols, "dp", axis=0, tiled=True),
        lax.all_gather(down_cols, "dp", axis=0, tiled=True),
        lax.all_gather(small_params, "dp", axis=1, tiled=True),
    )
    small_float = small_full.astype(jnp.float32)
    first_gain = small_float[0]
    second_gain = small_float[1]
    taps = small_float[2:5]
    inputs = tokens.reshape(row_count, model_width).astype(jnp.float32)
    normed, scale_mix = norm_forward(inputs, first_gain)
    normed_low = normed.astype(jnp.bfloat16)
    projected = jnp.dot(normed_low, full_in, preferred_element_type=jnp.float32)
    gate_b = projected[:, :model_width]
    gate_c = projected[:, model_width : 2 * model_width]
    values = projected[:, 2 * model_width :]
    product = (gate_b * values).reshape(seq_count, piece_len, model_width)
    previous = passed_along(product[:, piece_len - 2 :].astype(jnp.bfloat16), "ctx", 1).astype(
        jnp.float32
    )
    padded = jnp.concatenate([previous, product], axis=1)
    convolved = taps[0] * padded[:, :-2] + taps[1] * padded[:, 1:-1] + taps[2] * padded[:, 2:]
    convolved = convolved.reshape(row_count, model_width)
    mixer_out = (gate_c * convolved).astype(jnp.bfloat16)
    residual = inputs + jnp.dot(mixer_out, full_out, preferred_element_type=jnp.float32)
    feedforward_normed, scale_ffn = norm_forward(residual, second_gain)
    nffn_low = feedforward_normed.astype(jnp.bfloat16)
    gate = jnp.dot(nffn_low, full_gate, preferred_element_type=jnp.float32)
    up_value = jnp.dot(nffn_low, full_up, preferred_element_type=jnp.float32)
    sigmoid_gate = jax.nn.sigmoid(gate)
    activated = gate * sigmoid_gate
    hidden = (activated * up_value).astype(jnp.bfloat16)
    result = residual + jnp.dot(hidden, full_down, preferred_element_type=jnp.float32)
    result = result.astype(jnp.bfloat16).reshape(seq_count, piece_len, model_width)
    back_in, output_backward, back_gate, back_up, back_down = (
        lax.all_gather(w_in, "ctx", axis=1, tiled=True),
        lax.all_gather(w_out, "ctx", axis=1, tiled=True),
        lax.all_gather(w_gate, "ctx", axis=1, tiled=True),
        lax.all_gather(w_up, "ctx", axis=1, tiled=True),
        lax.all_gather(w_down, "ctx", axis=1, tiled=True),
    )
    input_weight_used, use_out, use_gate, use_up, use_down = (
        lax.all_gather(back_in, "dp", axis=0, tiled=True),
        lax.all_gather(output_backward, "dp", axis=0, tiled=True),
        lax.all_gather(back_gate, "dp", axis=0, tiled=True),
        lax.all_gather(back_up, "dp", axis=0, tiled=True),
        lax.all_gather(back_down, "dp", axis=0, tiled=True),
    )
    grad_out = cotangent.reshape(row_count, model_width)
    grad_out_float = grad_out.astype(jnp.float32)
    grad_w_down = cross_rows(hidden, grad_out)
    grad_hidden = cross_cols(grad_out, use_down)
    grad_gate = (
        grad_hidden * up_value * sigmoid_gate * (1.0 + gate * (1.0 - sigmoid_gate))
    ).astype(jnp.bfloat16)
    grad_up = (grad_hidden * activated).astype(jnp.bfloat16)
    grad_w_gate = cross_rows(nffn_low, grad_gate)
    grad_w_up = cross_rows(nffn_low, grad_up)
    grad_nffn = cross_cols(grad_gate, use_gate) + cross_cols(grad_up, use_up)
    residual_norm_gradient, grad_gain_ffn = norm_backward(
        residual, scale_ffn, second_gain, grad_nffn
    )
    grad_residual = grad_out_float + residual_norm_gradient
    grad_branch = grad_residual.astype(jnp.bfloat16)
    grad_w_out = cross_rows(mixer_out, grad_branch)
    grad_mix = cross_cols(grad_branch, use_out)
    grad_c = grad_mix * convolved
    grad_conv = (grad_mix * gate_c).reshape(seq_count, piece_len, model_width)
    following = passed_along(grad_conv[:, :2].astype(jnp.bfloat16), "ctx", -1).astype(jnp.float32)
    extended = jnp.concatenate([grad_conv, following], axis=1)
    grad_product = (
        taps[2] * extended[:, :-2] + taps[1] * extended[:, 1:-1] + taps[0] * extended[:, 2:]
    )
    grad_kernel = jnp.stack(
        [
            jnp.sum(grad_conv * padded[:, shift_at : shift_at + piece_len], axis=(0, 1))
            for shift_at in range(3)
        ],
        axis=0,
    )
    grad_product = grad_product.reshape(row_count, model_width)
    grad_projected = jnp.concatenate(
        [grad_product * values, grad_c, grad_product * gate_b], axis=1
    ).astype(jnp.bfloat16)
    grad_w_in = cross_rows(normed_low, grad_projected)
    grad_normed = cross_cols(grad_projected, input_weight_used)
    grad_in_norm, grad_gain_mix = norm_backward(inputs, scale_mix, first_gain, grad_normed)
    grad_tokens = (grad_residual + grad_in_norm).reshape(seq_count, piece_len, model_width)
    small_grad = jnp.concatenate([grad_gain_mix[None], grad_gain_ffn[None], grad_kernel], axis=0)
    part_in, part_out, part_gate, part_up, part_down, small_part = (
        lax.psum_scatter(grad_w_in, "dp", scatter_dimension=0, tiled=True),
        lax.psum_scatter(grad_w_out, "dp", scatter_dimension=0, tiled=True),
        lax.psum_scatter(grad_w_gate, "dp", scatter_dimension=0, tiled=True),
        lax.psum_scatter(grad_w_up, "dp", scatter_dimension=0, tiled=True),
        lax.psum_scatter(grad_w_down, "dp", scatter_dimension=0, tiled=True),
        lax.psum_scatter(small_grad, "dp", scatter_dimension=1, tiled=True),
    )
    final_in, final_out, final_gate, final_up, final_down = (
        lax.psum_scatter(part_in, "ctx", scatter_dimension=1, tiled=True),
        lax.psum_scatter(part_out, "ctx", scatter_dimension=1, tiled=True),
        lax.psum_scatter(part_gate, "ctx", scatter_dimension=1, tiled=True),
        lax.psum_scatter(part_up, "ctx", scatter_dimension=1, tiled=True),
        lax.psum_scatter(part_down, "ctx", scatter_dimension=1, tiled=True),
    )
    small_total = lax.psum(small_part, "ctx")
    return (
        result,
        grad_tokens,
        final_in,
        final_out,
        final_gate,
        final_up,
        final_down,
        small_total[0],
        small_total[1],
        small_total[2:5],
    )


SMALL_COST = pl.CostEstimate(flops=1 << 16, bytes_accessed=1 << 16, transcendentals=0)
VMEM_LIMIT = 60 * 1024 * 1024
NT = (((1,), (1,)), ((), ()))
TN = (((0,), (0,)), ((), ()))


def swap(block):
    return lax.ppermute(block, "core", [(0, 1), (1, 0)])


def across(block, mask):
    count = lax.axis_size("chip") * lax.axis_size("ctx")
    return lax.ppermute(block, ("chip", "ctx"), [(i, i ^ mask) for i in range(count)])


def bit_masks():
    n_chip, n_ctx = lax.axis_size("chip"), lax.axis_size("ctx")
    ctx_bits = [1 << b for b in range(n_ctx.bit_length() - 1)]
    near = [n_ctx]
    far = [n_ctx << b for b in range(1, n_chip.bit_length() - 1)]
    return far, near + ctx_bits, ctx_bits + near


def after(value, *done):
    return lax.optimization_barrier((value, *done))[0]


def gather_plan(cut, total):
    far, first_order, second_order = bit_masks()
    plan = []
    for operand, order, row0, rows in ((0, first_order, 0, cut), (2, second_order, cut, total - cut)):
        masks = [0]
        for mask in far + order[:-1]:
            masks = masks + [m ^ mask for m in masks]
        for index, mask in enumerate(masks):
            plan.append((operand, index, mask, row0, rows))
            plan.append((operand + 1, index, mask ^ order[-1], row0, rows))
    return plan


def gather(block, cut):
    far, first_order, second_order = bit_masks()
    hold = block[None]
    for mask in far:
        hold = jnp.concatenate([hold, across(hold, mask)], axis=0)
    parts = []
    for order, half in ((first_order, hold[:, :cut]), (second_order, hold[:, cut:])):
        for mask in order[:-1]:
            half = jnp.concatenate([half, across(half, mask)], axis=0)
        parts += [half, across(half, order[-1])]
    return parts


def scatter_steps(parts):
    far, first_order, second_order = bit_masks()

    def send(block, mask):
        return across(block.astype(bf16), mask)

    orders = (first_order, second_order)
    got = yield [send(parts[1], first_order[-1]), send(parts[3], second_order[-1])]
    keeps = [k.astype(f32) + g.astype(f32) for k, g in zip((parts[0], parts[2]), got)]
    for step in range(len(first_order) - 2, -1, -1):
        mid = keeps[0].shape[0] // 2
        got = yield [send(k[mid:], order[step]) for k, order in zip(keeps, orders)]
        keeps = [k[:mid] + g.astype(f32) for k, g in zip(keeps, got)]
    keep = jnp.concatenate(keeps, axis=1)
    for mask in reversed(far):
        mid = keep.shape[0] // 2
        (got,) = yield [send(keep[mid:], mask)]
        keep = keep[:mid] + got.astype(f32)
    return keep[0]


class Stages:
    def __init__(self, parts):
        self.steps = scatter_steps(parts)
        self.got = next(self.steps)
        self.total = None

    def advance(self, *done):
        if self.total is not None:
            return
        try:
            self.got = self.steps.send([after(g, *done) for g in self.got])
        except StopIteration as end:
            self.got, self.total = [], end.value


def slot_pairs(own, plan, refs, segments, n_ctx, targets):
    pairs = []
    for operand, index, mask, row0, nrows in plan:
        slot = index if mask is None else jnp.bitwise_xor(own, mask)
        y = lax.rem(slot, n_ctx)
        chip = lax.div(slot, n_ctx)
        src = refs[operand].at[index]
        for seg_row, seg_rows, lane0, lanes, target, row_step, row_add, lane_step, lane_add in segments:
            low, high = max(seg_row, row0), min(seg_row + seg_rows, row0 + nrows)
            if low >= high:
                continue
            row = pl.multiple_of(chip * row_step + row_add + (low - seg_row), 16)
            lane = pl.multiple_of(y * lane_step + lane_add, 128)
            pairs.append(
                (
                    src.at[pl.ds(low - row0, high - low), pl.ds(lane0, lanes)],
                    targets[target].at[pl.ds(row, high - low), pl.ds(lane, lanes)],
                )
            )
    return pairs


def copy_all(pairs, sems):
    copies = [pltpu.make_async_copy(a, b, sems.at[i]) for i, (a, b) in enumerate(pairs)]
    for copy in copies:
        copy.start()
    for copy in copies:
        copy.wait()


def part_count(plan):
    return 1 + max(entry[0] for entry in plan)


def part_shapes(plan, lanes):
    shapes = {}
    for operand, index, _, _, rows in plan:
        shapes[operand] = (max(index + 1, shapes.get(operand, (0,))[0]), rows, lanes)
    return [shapes[operand] for operand in sorted(shapes)]


def ffn_kernel(geometry, out_geometry, first, own_ref, n_ref, go_ref, *refs):
    plan, segments, n_ctx = geometry
    out_plan = out_geometry[0]
    count, out_count = part_count(plan), part_count(out_plan)
    weights, refs = refs[:count], refs[count:]
    if not first:
        res_in, gn_in = refs[:2]
        refs = refs[2:]
    res_ref, gn_ref = refs[:2]
    refs = refs[2:]
    grads, refs = refs[:out_count], refs[out_count:]
    gate_m, up_m, down_m, d_gate, d_up, d_down, h_m, gg_m, gu_m, sems = refs
    own = own_ref[0]
    targets = (gate_m, up_m, down_m)

    @pl.when(pl.program_id(0) == 0)
    def _():
        d_gate[...] = jnp.zeros_like(d_gate)
        d_up[...] = jnp.zeros_like(d_up)
        d_down[...] = jnp.zeros_like(d_down)
        copy_all(slot_pairs(own, plan, weights, segments, n_ctx, targets), sems)

    n = n_ref[...]
    go = go_ref[...]
    hidden_count = gate_m.shape[1]
    step = 256
    for start in range(0, hidden_count, step):
        cols = slice(start, start + step)
        g = jnp.dot(n, gate_m[:, cols], preferred_element_type=f32)
        u = jnp.dot(n, up_m[:, cols], preferred_element_type=f32)
        gh = lax.dot_general(go, down_m[cols, :], NT, preferred_element_type=f32)
        s = jax.nn.sigmoid(g)
        act = g * s
        h_m[:, cols] = (act * u).astype(bf16)
        gg_m[:, cols] = (gh * u * s * (1.0 + g * (1.0 - s))).astype(bf16)
        gu_m[:, cols] = (gh * act).astype(bf16)
    res = jnp.dot(h_m[...], down_m[...], preferred_element_type=f32)
    gn = lax.dot_general(gg_m[...], gate_m[...], NT, preferred_element_type=f32)
    gn = gn + lax.dot_general(gu_m[...], up_m[...], NT, preferred_element_type=f32)
    if not first:
        res = res_in[...] + res
        gn = gn_in[...] + gn
    res_ref[...] = res
    gn_ref[...] = gn.astype(gn_ref.dtype)
    d_gate[...] += lax.dot_general(n, gg_m[...], TN, preferred_element_type=f32)
    d_up[...] += lax.dot_general(n, gu_m[...], TN, preferred_element_type=f32)
    d_down[...] += lax.dot_general(h_m[...], go, TN, preferred_element_type=f32)

    @pl.when(pl.program_id(0) == pl.num_programs(0) - 1)
    def _():
        gate_m[...] = d_gate[...].astype(bf16)
        up_m[...] = d_up[...].astype(bf16)
        down_m[...] = d_down[...].astype(bf16)
        pairs = slot_pairs(own, out_plan, grads, segments, n_ctx, targets)
        copy_all([(b, a) for a, b in pairs], sems)


def ffn_chunk(
    own, nffn, go, weights, totals, geometry, out_geometry, hidden_count, last=False, rows=256
):
    total, width = nffn.shape
    first = totals is None
    plan, segments, _ = geometry
    out_plan = out_geometry[0]
    count, out_count = part_count(plan), part_count(out_plan)
    lanes = weights[0].shape[-1]
    row_spec = pl.BlockSpec((rows, width), lambda i, o: (i, 0))
    any_spec = pl.BlockSpec(memory_space=pl.ANY)
    outs = pl.pallas_call(
        functools.partial(ffn_kernel, geometry, out_geometry, first),
        out_shape=[jax.ShapeDtypeStruct((total, width), d) for d in (f32, bf16 if last else f32)]
        + [jax.ShapeDtypeStruct(s, bf16) for s in part_shapes(out_plan, lanes)],
        grid_spec=pltpu.PrefetchScalarGridSpec(
            num_scalar_prefetch=1,
            grid=(total // rows,),
            in_specs=[row_spec] * 2 + [any_spec] * count + [row_spec] * (0 if first else 2),
            out_specs=[row_spec] * 2 + [any_spec] * out_count,
            scratch_shapes=[
                pltpu.VMEM((width, hidden_count), bf16),
                pltpu.VMEM((width, hidden_count), bf16),
                pltpu.VMEM((hidden_count, width), bf16),
                pltpu.VMEM((width, hidden_count), f32),
                pltpu.VMEM((width, hidden_count), f32),
                pltpu.VMEM((hidden_count, width), f32),
                pltpu.VMEM((rows, hidden_count), bf16),
                pltpu.VMEM((rows, hidden_count), bf16),
                pltpu.VMEM((rows, hidden_count), bf16),
                pltpu.SemaphoreType.DMA((max(len(plan), len(out_plan)) * len(segments),)),
            ],
        ),
        input_output_aliases={} if first else {3 + count: 0} if last else {3 + count: 0, 4 + count: 1},
        compiler_params=pltpu.CompilerParams(
            vmem_limit_bytes=VMEM_LIMIT, dimension_semantics=("arbitrary",)
        ),
        cost_estimate=SMALL_COST,
    )(own, nffn, go, *weights, *(() if first else totals))
    return outs[:2], outs[2:]


def move_kernel(geometry, count, outward, own_ref, *refs):
    plan, segments, n_ctx = geometry
    sems = refs[-1]
    refs = refs[:-1]
    if outward:
        targets, parts = refs[: len(refs) - count], refs[len(refs) - count :]
    else:
        parts, targets = refs[:count], refs[count:]
    pairs = slot_pairs(own_ref[0], plan, parts, segments, n_ctx, targets)
    copy_all([(b, a) for a, b in pairs] if outward else pairs, sems)


def move(own, arrays, shapes, geometry, count, outward):
    plan, segments, _ = geometry
    any_spec = pl.BlockSpec(memory_space=pl.ANY)
    vmem_spec = pl.BlockSpec(memory_space=pltpu.VMEM)
    return pl.pallas_call(
        functools.partial(move_kernel, geometry, count, outward),
        out_shape=[jax.ShapeDtypeStruct(s, bf16) for s in shapes],
        in_specs=[pl.BlockSpec(memory_space=pltpu.SMEM)]
        + [vmem_spec if outward else any_spec] * len(arrays),
        out_specs=[any_spec if outward else vmem_spec] * len(shapes),
        scratch_shapes=[pltpu.SemaphoreType.DMA((len(plan) * len(segments),))],
        compiler_params=pltpu.CompilerParams(vmem_limit_bytes=VMEM_LIMIT),
        cost_estimate=SMALL_COST,
    )(own, *arrays)


def shifted_down(block, before):
    row = lax.broadcasted_iota(jnp.int32, block.shape, 0)
    one = jnp.where(row == 0, before[1:2], pltpu.roll(block, 1, 0))
    two = jnp.where(row == 0, before[0:1], pltpu.roll(block, 2, 0))
    return one, jnp.where(row == 1, before[1:2], two)


def shifted_up(block, behind):
    count = block.shape[0]
    row = lax.broadcasted_iota(jnp.int32, block.shape, 0)
    one = jnp.where(row == count - 1, behind[0:1], pltpu.roll(block, count - 1, 0))
    two = jnp.where(row == count - 2, behind[0:1], pltpu.roll(block, count - 2, 0))
    return one, jnp.where(row == count - 1, behind[1:2], two)


def in_kernel(x_ref, gain_ref, w_ref, normed_ref, projected_ref):
    x = x_ref[...].astype(f32)
    scale = lax.rsqrt(jnp.mean(x * x, axis=-1, keepdims=True) + EPSILON)
    normed = (x * scale * gain_ref[...]).astype(bf16)
    normed_ref[...] = normed
    projected_ref[...] = jnp.dot(normed, w_ref[...], preferred_element_type=f32)


def conv_kernel(projected_ref, before_ref, taps_ref, w_ref, mixer_ref, conv_ref, branch_ref):
    channels = conv_ref.shape[1]
    product = projected_ref[:, :channels] * projected_ref[:, 2 * channels :]
    one, two = shifted_down(product, before_ref[0].astype(f32))
    conv = taps_ref[0:1] * two + taps_ref[1:2] * one + taps_ref[2:3] * product
    conv_ref[...] = conv
    mixer = (projected_ref[:, channels : 2 * channels] * conv).astype(bf16)
    mixer_ref[...] = mixer
    branch_ref[...] = jnp.dot(mixer, w_ref[...], preferred_element_type=f32).astype(bf16)


def norm_kernel(x_ref, branch_ref, got_ref, gain_ref, residual_ref, normed_ref):
    residual = x_ref[...].astype(f32) + (branch_ref[...].astype(f32) + got_ref[...].astype(f32))
    residual_ref[...] = residual
    scale = lax.rsqrt(jnp.mean(residual * residual, axis=-1, keepdims=True) + EPSILON)
    normed_ref[...] = (residual * scale * gain_ref[...]).astype(bf16)


def branch_grad_kernel(
    own_first, geometry, own_ref, gn_ref, got_ref, residual_ref, go_ref, gain_ref, mixer_ref,
    conv_ref, gate_c_ref, w_ref, grad_residual_ref, grad_conv_ref, grad_c_ref, grad_gain_ref,
    part_ref, total_ref, low_ref, sems,
):
    plan, segments, n_ctx = geometry
    step = pl.program_id(0)

    @pl.when(step == 0)
    def _():
        total_ref[...] = jnp.zeros_like(total_ref)
        grad_gain_ref[...] = jnp.zeros_like(grad_gain_ref)

    incoming = gn_ref[...].astype(f32) + got_ref[...].astype(f32)
    residual = residual_ref[...]
    scale = lax.rsqrt(jnp.mean(residual * residual, axis=-1, keepdims=True) + EPSILON)
    weighted = incoming * gain_ref[...]

    @pl.when(step >= own_first)
    def _():
        grad_gain_ref[...] += jnp.sum(incoming * residual * scale, axis=0, keepdims=True)

    inner = jnp.mean(weighted * residual, axis=-1, keepdims=True)
    grad_residual = go_ref[...].astype(f32) + (
        scale * weighted - residual * (scale * scale * scale) * inner
    )
    grad_residual_ref[...] = grad_residual
    grad_branch = grad_residual.astype(bf16)
    grad_mix = lax.dot_general(grad_branch, w_ref[...], NT, preferred_element_type=f32)
    grad_c_ref[...] = (grad_mix * conv_ref[...]).astype(bf16)
    grad_conv_ref[...] = grad_mix * gate_c_ref[...]
    total_ref[...] += lax.dot_general(mixer_ref[...], grad_branch, TN, preferred_element_type=f32)

    @pl.when(step == pl.num_programs(0) - 1)
    def _():
        low_ref[...] = total_ref[...].astype(bf16)
        pairs = slot_pairs(own_ref[0], plan, (part_ref,), segments, n_ctx, (low_ref,))
        copy_all([(b, a) for a, b in pairs], sems)


def in_grad_kernel(
    geometry, count, own_ref, grad_conv_ref, behind_ref, before_ref, projected_ref, grad_c_ref,
    normed_ref, taps_ref, grad_projected_ref, grad_taps_ref, *refs
):
    parts, (total_ref, low_ref, sems) = refs[:count], refs[count:]
    plan, segments, n_ctx = geometry
    step = pl.program_id(0)

    @pl.when(step == 0)
    def _():
        total_ref[...] = jnp.zeros_like(total_ref)
        grad_taps_ref[...] = jnp.zeros_like(grad_taps_ref)

    channels = grad_c_ref.shape[1]
    grad_conv = grad_conv_ref[...]
    gate_b = projected_ref[:, :channels]
    values = projected_ref[:, 2 * channels :]
    product = gate_b * values
    one, two = shifted_down(product, before_ref[0].astype(f32))
    for k, shifted in enumerate((two, one, product)):
        grad_taps_ref[k : k + 1] += jnp.sum(grad_conv * shifted, axis=0, keepdims=True)
    one, two = shifted_up(grad_conv, behind_ref[0].astype(f32))
    grad_product = taps_ref[2:3] * grad_conv + taps_ref[1:2] * one + taps_ref[0:1] * two
    grad_projected_ref[:, :channels] = (grad_product * values).astype(bf16)
    grad_projected_ref[:, channels : 2 * channels] = grad_c_ref[...]
    grad_projected_ref[:, 2 * channels :] = (grad_product * gate_b).astype(bf16)
    total_ref[...] += lax.dot_general(
        normed_ref[...], grad_projected_ref[...], TN, preferred_element_type=f32
    )

    @pl.when(step == pl.num_programs(0) - 1)
    def _():
        low_ref[...] = total_ref[...].astype(bf16)
        pairs = slot_pairs(own_ref[0], plan, parts, segments, n_ctx, (low_ref,))
        copy_all([(b, a) for a, b in pairs], sems)


def row_call(body, steps, ins, outs, scratch=()):
    return pl.pallas_call(
        body,
        grid=(steps,),
        in_specs=[
            pl.BlockSpec(memory_space=pltpu.SMEM) if block is None else pl.BlockSpec(block, place)
            for _, block, place in ins
        ],
        out_specs=[
            pl.BlockSpec(memory_space=pl.ANY) if block is None else pl.BlockSpec(block, place)
            for _, _, block, place in outs
        ],
        out_shape=[jax.ShapeDtypeStruct(shape, dtype) for shape, dtype, _, _ in outs],
        scratch_shapes=list(scratch),
        compiler_params=pltpu.CompilerParams(
            vmem_limit_bytes=VMEM_LIMIT, dimension_semantics=("arbitrary",)
        ),
        cost_estimate=SMALL_COST,
    )(*[a for a, _, _ in ins])


def fits(tokens, w_in, w_out, w_gate, w_down, n_dp, n_ctx):
    width, hidden = w_gate.shape
    if n_dp % 2 or n_dp % (2 * n_ctx) or n_dp & (n_dp - 1) or n_ctx & (n_ctx - 1) or n_ctx < 2:
        return False
    depth = width // n_dp
    if width % n_dp or hidden % (n_dp * CHUNKS * 48) or w_in.shape[1] % (2 * n_ctx * 256):
        return False
    lanes = hidden // n_dp // CHUNKS * (n_dp // n_ctx // 2)
    wide = width // n_ctx
    return (
        lanes % 128 == 0
        and wide == lanes + 128
        and lanes == 384
        and wide % 256 == 0
        and depth % 16 == 0
        and 2 * depth <= 256
        and (w_in.shape[1] // n_ctx) % (2 * depth) == 0
        and width % (2 * depth) == 0
        and tokens.shape[1] % n_ctx == 0
        and n_ctx == 2
        and n_dp >= 16
    )


def fast_shards(tokens, w_in, w_out, w_gate, w_up, w_down, gain_mix, gain_ffn, kernel, cotangent):
    seqs, piece, width = tokens.shape
    rows = seqs * piece
    n_chip, n_ctx = lax.axis_size("chip"), lax.axis_size("ctx")
    slots = n_chip * n_ctx
    core = lax.axis_index("core")
    own_slot = lax.axis_index("chip") * n_ctx + lax.axis_index("ctx")
    own = own_slot.astype(jnp.int32)[None]
    depth = w_in.shape[0]
    groups = n_chip // n_ctx
    sub = w_down.shape[0] // CHUNKS
    lanes = groups * sub
    wide = w_out.shape[1]
    in_cols = w_in.shape[1] // 2
    in_parts, out_parts = in_cols // 256, wide // 256
    hidden_count = n_chip * sub
    channels = width // 2

    def mine_other(pair):
        return jnp.where(core == 0, pair[0], pair[1]), jnp.where(core == 0, pair[1], pair[0])

    def in_core_order(mine, other, axis):
        return jnp.where(
            core == 0,
            jnp.concatenate([mine, other], axis=axis),
            jnp.concatenate([other, mine], axis=axis),
        )

    small = jnp.concatenate([gain_mix[None], gain_ffn[None], kernel], axis=0)
    in_pair = w_in.reshape(depth, in_cols // depth, 2, depth).transpose(2, 0, 1, 3)
    in_pair = in_pair.reshape(2, depth, in_parts, 256).transpose(0, 2, 1, 3)
    in_mine, in_other = mine_other(in_pair)
    small_rows = jnp.pad(small, ((0, 11), (0, 256 - depth)))
    swapped = swap(jnp.concatenate([in_other.reshape(in_parts * depth, 256), small_rows], axis=0))
    in_got = swapped[: in_parts * depth].reshape(in_parts, depth, 256)
    in_block = in_core_order(in_mine, in_got, 1).reshape(in_parts * 2 * depth, 256)
    small_block = in_core_order(small, swapped[in_parts * depth :][:5, :depth], 1)
    small_block = jnp.pad(small_block, ((0, 11), (0, 256 - 2 * depth)))
    out_block = w_out.reshape(depth, out_parts, 256).transpose(1, 0, 2).reshape(-1, 256)
    mix_block = jnp.concatenate([in_block, out_block, small_block], axis=0)

    both = jnp.stack([w_gate, w_up]).reshape(2, depth, groups, 2, CHUNKS, sub)
    both = both.transpose(3, 4, 0, 1, 2, 5).reshape(2, CHUNKS, 2, depth, lanes)
    both_mine, both_other = mine_other(both)
    both_block = in_core_order(both_mine, swap(both_other), 2)
    both_block = both_block.reshape(CHUNKS, 4 * depth, lanes)
    down = w_down.reshape(CHUNKS, sub, wide)
    down_rest = down[:, :, lanes:].reshape(CHUNKS, 3, sub // 3, 128).transpose(0, 2, 1, 3)
    chunk_blocks = jnp.concatenate(
        [both_block, down[:, :, :lanes], down_rest.reshape(CHUNKS, sub // 3, lanes)], axis=1
    )

    mix_rows = mix_block.shape[0]
    mix_cut = -(-mix_rows // 32) * 16
    in_rows = in_parts * 2 * depth
    mix_segments = [
        (k * 2 * depth, 2 * depth, 0, 256, 0, 2 * depth, 0, in_cols, 256 * k)
        for k in range(in_parts)
    ]
    def out_segments(base, target):
        return [
            (base + k * depth, depth, 0, 256, target, depth, 0, wide, 256 * k)
            for k in range(out_parts)
        ]

    small_segment = (in_rows + out_parts * depth, 16, 0, 256, 2, 16, 0, 256, 0)
    mix_plan = gather_plan(mix_cut, mix_rows)
    chunk_rows = chunk_blocks.shape[1]
    chunk_cut = chunk_rows // 2
    chunk_segments = [
        (0, 2 * depth, 0, lanes, 0, 2 * depth, 0, lanes, 0),
        (2 * depth, 2 * depth, 0, lanes, 1, 2 * depth, 0, lanes, 0),
        (4 * depth, sub, 0, lanes, 2, sub, 0, wide, 0),
    ] + [
        (4 * depth + sub, sub // 3, 128 * k, 128, 2, sub, k * (sub // 3), wide, lanes)
        for k in range(3)
    ]
    whole_plan = [(0, i, None, 0, chunk_rows) for i in range(slots)]
    whole_geometry = (whole_plan, chunk_segments, n_ctx)
    step_geometry = (gather_plan(chunk_cut, chunk_rows), chunk_segments, n_ctx)

    token_rows = tokens.reshape(rows, width)
    inputs = jnp.concatenate([token_rows, swap(token_rows)], axis=0)
    go_rows = cotangent.reshape(rows, width)
    go = jnp.concatenate([go_rows, swap(go_rows)], axis=0)

    far, first_order, second_order = bit_masks()
    orders = (first_order, second_order)

    def doubled(hold, got):
        return jnp.concatenate([hold, got], axis=0)

    hold = mix_block[None]
    for mask in far:
        hold = doubled(hold, across(hold, mask))
    second_all, last_all = [
        lax.all_gather(after(block, hold), ("chip", "ctx")) for block in chunk_blocks[1:]
    ]
    mix_halves = [hold[:, :mix_cut], hold[:, mix_cut:]]
    next_hold = after(chunk_blocks[0][None], hold)
    far_left = list(far)
    early = [inputs, go]
    for step in range(len(first_order)):
        got = [across(h, order[step]) for h, order in zip(mix_halves, orders)]
        if far_left:
            next_got = across(next_hold, far_left.pop(0))
            next_hold = doubled(next_hold, next_got)
        if early:
            got = [after(g, early[0]) for g in got]
            early = early[1:]
        if step + 1 < len(first_order):
            got = [after(g, next_got) for g in got]
            mix_halves = [doubled(h, g) for h, g in zip(mix_halves, got)]
            next_hold = after(next_hold, *got)
    mix_parts = [mix_halves[0], got[0], mix_halves[1], got[1]]
    for mask in far_left:
        next_got = across(next_hold, mask)
        next_hold = doubled(next_hold, next_got)
    in_half, out_half, small_all = move(
        own,
        mix_parts,
        [(width, n_ctx * in_cols), (channels, width), (n_chip * 16, n_ctx * 256)],
        (mix_plan, mix_segments + out_segments(in_rows, 1) + [small_segment], n_ctx),
        4,
        False,
    )
    in_half = after(in_half, next_got)
    next_halves = [next_hold[:, :chunk_cut], next_hold[:, chunk_cut:]]

    def step_of(halves, step):
        return [across(h, order[step]) for h, order in zip(halves, orders)]

    def all_after(blocks, *done):
        return [after(block, *done) for block in blocks]

    small_all = small_all.reshape(n_chip, 16, n_ctx * 256)[:, :5, : 2 * depth].astype(f32)
    first_gain = small_all[:, 0].reshape(width)
    second_gain = small_all[:, 1].reshape(width)
    taps = small_all[:, 2:].reshape(n_chip, 3, 2, depth)
    taps = jnp.where(core == 0, taps[:, :, 0], taps[:, :, 1]).transpose(1, 0, 2)
    taps = taps.reshape(3, channels)

    blocks = 2 * seqs

    def at(i):
        return (i, 0)

    def still(i):
        return (0, 0)

    def other(i):
        return ((i + seqs) % blocks, 0)

    wide_rows, thin_rows = (piece, width), (piece, channels)
    taps = jnp.pad(taps, ((0, 5), (0, 0)))
    next_got = step_of(next_halves, 0)
    normed_low, projected = row_call(
        in_kernel,
        blocks,
        [
            (inputs, wide_rows, at),
            (first_gain[None], (1, width), still),
            (in_half, in_half.shape, still),
        ],
        [
            ((2 * rows, width), bf16, wide_rows, at),
            ((2 * rows, 3 * channels), f32, (piece, 3 * channels), at),
        ],
    )
    tail = projected.reshape(blocks, piece, 3 * channels)[:, piece - 2 :]
    tail = (tail[:, :, :channels] * tail[:, :, 2 * channels :]).astype(bf16)
    before = passed_along(tail, "ctx", 1)
    halo = (1, 2, channels)

    def halo_at(i):
        return (i, 0, 0)

    conv_taps = after(taps, *next_got)
    next_halves = [
        doubled(h, g) for h, g in zip(next_halves, all_after(next_got, projected))
    ]
    next_got = step_of(next_halves, 1)
    mixer_out, convolved, branch = row_call(
        conv_kernel,
        blocks,
        [
            (projected, (piece, 3 * channels), at),
            (before, halo, halo_at),
            (conv_taps, taps.shape, still),
            (out_half, out_half.shape, still),
        ],
        [
            ((2 * rows, channels), bf16, thin_rows, at),
            ((2 * rows, channels), f32, thin_rows, at),
            ((2 * rows, width), bf16, wide_rows, at),
        ],
    )
    residual, nffn_low = row_call(
        norm_kernel,
        blocks,
        [
            (inputs, wide_rows, at),
            (branch, wide_rows, at),
            (swap(branch), wide_rows, other),
            (second_gain[None], (1, width), still),
        ],
        [((2 * rows, width), f32, wide_rows, at), ((2 * rows, width), bf16, wide_rows, at)],
    )

    next_parts = [next_halves[0], next_got[0], next_halves[1], next_got[1]]
    next_parts = all_after(next_parts, nffn_low)

    totals, first_grads = ffn_chunk(
        own, nffn_low, go, next_parts, None, step_geometry, step_geometry, hidden_count
    )
    first_stages = Stages(first_grads)
    totals, second_grads = ffn_chunk(
        own, nffn_low, go, [second_all], totals, whole_geometry, step_geometry, hidden_count
    )
    second_stages = Stages(second_grads)
    nffn_then = after(nffn_low, *first_stages.got)
    first_stages.advance(totals[1])
    totals, last_grads = ffn_chunk(
        own, nffn_then, go, [last_all], totals, whole_geometry, step_geometry, hidden_count, last=True
    )
    ffn_out, grad_low = totals
    last_stages = Stages(last_grads)
    grad_got = swap(after(grad_low, *first_stages.got, *second_stages.got))
    first_stages.advance(grad_low)
    second_stages.advance(grad_low)

    def turned(i):
        return ((i + seqs) % blocks, 0)

    def turned_back(i):
        return (i, 0)

    def own_place(i):
        return (jnp.maximum(i - seqs, 0), 0)

    def gate_c_place(i):
        return ((i + seqs) % blocks, 1)

    out_plan = [(0, i, None, 0, out_parts * depth) for i in range(slots)]
    grad_residual, grad_conv, grad_c, grad_gain_ffn, grad_out_slots = row_call(
        functools.partial(branch_grad_kernel, seqs, (out_plan, out_segments(0, 0), n_ctx)),
        blocks,
        [
            (own, None, None),
            (grad_low, wide_rows, turned),
            (grad_got, wide_rows, turned_back),
            (residual, wide_rows, turned),
            (go, wide_rows, turned),
            (second_gain[None], (1, width), still),
            (mixer_out, thin_rows, turned),
            (convolved, thin_rows, turned),
            (projected, thin_rows, gate_c_place),
            (out_half, out_half.shape, still),
        ],
        [
            ((rows, width), f32, wide_rows, own_place),
            ((2 * rows, channels), f32, thin_rows, turned),
            ((2 * rows, channels), bf16, thin_rows, turned),
            ((1, width), f32, (1, width), still),
            ((slots, out_parts * depth, 256), bf16, None, None),
        ],
        scratch=[
            pltpu.VMEM((channels, width), f32),
            pltpu.VMEM((channels, width), bf16),
            pltpu.SemaphoreType.DMA((slots * out_parts,)),
        ],
    )
    grad_gain_ffn = grad_gain_ffn[0]
    stages = (first_stages, second_stages, last_stages)
    grad_c_then = after(grad_c, *(g for s in stages for g in s.got))
    for s in stages:
        s.advance(grad_c)
    head = grad_conv.reshape(blocks, piece, channels)[:, :2].astype(bf16)
    behind = passed_along(head, "ctx", -1)
    out_sum = lax.psum_scatter(grad_out_slots, ("chip", "ctx"), scatter_dimension=0).astype(f32)
    sum_plan = gather_plan(in_rows // 2, in_rows)
    grad_projected, grad_kernel, *mix_grad_parts = row_call(
        functools.partial(in_grad_kernel, (sum_plan, mix_segments, n_ctx), 4),
        blocks,
        [
            (own, None, None),
            (grad_conv, thin_rows, at),
            (behind, halo, halo_at),
            (before, halo, halo_at),
            (projected, (piece, 3 * channels), at),
            (grad_c_then, thin_rows, at),
            (normed_low, wide_rows, at),
            (taps, taps.shape, still),
        ],
        [
            ((2 * rows, 3 * channels), bf16, (piece, 3 * channels), at),
            ((8, channels), f32, (8, channels), still),
        ]
        + [(shape, bf16, None, None) for shape in part_shapes(sum_plan, 256)],
        scratch=[
            pltpu.VMEM((width, 3 * channels), f32),
            pltpu.VMEM((width, 3 * channels), bf16),
            pltpu.SemaphoreType.DMA((len(sum_plan) * len(mix_segments),)),
        ],
    )
    grad_kernel = grad_kernel[:3]
    mix_stages = Stages(mix_grad_parts)
    for s in stages:
        s.advance(grad_projected)
    grad_other = cross_cols(grad_projected[rows:], in_half).astype(bf16)
    for s in (mix_stages, *stages):
        s.advance(grad_other)
    other_got = swap(grad_other)
    grad_mine = cross_cols(after(grad_projected[:rows], other_got), in_half)
    for s in (mix_stages, second_stages, last_stages):
        s.advance(grad_mine)
    grad_normed = grad_mine + other_got.astype(f32)
    ffn_late = after(ffn_out, grad_other)
    ffn_got = swap(ffn_late[rows:].astype(bf16))
    result = after(residual, grad_mine)[:rows] + (ffn_late[:rows] + ffn_got.astype(f32))
    result = result.astype(bf16).reshape(seqs, piece, width)
    own_inputs = token_rows.astype(f32)
    scale_mix = lax.rsqrt(jnp.mean(own_inputs * own_inputs, axis=-1, keepdims=True) + EPSILON)
    grad_in_norm, grad_gain_mix = norm_backward(own_inputs, scale_mix, first_gain, grad_normed)
    grad_tokens = (grad_residual + grad_in_norm).reshape(seqs, piece, width)

    mix_stages.advance(grad_tokens)
    last_stages.advance(grad_tokens)
    while mix_stages.total is None:
        mix_stages.advance()

    chunk_sum = jnp.stack([s.total for s in stages])
    both_sum = chunk_sum[:, : 4 * depth].reshape(CHUNKS, 2, 2, depth, lanes).transpose(2, 0, 1, 3, 4)
    both_mine, both_other = mine_other(both_sum)
    both_got = swap(both_other)
    both_sum = in_core_order(both_mine[None], both_got[None], 0)
    both_sum = both_sum.reshape(2, CHUNKS, 2, depth, groups, sub).transpose(2, 3, 4, 0, 1, 5)
    both_sum = both_sum.reshape(2, depth, 2 * CHUNKS * lanes)
    down_rest = chunk_sum[:, 4 * depth + sub :].reshape(CHUNKS, sub // 3, 3, 128)
    down_rest = down_rest.transpose(0, 2, 1, 3).reshape(CHUNKS, sub, 128)
    final_down = jnp.concatenate([chunk_sum[:, 4 * depth : 4 * depth + sub], down_rest], axis=2)
    final_down = final_down.reshape(CHUNKS * sub, wide)

    in_sum = mix_stages.total.reshape(in_parts, 2, depth, 256).transpose(1, 0, 2, 3)
    in_mine, in_other = mine_other(in_sum)
    in_sum = in_core_order(in_mine[None], swap(in_other)[None], 0)
    in_sum = in_sum.transpose(0, 2, 1, 3).reshape(2, depth, in_cols // depth, depth)
    final_in = in_sum.transpose(1, 2, 0, 3).reshape(depth, 2 * in_cols)
    final_out = out_sum.reshape(out_parts, depth, 256).transpose(1, 0, 2)
    final_out = final_out.reshape(depth, wide)

    grad_taps = grad_kernel.reshape(3, n_chip, 1, depth)
    grad_taps = jnp.where(
        jnp.arange(2).reshape(1, 1, 2, 1) == core, grad_taps, jnp.zeros_like(grad_taps)
    ).reshape(3, width)
    small_grad = jnp.concatenate([grad_gain_mix[None], grad_gain_ffn[None], grad_taps], axis=0)
    small_sum = small_grad.reshape(5, n_chip, 2 * depth).transpose(1, 0, 2)
    for bit in range(n_ctx.bit_length() - 1):
        small_sum = small_sum + across(small_sum, 1 << bit)
    for bit in range(n_chip.bit_length() - 1):
        mask = n_chip >> (bit + 1)
        low, high = small_sum[: small_sum.shape[0] // 2], small_sum[small_sum.shape[0] // 2 :]
        upper = jnp.bitwise_and(lax.axis_index("chip"), mask) != 0
        small_sum = jnp.where(upper, high, low) + across(jnp.where(upper, low, high), mask * n_ctx)
    small_mine, small_other = mine_other(small_sum[0].reshape(5, 2, depth).transpose(1, 0, 2))
    small_sum = small_mine + swap(small_other)
    return (
        result,
        grad_tokens,
        final_in,
        final_out,
        both_sum[0],
        both_sum[1],
        final_down,
        small_sum[0],
        small_sum[1],
        small_sum[2:5],
    )


def solution(mesh):
    n_dp, n_ctx = mesh.shape["dp"], mesh.shape["ctx"]

    def placed(dp):
        whole, cut = P(dp, "ctx", None), P(dp, "ctx")
        ins = (whole, cut, cut, cut, cut, cut, P(dp), P(dp), P(None, dp), whole)
        outs = (whole, whole, cut, cut, cut, cut, cut, P(dp), P(dp), P(None, dp))
        return ins, outs

    def run(tokens, w_in, w_out, w_gate, w_up, w_down, gain_mix, gain_ffn, kernel, cotangent):
        if fits(tokens, w_in, w_out, w_gate, w_down, n_dp, n_ctx):
            cut_mesh = Mesh(mesh.devices.reshape(n_dp // 2, 2, n_ctx), ("chip", "core", "ctx"))
            body, on, (ins, outs) = fast_shards, cut_mesh, placed(("chip", "core"))
        else:
            body, on, (ins, outs) = plain_shards, mesh, placed("dp")
        call = jax.shard_map(body, mesh=on, in_specs=ins, out_specs=outs, check_vma=False)
        return call(
            tokens, w_in, w_out, w_gate, w_up, w_down, gain_mix, gain_ffn, kernel, cotangent
        )

    return run
```

```python
import functools
import jax
import jax.numpy as jnp
from jax import lax
from jax.experimental import pallas as pl
from jax.experimental.pallas import tpu as pltpu
from jax.sharding import Mesh
from jax.sharding import PartitionSpec as P

EPSILON = 1e-05
CHUNKS = 3
f32 = jnp.float32
bf16 = jnp.bfloat16


def passed_along(block, axis, distance):
    devices = range(lax.axis_size(axis))
    route = [(i - distance, i) for i in devices if i - distance in devices]
    return lax.ppermute(block, axis, route)


def cross_rows(left_operand, right_operand):
    return lax.dot_general(
        left_operand, right_operand, (((0,), (0,)), ((), ())), preferred_element_type=jnp.float32
    )


def cross_cols(left_operand, right_operand):
    return lax.dot_general(
        left_operand, right_operand, (((1,), (1,)), ((), ())), preferred_element_type=jnp.float32
    )


def norm_forward(values, gain):
    scale = lax.rsqrt(jnp.mean(values * values, axis=-1, keepdims=True) + EPSILON)
    return (values * scale * gain, scale)


def norm_backward(values, scale, gain, incoming):
    weighted = incoming * gain
    gain_grad = jnp.sum(incoming * values * scale, axis=0)
    inner = jnp.mean(weighted * values, axis=-1, keepdims=True)
    return (scale * weighted - values * (scale * scale * scale) * inner, gain_grad)


def plain_shards(tokens, w_in, w_out, w_gate, w_up, w_down, gain_mix, gain_ffn, kernel, cotangent):
    seq_count, piece_len, model_width = tokens.shape
    row_count = seq_count * piece_len
    small_params = jnp.concatenate([gain_mix[None], gain_ffn[None], kernel], axis=0)
    input_columns, out_cols, gate_cols, up_cols, down_cols = (
        lax.all_gather(w_in, "ctx", axis=1, tiled=True),
        lax.all_gather(w_out, "ctx", axis=1, tiled=True),
        lax.all_gather(w_gate, "ctx", axis=1, tiled=True),
        lax.all_gather(w_up, "ctx", axis=1, tiled=True),
        lax.all_gather(w_down, "ctx", axis=1, tiled=True),
    )
    full_in, full_out, full_gate, full_up, full_down, small_full = (
        lax.all_gather(input_columns, "dp", axis=0, tiled=True),
        lax.all_gather(out_cols, "dp", axis=0, tiled=True),
        lax.all_gather(gate_cols, "dp", axis=0, tiled=True),
        lax.all_gather(up_cols, "dp", axis=0, tiled=True),
        lax.all_gather(down_cols, "dp", axis=0, tiled=True),
        lax.all_gather(small_params, "dp", axis=1, tiled=True),
    )
    small_float = small_full.astype(jnp.float32)
    first_gain = small_float[0]
    second_gain = small_float[1]
    taps = small_float[2:5]
    inputs = tokens.reshape(row_count, model_width).astype(jnp.float32)
    normed, scale_mix = norm_forward(inputs, first_gain)
    normed_low = normed.astype(jnp.bfloat16)
    projected = jnp.dot(normed_low, full_in, preferred_element_type=jnp.float32)
    gate_b = projected[:, :model_width]
    gate_c = projected[:, model_width : 2 * model_width]
    values = projected[:, 2 * model_width :]
    product = (gate_b * values).reshape(seq_count, piece_len, model_width)
    previous = passed_along(product[:, piece_len - 2 :].astype(jnp.bfloat16), "ctx", 1).astype(
        jnp.float32
    )
    padded = jnp.concatenate([previous, product], axis=1)
    convolved = taps[0] * padded[:, :-2] + taps[1] * padded[:, 1:-1] + taps[2] * padded[:, 2:]
    convolved = convolved.reshape(row_count, model_width)
    mixer_out = (gate_c * convolved).astype(jnp.bfloat16)
    residual = inputs + jnp.dot(mixer_out, full_out, preferred_element_type=jnp.float32)
    feedforward_normed, scale_ffn = norm_forward(residual, second_gain)
    nffn_low = feedforward_normed.astype(jnp.bfloat16)
    gate = jnp.dot(nffn_low, full_gate, preferred_element_type=jnp.float32)
    up_value = jnp.dot(nffn_low, full_up, preferred_element_type=jnp.float32)
    sigmoid_gate = jax.nn.sigmoid(gate)
    activated = gate * sigmoid_gate
    hidden = (activated * up_value).astype(jnp.bfloat16)
    result = residual + jnp.dot(hidden, full_down, preferred_element_type=jnp.float32)
    result = result.astype(jnp.bfloat16).reshape(seq_count, piece_len, model_width)
    back_in, output_backward, back_gate, back_up, back_down = (
        lax.all_gather(w_in, "ctx", axis=1, tiled=True),
        lax.all_gather(w_out, "ctx", axis=1, tiled=True),
        lax.all_gather(w_gate, "ctx", axis=1, tiled=True),
        lax.all_gather(w_up, "ctx", axis=1, tiled=True),
        lax.all_gather(w_down, "ctx", axis=1, tiled=True),
    )
    input_weight_used, use_out, use_gate, use_up, use_down = (
        lax.all_gather(back_in, "dp", axis=0, tiled=True),
        lax.all_gather(output_backward, "dp", axis=0, tiled=True),
        lax.all_gather(back_gate, "dp", axis=0, tiled=True),
        lax.all_gather(back_up, "dp", axis=0, tiled=True),
        lax.all_gather(back_down, "dp", axis=0, tiled=True),
    )
    grad_out = cotangent.reshape(row_count, model_width)
    grad_out_float = grad_out.astype(jnp.float32)
    grad_w_down = cross_rows(hidden, grad_out)
    grad_hidden = cross_cols(grad_out, use_down)
    grad_gate = (
        grad_hidden * up_value * sigmoid_gate * (1.0 + gate * (1.0 - sigmoid_gate))
    ).astype(jnp.bfloat16)
    grad_up = (grad_hidden * activated).astype(jnp.bfloat16)
    grad_w_gate = cross_rows(nffn_low, grad_gate)
    grad_w_up = cross_rows(nffn_low, grad_up)
    grad_nffn = cross_cols(grad_gate, use_gate) + cross_cols(grad_up, use_up)
    residual_norm_gradient, grad_gain_ffn = norm_backward(
        residual, scale_ffn, second_gain, grad_nffn
    )
    grad_residual = grad_out_float + residual_norm_gradient
    grad_branch = grad_residual.astype(jnp.bfloat16)
    grad_w_out = cross_rows(mixer_out, grad_branch)
    grad_mix = cross_cols(grad_branch, use_out)
    grad_c = grad_mix * convolved
    grad_conv = (grad_mix * gate_c).reshape(seq_count, piece_len, model_width)
    following = passed_along(grad_conv[:, :2].astype(jnp.bfloat16), "ctx", -1).astype(jnp.float32)
    extended = jnp.concatenate([grad_conv, following], axis=1)
    grad_product = (
        taps[2] * extended[:, :-2] + taps[1] * extended[:, 1:-1] + taps[0] * extended[:, 2:]
    )
    grad_kernel = jnp.stack(
        [
            jnp.sum(grad_conv * padded[:, shift_at : shift_at + piece_len], axis=(0, 1))
            for shift_at in range(3)
        ],
        axis=0,
    )
    grad_product = grad_product.reshape(row_count, model_width)
    grad_projected = jnp.concatenate(
        [grad_product * values, grad_c, grad_product * gate_b], axis=1
    ).astype(jnp.bfloat16)
    grad_w_in = cross_rows(normed_low, grad_projected)
    grad_normed = cross_cols(grad_projected, input_weight_used)
    grad_in_norm, grad_gain_mix = norm_backward(inputs, scale_mix, first_gain, grad_normed)
    grad_tokens = (grad_residual + grad_in_norm).reshape(seq_count, piece_len, model_width)
    small_grad = jnp.concatenate([grad_gain_mix[None], grad_gain_ffn[None], grad_kernel], axis=0)
    part_in, part_out, part_gate, part_up, part_down, small_part = (
        lax.psum_scatter(grad_w_in, "dp", scatter_dimension=0, tiled=True),
        lax.psum_scatter(grad_w_out, "dp", scatter_dimension=0, tiled=True),
        lax.psum_scatter(grad_w_gate, "dp", scatter_dimension=0, tiled=True),
        lax.psum_scatter(grad_w_up, "dp", scatter_dimension=0, tiled=True),
        lax.psum_scatter(grad_w_down, "dp", scatter_dimension=0, tiled=True),
        lax.psum_scatter(small_grad, "dp", scatter_dimension=1, tiled=True),
    )
    final_in, final_out, final_gate, final_up, final_down = (
        lax.psum_scatter(part_in, "ctx", scatter_dimension=1, tiled=True),
        lax.psum_scatter(part_out, "ctx", scatter_dimension=1, tiled=True),
        lax.psum_scatter(part_gate, "ctx", scatter_dimension=1, tiled=True),
        lax.psum_scatter(part_up, "ctx", scatter_dimension=1, tiled=True),
        lax.psum_scatter(part_down, "ctx", scatter_dimension=1, tiled=True),
    )
    small_total = lax.psum(small_part, "ctx")
    return (
        result,
        grad_tokens,
        final_in,
        final_out,
        final_gate,
        final_up,
        final_down,
        small_total[0],
        small_total[1],
        small_total[2:5],
    )


SMALL_COST = pl.CostEstimate(flops=1 << 16, bytes_accessed=1 << 16, transcendentals=0)
VMEM_LIMIT = 60 * 1024 * 1024
NT = (((1,), (1,)), ((), ()))
TN = (((0,), (0,)), ((), ()))


def swap(block):
    return lax.ppermute(block, "core", [(0, 1), (1, 0)])


def across(block, mask):
    count = lax.axis_size("chip") * lax.axis_size("ctx")
    return lax.ppermute(block, ("chip", "ctx"), [(i, i ^ mask) for i in range(count)])


def bit_masks():
    n_chip, n_ctx = lax.axis_size("chip"), lax.axis_size("ctx")
    ctx_bits = [1 << b for b in range(n_ctx.bit_length() - 1)]
    near = [n_ctx]
    far = [n_ctx << b for b in range(1, n_chip.bit_length() - 1)]
    return far, near + ctx_bits, ctx_bits + near


def after(value, *done):
    return lax.optimization_barrier((value, *done))[0]


def gather_plan(cut, total):
    far, first_order, second_order = bit_masks()
    plan = []
    for operand, order, row0, rows in ((0, first_order, 0, cut), (2, second_order, cut, total - cut)):
        masks = [0]
        for mask in far + order[:-1]:
            masks = masks + [m ^ mask for m in masks]
        for index, mask in enumerate(masks):
            plan.append((operand, index, mask, row0, rows))
            plan.append((operand + 1, index, mask ^ order[-1], row0, rows))
    return plan


def gather(block, cut):
    far, first_order, second_order = bit_masks()
    hold = block[None]
    for mask in far:
        hold = jnp.concatenate([hold, across(hold, mask)], axis=0)
    parts = []
    for order, half in ((first_order, hold[:, :cut]), (second_order, hold[:, cut:])):
        for mask in order[:-1]:
            half = jnp.concatenate([half, across(half, mask)], axis=0)
        parts += [half, across(half, order[-1])]
    return parts


def scatter_steps(parts):
    far, first_order, second_order = bit_masks()

    def send(block, mask):
        return across(block.astype(bf16), mask)

    orders = (first_order, second_order)
    got = yield [send(parts[1], first_order[-1]), send(parts[3], second_order[-1])]
    keeps = [k.astype(f32) + g.astype(f32) for k, g in zip((parts[0], parts[2]), got)]
    for step in range(len(first_order) - 2, -1, -1):
        mid = keeps[0].shape[0] // 2
        got = yield [send(k[mid:], order[step]) for k, order in zip(keeps, orders)]
        keeps = [k[:mid] + g.astype(f32) for k, g in zip(keeps, got)]
    keep = jnp.concatenate(keeps, axis=1)
    for mask in reversed(far):
        mid = keep.shape[0] // 2
        (got,) = yield [send(keep[mid:], mask)]
        keep = keep[:mid] + got.astype(f32)
    return keep[0]


class Stages:
    def __init__(self, parts):
        self.steps = scatter_steps(parts)
        self.got = next(self.steps)
        self.total = None

    def advance(self, *done):
        if self.total is not None:
            return
        try:
            self.got = self.steps.send([after(g, *done) for g in self.got])
        except StopIteration as end:
            self.got, self.total = [], end.value


def slot_pairs(own, plan, refs, segments, n_ctx, targets):
    pairs = []
    for operand, index, mask, row0, nrows in plan:
        slot = index if mask is None else jnp.bitwise_xor(own, mask)
        y = lax.rem(slot, n_ctx)
        chip = lax.div(slot, n_ctx)
        src = refs[operand].at[index]
        for seg_row, seg_rows, lane0, lanes, target, row_step, row_add, lane_step, lane_add in segments:
            low, high = max(seg_row, row0), min(seg_row + seg_rows, row0 + nrows)
            if low >= high:
                continue
            row = pl.multiple_of(chip * row_step + row_add + (low - seg_row), 16)
            lane = pl.multiple_of(y * lane_step + lane_add, 128)
            pairs.append(
                (
                    src.at[pl.ds(low - row0, high - low), pl.ds(lane0, lanes)],
                    targets[target].at[pl.ds(row, high - low), pl.ds(lane, lanes)],
                )
            )
    return pairs


def copy_all(pairs, sems):
    copies = [pltpu.make_async_copy(a, b, sems.at[i]) for i, (a, b) in enumerate(pairs)]
    for copy in copies:
        copy.start()
    for copy in copies:
        copy.wait()


def part_count(plan):
    return 1 + max(entry[0] for entry in plan)


def part_shapes(plan, lanes):
    shapes = {}
    for operand, index, _, _, rows in plan:
        shapes[operand] = (max(index + 1, shapes.get(operand, (0,))[0]), rows, lanes)
    return [shapes[operand] for operand in sorted(shapes)]


def ffn_kernel(geometry, out_geometry, first, own_ref, n_ref, go_ref, *refs):
    plan, segments, n_ctx = geometry
    out_plan = out_geometry[0]
    count, out_count = part_count(plan), part_count(out_plan)
    weights, refs = refs[:count], refs[count:]
    if not first:
        res_in, gn_in = refs[:2]
        refs = refs[2:]
    res_ref, gn_ref = refs[:2]
    refs = refs[2:]
    grads, refs = refs[:out_count], refs[out_count:]
    gate_m, up_m, down_m, d_gate, d_up, d_down, h_m, gg_m, gu_m, sems = refs
    own = own_ref[0]
    targets = (gate_m, up_m, down_m)

    @pl.when(pl.program_id(0) == 0)
    def _():
        d_gate[...] = jnp.zeros_like(d_gate)
        d_up[...] = jnp.zeros_like(d_up)
        d_down[...] = jnp.zeros_like(d_down)
        copy_all(slot_pairs(own, plan, weights, segments, n_ctx, targets), sems)

    n = n_ref[...]
    go = go_ref[...]
    hidden_count = gate_m.shape[1]
    step = 256
    for start in range(0, hidden_count, step):
        cols = slice(start, start + step)
        g = jnp.dot(n, gate_m[:, cols], preferred_element_type=f32)
        u = jnp.dot(n, up_m[:, cols], preferred_element_type=f32)
        gh = lax.dot_general(go, down_m[cols, :], NT, preferred_element_type=f32)
        s = jax.nn.sigmoid(g)
        act = g * s
        h_m[:, cols] = (act * u).astype(bf16)
        gg_m[:, cols] = (gh * u * s * (1.0 + g * (1.0 - s))).astype(bf16)
        gu_m[:, cols] = (gh * act).astype(bf16)
    res = jnp.dot(h_m[...], down_m[...], preferred_element_type=f32)
    gn = lax.dot_general(gg_m[...], gate_m[...], NT, preferred_element_type=f32)
    gn = gn + lax.dot_general(gu_m[...], up_m[...], NT, preferred_element_type=f32)
    if not first:
        res = res_in[...] + res
        gn = gn_in[...] + gn
    res_ref[...] = res
    gn_ref[...] = gn.astype(gn_ref.dtype)
    d_gate[...] += lax.dot_general(n, gg_m[...], TN, preferred_element_type=f32)
    d_up[...] += lax.dot_general(n, gu_m[...], TN, preferred_element_type=f32)
    d_down[...] += lax.dot_general(h_m[...], go, TN, preferred_element_type=f32)

    @pl.when(pl.program_id(0) == pl.num_programs(0) - 1)
    def _():
        gate_m[...] = d_gate[...].astype(bf16)
        up_m[...] = d_up[...].astype(bf16)
        down_m[...] = d_down[...].astype(bf16)
        pairs = slot_pairs(own, out_plan, grads, segments, n_ctx, targets)
        copy_all([(b, a) for a, b in pairs], sems)


def ffn_chunk(
    own, nffn, go, weights, totals, geometry, out_geometry, hidden_count, last=False, rows=256
):
    total, width = nffn.shape
    first = totals is None
    plan, segments, _ = geometry
    out_plan = out_geometry[0]
    count, out_count = part_count(plan), part_count(out_plan)
    lanes = weights[0].shape[-1]
    row_spec = pl.BlockSpec((rows, width), lambda i, o: (i, 0))
    any_spec = pl.BlockSpec(memory_space=pl.ANY)
    outs = pl.pallas_call(
        functools.partial(ffn_kernel, geometry, out_geometry, first),
        out_shape=[jax.ShapeDtypeStruct((total, width), d) for d in (f32, bf16 if last else f32)]
        + [jax.ShapeDtypeStruct(s, bf16) for s in part_shapes(out_plan, lanes)],
        grid_spec=pltpu.PrefetchScalarGridSpec(
            num_scalar_prefetch=1,
            grid=(total // rows,),
            in_specs=[row_spec] * 2 + [any_spec] * count + [row_spec] * (0 if first else 2),
            out_specs=[row_spec] * 2 + [any_spec] * out_count,
            scratch_shapes=[
                pltpu.VMEM((width, hidden_count), bf16),
                pltpu.VMEM((width, hidden_count), bf16),
                pltpu.VMEM((hidden_count, width), bf16),
                pltpu.VMEM((width, hidden_count), f32),
                pltpu.VMEM((width, hidden_count), f32),
                pltpu.VMEM((hidden_count, width), f32),
                pltpu.VMEM((rows, hidden_count), bf16),
                pltpu.VMEM((rows, hidden_count), bf16),
                pltpu.VMEM((rows, hidden_count), bf16),
                pltpu.SemaphoreType.DMA((max(len(plan), len(out_plan)) * len(segments),)),
            ],
        ),
        input_output_aliases={} if first else {3 + count: 0} if last else {3 + count: 0, 4 + count: 1},
        compiler_params=pltpu.CompilerParams(
            vmem_limit_bytes=VMEM_LIMIT, dimension_semantics=("arbitrary",)
        ),
        cost_estimate=SMALL_COST,
    )(own, nffn, go, *weights, *(() if first else totals))
    return outs[:2], outs[2:]


def move_kernel(geometry, count, outward, own_ref, *refs):
    plan, segments, n_ctx = geometry
    sems = refs[-1]
    refs = refs[:-1]
    if outward:
        targets, parts = refs[: len(refs) - count], refs[len(refs) - count :]
    else:
        parts, targets = refs[:count], refs[count:]
    pairs = slot_pairs(own_ref[0], plan, parts, segments, n_ctx, targets)
    copy_all([(b, a) for a, b in pairs] if outward else pairs, sems)


def move(own, arrays, shapes, geometry, count, outward):
    plan, segments, _ = geometry
    any_spec = pl.BlockSpec(memory_space=pl.ANY)
    vmem_spec = pl.BlockSpec(memory_space=pltpu.VMEM)
    return pl.pallas_call(
        functools.partial(move_kernel, geometry, count, outward),
        out_shape=[jax.ShapeDtypeStruct(s, bf16) for s in shapes],
        in_specs=[pl.BlockSpec(memory_space=pltpu.SMEM)]
        + [vmem_spec if outward else any_spec] * len(arrays),
        out_specs=[any_spec if outward else vmem_spec] * len(shapes),
        scratch_shapes=[pltpu.SemaphoreType.DMA((len(plan) * len(segments),))],
        compiler_params=pltpu.CompilerParams(vmem_limit_bytes=VMEM_LIMIT),
        cost_estimate=SMALL_COST,
    )(own, *arrays)


def shifted_down(block, before):
    row = lax.broadcasted_iota(jnp.int32, block.shape, 0)
    one = jnp.where(row == 0, before[1:2], pltpu.roll(block, 1, 0))
    two = jnp.where(row == 0, before[0:1], pltpu.roll(block, 2, 0))
    return one, jnp.where(row == 1, before[1:2], two)


def shifted_up(block, behind):
    count = block.shape[0]
    row = lax.broadcasted_iota(jnp.int32, block.shape, 0)
    one = jnp.where(row == count - 1, behind[0:1], pltpu.roll(block, count - 1, 0))
    two = jnp.where(row == count - 2, behind[0:1], pltpu.roll(block, count - 2, 0))
    return one, jnp.where(row == count - 1, behind[1:2], two)


def in_kernel(x_ref, gain_ref, w_ref, normed_ref, projected_ref, tail_ref):
    x = x_ref[...].astype(f32)
    scale = lax.rsqrt(jnp.mean(x * x, axis=-1, keepdims=True) + EPSILON)
    normed = (x * scale * gain_ref[...]).astype(bf16)
    normed_ref[...] = normed
    projected = jnp.dot(normed, w_ref[...], preferred_element_type=f32)
    projected_ref[...] = projected
    channels = projected.shape[1] // 3
    product = projected[-8:, :channels] * projected[-8:, 2 * channels :]
    tail_ref[0] = product[6:].astype(bf16)


def conv_kernel(projected_ref, before_ref, taps_ref, w_ref, mixer_ref, conv_ref, branch_ref):
    channels = conv_ref.shape[1]
    product = projected_ref[:, :channels] * projected_ref[:, 2 * channels :]
    one, two = shifted_down(product, before_ref[0].astype(f32))
    conv = taps_ref[0:1] * two + taps_ref[1:2] * one + taps_ref[2:3] * product
    conv_ref[...] = conv
    mixer = (projected_ref[:, channels : 2 * channels] * conv).astype(bf16)
    mixer_ref[...] = mixer
    branch_ref[...] = jnp.dot(mixer, w_ref[...], preferred_element_type=f32).astype(bf16)


def norm_kernel(x_ref, branch_ref, got_ref, gain_ref, residual_ref, normed_ref):
    residual = x_ref[...].astype(f32) + (branch_ref[...].astype(f32) + got_ref[...].astype(f32))
    residual_ref[...] = residual
    scale = lax.rsqrt(jnp.mean(residual * residual, axis=-1, keepdims=True) + EPSILON)
    normed_ref[...] = (residual * scale * gain_ref[...]).astype(bf16)


def branch_grad_kernel(
    own_first, geometry, own_ref, gn_ref, got_ref, residual_ref, go_ref, gain_ref, mixer_ref,
    conv_ref, gate_c_ref, w_ref, grad_residual_ref, grad_conv_ref, grad_c_ref, grad_gain_ref,
    head_ref, part_ref, total_ref, low_ref, sems,
):
    plan, segments, n_ctx = geometry
    step = pl.program_id(0)

    @pl.when(step == 0)
    def _():
        total_ref[...] = jnp.zeros_like(total_ref)
        grad_gain_ref[...] = jnp.zeros_like(grad_gain_ref)

    incoming = gn_ref[...].astype(f32) + got_ref[...].astype(f32)
    residual = residual_ref[...]
    scale = lax.rsqrt(jnp.mean(residual * residual, axis=-1, keepdims=True) + EPSILON)
    weighted = incoming * gain_ref[...]

    @pl.when(step >= own_first)
    def _():
        grad_gain_ref[...] += jnp.sum(incoming * residual * scale, axis=0, keepdims=True)

    inner = jnp.mean(weighted * residual, axis=-1, keepdims=True)
    grad_residual = go_ref[...].astype(f32) + (
        scale * weighted - residual * (scale * scale * scale) * inner
    )
    grad_residual_ref[...] = grad_residual
    grad_branch = grad_residual.astype(bf16)
    grad_mix = lax.dot_general(grad_branch, w_ref[...], NT, preferred_element_type=f32)
    grad_c_ref[...] = (grad_mix * conv_ref[...]).astype(bf16)
    grad_conv = grad_mix * gate_c_ref[...]
    grad_conv_ref[...] = grad_conv
    head_ref[0] = grad_conv[:8][:2].astype(bf16)
    total_ref[...] += lax.dot_general(mixer_ref[...], grad_branch, TN, preferred_element_type=f32)

    @pl.when(step == pl.num_programs(0) - 1)
    def _():
        low_ref[...] = total_ref[...].astype(bf16)
        pairs = slot_pairs(own_ref[0], plan, (part_ref,), segments, n_ctx, (low_ref,))
        copy_all([(b, a) for a, b in pairs], sems)


def in_grad_kernel(
    geometry, count, own_ref, grad_conv_ref, behind_ref, before_ref, projected_ref, grad_c_ref,
    normed_ref, taps_ref, grad_projected_ref, grad_taps_ref, *refs
):
    parts, (total_ref, low_ref, sems) = refs[:count], refs[count:]
    plan, segments, n_ctx = geometry
    step = pl.program_id(0)

    @pl.when(step == 0)
    def _():
        total_ref[...] = jnp.zeros_like(total_ref)
        grad_taps_ref[...] = jnp.zeros_like(grad_taps_ref)

    channels = grad_c_ref.shape[1]
    grad_conv = grad_conv_ref[...]
    gate_b = projected_ref[:, :channels]
    values = projected_ref[:, 2 * channels :]
    product = gate_b * values
    one, two = shifted_down(product, before_ref[0].astype(f32))
    for k, shifted in enumerate((two, one, product)):
        grad_taps_ref[k : k + 1] += jnp.sum(grad_conv * shifted, axis=0, keepdims=True)
    one, two = shifted_up(grad_conv, behind_ref[0].astype(f32))
    grad_product = taps_ref[2:3] * grad_conv + taps_ref[1:2] * one + taps_ref[0:1] * two
    grad_projected_ref[:, :channels] = (grad_product * values).astype(bf16)
    grad_projected_ref[:, channels : 2 * channels] = grad_c_ref[...]
    grad_projected_ref[:, 2 * channels :] = (grad_product * gate_b).astype(bf16)
    total_ref[...] += lax.dot_general(
        normed_ref[...], grad_projected_ref[...], TN, preferred_element_type=f32
    )

    @pl.when(step == pl.num_programs(0) - 1)
    def _():
        low_ref[...] = total_ref[...].astype(bf16)
        pairs = slot_pairs(own_ref[0], plan, parts, segments, n_ctx, (low_ref,))
        copy_all([(b, a) for a, b in pairs], sems)


def row_call(body, steps, ins, outs, scratch=()):
    return pl.pallas_call(
        body,
        grid=(steps,),
        in_specs=[
            pl.BlockSpec(memory_space=pltpu.SMEM) if block is None else pl.BlockSpec(block, place)
            for _, block, place in ins
        ],
        out_specs=[
            pl.BlockSpec(memory_space=pl.ANY) if block is None else pl.BlockSpec(block, place)
            for _, _, block, place in outs
        ],
        out_shape=[jax.ShapeDtypeStruct(shape, dtype) for shape, dtype, _, _ in outs],
        scratch_shapes=list(scratch),
        compiler_params=pltpu.CompilerParams(
            vmem_limit_bytes=VMEM_LIMIT, dimension_semantics=("arbitrary",)
        ),
        cost_estimate=SMALL_COST,
    )(*[a for a, _, _ in ins])


def fits(tokens, w_in, w_out, w_gate, w_down, n_dp, n_ctx):
    width, hidden = w_gate.shape
    if n_dp % 2 or n_dp % (2 * n_ctx) or n_dp & (n_dp - 1) or n_ctx & (n_ctx - 1) or n_ctx < 2:
        return False
    depth = width // n_dp
    if width % n_dp or hidden % (n_dp * CHUNKS * 48) or w_in.shape[1] % (2 * n_ctx * 256):
        return False
    lanes = hidden // n_dp // CHUNKS * (n_dp // n_ctx // 2)
    wide = width // n_ctx
    return (
        lanes % 128 == 0
        and wide == lanes + 128
        and lanes == 384
        and wide % 256 == 0
        and depth % 16 == 0
        and 2 * depth <= 256
        and (w_in.shape[1] // n_ctx) % (2 * depth) == 0
        and width % (2 * depth) == 0
        and tokens.shape[1] % n_ctx == 0
        and n_ctx == 2
        and n_dp >= 16
    )


def fast_shards(tokens, w_in, w_out, w_gate, w_up, w_down, gain_mix, gain_ffn, kernel, cotangent):
    seqs, piece, width = tokens.shape
    rows = seqs * piece
    n_chip, n_ctx = lax.axis_size("chip"), lax.axis_size("ctx")
    slots = n_chip * n_ctx
    core = lax.axis_index("core")
    own_slot = lax.axis_index("chip") * n_ctx + lax.axis_index("ctx")
    own = own_slot.astype(jnp.int32)[None]
    depth = w_in.shape[0]
    groups = n_chip // n_ctx
    sub = w_down.shape[0] // CHUNKS
    lanes = groups * sub
    wide = w_out.shape[1]
    in_cols = w_in.shape[1] // 2
    in_parts, out_parts = in_cols // 256, wide // 256
    hidden_count = n_chip * sub
    channels = width // 2

    def mine_other(pair):
        return jnp.where(core == 0, pair[0], pair[1]), jnp.where(core == 0, pair[1], pair[0])

    def in_core_order(mine, other, axis):
        return jnp.where(
            core == 0,
            jnp.concatenate([mine, other], axis=axis),
            jnp.concatenate([other, mine], axis=axis),
        )

    small = jnp.concatenate([gain_mix[None], gain_ffn[None], kernel], axis=0)
    in_pair = w_in.reshape(depth, in_cols // depth, 2, depth).transpose(2, 0, 1, 3)
    in_pair = in_pair.reshape(2, depth, in_parts, 256).transpose(0, 2, 1, 3)
    in_mine, in_other = mine_other(in_pair)
    small_rows = jnp.pad(small, ((0, 11), (0, 256 - depth)))
    swapped = swap(jnp.concatenate([in_other.reshape(in_parts * depth, 256), small_rows], axis=0))
    in_got = swapped[: in_parts * depth].reshape(in_parts, depth, 256)
    in_block = in_core_order(in_mine, in_got, 1).reshape(in_parts * 2 * depth, 256)
    small_block = in_core_order(small, swapped[in_parts * depth :][:5, :depth], 1)
    small_block = jnp.pad(small_block, ((0, 11), (0, 256 - 2 * depth)))
    out_block = w_out.reshape(depth, out_parts, 256).transpose(1, 0, 2).reshape(-1, 256)
    mix_block = jnp.concatenate([in_block, out_block, small_block], axis=0)

    both = jnp.stack([w_gate, w_up]).reshape(2, depth, groups, 2, CHUNKS, sub)
    both = both.transpose(3, 4, 0, 1, 2, 5).reshape(2, CHUNKS, 2, depth, lanes)
    both_mine, both_other = mine_other(both)
    both_block = in_core_order(both_mine, swap(both_other), 2)
    both_block = both_block.reshape(CHUNKS, 4 * depth, lanes)
    down = w_down.reshape(CHUNKS, sub, wide)
    down_rest = down[:, :, lanes:].reshape(CHUNKS, 3, sub // 3, 128).transpose(0, 2, 1, 3)
    chunk_blocks = jnp.concatenate(
        [both_block, down[:, :, :lanes], down_rest.reshape(CHUNKS, sub // 3, lanes)], axis=1
    )

    mix_rows = mix_block.shape[0]
    mix_cut = -(-mix_rows // 32) * 16
    in_rows = in_parts * 2 * depth
    mix_segments = [
        (k * 2 * depth, 2 * depth, 0, 256, 0, 2 * depth, 0, in_cols, 256 * k)
        for k in range(in_parts)
    ]
    def out_segments(base, target):
        return [
            (base + k * depth, depth, 0, 256, target, depth, 0, wide, 256 * k)
            for k in range(out_parts)
        ]

    small_segment = (in_rows + out_parts * depth, 16, 0, 256, 2, 16, 0, 256, 0)
    mix_plan = gather_plan(mix_cut, mix_rows)
    chunk_rows = chunk_blocks.shape[1]
    chunk_cut = chunk_rows // 2
    chunk_segments = [
        (0, 2 * depth, 0, lanes, 0, 2 * depth, 0, lanes, 0),
        (2 * depth, 2 * depth, 0, lanes, 1, 2 * depth, 0, lanes, 0),
        (4 * depth, sub, 0, lanes, 2, sub, 0, wide, 0),
    ] + [
        (4 * depth + sub, sub // 3, 128 * k, 128, 2, sub, k * (sub // 3), wide, lanes)
        for k in range(3)
    ]
    whole_plan = [(0, i, None, 0, chunk_rows) for i in range(slots)]
    whole_geometry = (whole_plan, chunk_segments, n_ctx)
    step_geometry = (gather_plan(chunk_cut, chunk_rows), chunk_segments, n_ctx)

    token_rows = tokens.reshape(rows, width)
    inputs = jnp.concatenate([token_rows, swap(token_rows)], axis=0)
    go_rows = cotangent.reshape(rows, width)
    go = jnp.concatenate([go_rows, swap(go_rows)], axis=0)

    far, first_order, second_order = bit_masks()
    orders = (first_order, second_order)

    def doubled(hold, got):
        return jnp.concatenate([hold, got], axis=0)

    hold = mix_block[None]
    for mask in far:
        hold = doubled(hold, across(hold, mask))
    mix_halves = [hold[:, :mix_cut], hold[:, mix_cut:]]
    next_hold = after(chunk_blocks[0][None], hold)
    far_left = list(far)
    early = [inputs, go]
    for step in range(len(first_order)):
        got = [across(h, order[step]) for h, order in zip(mix_halves, orders)]
        if far_left:
            next_got = across(next_hold, far_left.pop(0))
            next_hold = doubled(next_hold, next_got)
        if early:
            got = [after(g, early[0]) for g in got]
            early = early[1:]
        if step + 1 < len(first_order):
            got = [after(g, next_got) for g in got]
            mix_halves = [doubled(h, g) for h, g in zip(mix_halves, got)]
            next_hold = after(next_hold, *got)
    mix_parts = [mix_halves[0], got[0], mix_halves[1], got[1]]
    for mask in far_left:
        next_got = across(next_hold, mask)
        next_hold = doubled(next_hold, next_got)
    in_half, out_half, small_all = move(
        own,
        mix_parts,
        [(width, n_ctx * in_cols), (channels, width), (n_chip * 16, n_ctx * 256)],
        (mix_plan, mix_segments + out_segments(in_rows, 1) + [small_segment], n_ctx),
        4,
        False,
    )
    in_half = after(in_half, next_got)
    second_all, last_all = [
        lax.all_gather(after(block, next_got), ("chip", "ctx")) for block in chunk_blocks[1:]
    ]
    next_halves = [next_hold[:, :chunk_cut], next_hold[:, chunk_cut:]]

    def step_of(halves, step):
        return [across(h, order[step]) for h, order in zip(halves, orders)]

    def all_after(blocks, *done):
        return [after(block, *done) for block in blocks]

    small_all = small_all.reshape(n_chip, 16, n_ctx * 256)[:, :5, : 2 * depth].astype(f32)
    first_gain = small_all[:, 0].reshape(width)
    second_gain = small_all[:, 1].reshape(width)
    taps = small_all[:, 2:].reshape(n_chip, 3, 2, depth)
    taps = jnp.where(core == 0, taps[:, :, 0], taps[:, :, 1]).transpose(1, 0, 2)
    taps = taps.reshape(3, channels)

    blocks = 2 * seqs

    def at(i):
        return (i, 0)

    def still(i):
        return (0, 0)

    def other(i):
        return ((i + seqs) % blocks, 0)

    wide_rows, thin_rows = (piece, width), (piece, channels)
    taps = jnp.pad(taps, ((0, 5), (0, 0)))
    next_got = step_of(next_halves, 0)
    halo = (1, 2, channels)

    def halo_at(i):
        return (i, 0, 0)

    normed_low, projected, tail = row_call(
        in_kernel,
        blocks,
        [
            (inputs, wide_rows, at),
            (first_gain[None], (1, width), still),
            (in_half, in_half.shape, still),
        ],
        [
            ((2 * rows, width), bf16, wide_rows, at),
            ((2 * rows, 3 * channels), f32, (piece, 3 * channels), at),
            ((blocks, 2, channels), bf16, (1, 2, channels), halo_at),
        ],
    )
    before = passed_along(tail, "ctx", 1)
    conv_taps = after(taps, *next_got)
    next_halves = [
        doubled(h, g) for h, g in zip(next_halves, all_after(next_got, projected))
    ]
    next_got = step_of(next_halves, 1)
    mixer_out, convolved, branch = row_call(
        conv_kernel,
        blocks,
        [
            (projected, (piece, 3 * channels), at),
            (before, halo, halo_at),
            (conv_taps, taps.shape, still),
            (out_half, out_half.shape, still),
        ],
        [
            ((2 * rows, channels), bf16, thin_rows, at),
            ((2 * rows, channels), f32, thin_rows, at),
            ((2 * rows, width), bf16, wide_rows, at),
        ],
    )
    residual, nffn_low = row_call(
        norm_kernel,
        blocks,
        [
            (inputs, wide_rows, at),
            (branch, wide_rows, at),
            (swap(branch), wide_rows, other),
            (second_gain[None], (1, width), still),
        ],
        [((2 * rows, width), f32, wide_rows, at), ((2 * rows, width), bf16, wide_rows, at)],
    )

    next_parts = [next_halves[0], next_got[0], next_halves[1], next_got[1]]
    next_parts = all_after(next_parts, nffn_low)

    totals, first_grads = ffn_chunk(
        own, nffn_low, go, next_parts, None, step_geometry, step_geometry, hidden_count
    )
    first_stages = Stages(first_grads)
    totals, second_grads = ffn_chunk(
        own, nffn_low, go, [second_all], totals, whole_geometry, step_geometry, hidden_count
    )
    second_stages = Stages(second_grads)
    nffn_then = after(nffn_low, *first_stages.got)
    first_stages.advance(totals[1])
    totals, last_grads = ffn_chunk(
        own, nffn_then, go, [last_all], totals, whole_geometry, step_geometry, hidden_count, last=True
    )
    ffn_out, grad_low = totals
    last_stages = Stages(last_grads)
    grad_got = swap(after(grad_low, *first_stages.got, *second_stages.got))
    first_stages.advance(grad_low)
    second_stages.advance(grad_low)

    def turned(i):
        return ((i + seqs) % blocks, 0)

    def turned_back(i):
        return (i, 0)

    def own_place(i):
        return (jnp.maximum(i - seqs, 0), 0)

    def gate_c_place(i):
        return ((i + seqs) % blocks, 1)

    out_plan = [(0, i, None, 0, out_parts * depth) for i in range(slots)]
    grad_residual, grad_conv, grad_c, grad_gain_ffn, head, grad_out_slots = row_call(
        functools.partial(branch_grad_kernel, seqs, (out_plan, out_segments(0, 0), n_ctx)),
        blocks,
        [
            (own, None, None),
            (grad_low, wide_rows, turned),
            (grad_got, wide_rows, turned_back),
            (residual, wide_rows, turned),
            (go, wide_rows, turned),
            (second_gain[None], (1, width), still),
            (mixer_out, thin_rows, turned),
            (convolved, thin_rows, turned),
            (projected, thin_rows, gate_c_place),
            (out_half, out_half.shape, still),
        ],
        [
            ((rows, width), f32, wide_rows, own_place),
            ((2 * rows, channels), f32, thin_rows, turned),
            ((2 * rows, channels), bf16, thin_rows, turned),
            ((1, width), f32, (1, width), still),
            ((blocks, 2, channels), bf16, halo, lambda i: ((i + seqs) % blocks, 0, 0)),
            ((slots, out_parts * depth, 256), bf16, None, None),
        ],
        scratch=[
            pltpu.VMEM((channels, width), f32),
            pltpu.VMEM((channels, width), bf16),
            pltpu.SemaphoreType.DMA((slots * out_parts,)),
        ],
    )
    grad_gain_ffn = grad_gain_ffn[0]
    stages = (first_stages, second_stages, last_stages)
    behind = passed_along(head, "ctx", -1)
    grad_c_then = after(grad_c, *second_stages.got, *last_stages.got)
    second_stages.advance(grad_c)
    last_stages.advance(grad_c)
    out_sum = lax.psum_scatter(grad_out_slots, ("chip", "ctx"), scatter_dimension=0).astype(f32)
    sum_plan = gather_plan(in_rows // 2, in_rows)
    grad_projected, grad_kernel, *mix_grad_parts = row_call(
        functools.partial(in_grad_kernel, (sum_plan, mix_segments, n_ctx), 4),
        blocks,
        [
            (own, None, None),
            (grad_conv, thin_rows, at),
            (behind, halo, halo_at),
            (before, halo, halo_at),
            (projected, (piece, 3 * channels), at),
            (grad_c_then, thin_rows, at),
            (normed_low, wide_rows, at),
            (taps, taps.shape, still),
        ],
        [
            ((2 * rows, 3 * channels), bf16, (piece, 3 * channels), at),
            ((8, channels), f32, (8, channels), still),
        ]
        + [(shape, bf16, None, None) for shape in part_shapes(sum_plan, 256)],
        scratch=[
            pltpu.VMEM((width, 3 * channels), f32),
            pltpu.VMEM((width, 3 * channels), bf16),
            pltpu.SemaphoreType.DMA((len(sum_plan) * len(mix_segments),)),
        ],
    )
    grad_kernel = grad_kernel[:3]
    mix_stages = Stages(mix_grad_parts)
    stages = (first_stages, second_stages, last_stages)
    for s in stages:
        s.advance(grad_projected)
    late_projected = after(grad_projected, *mix_stages.got)
    mix_stages.advance()
    grad_other = cross_cols(late_projected[rows:], in_half).astype(bf16)
    for s in (mix_stages, *stages):
        s.advance(grad_other)
    other_got = swap(grad_other)
    grad_mine = cross_cols(after(late_projected, grad_other)[:rows], in_half)
    for s in stages:
        s.advance(grad_mine)
    grad_normed = grad_mine + other_got.astype(f32)
    ffn_late = after(ffn_out, grad_other)
    ffn_got = swap(ffn_late[rows:].astype(bf16))
    result = after(residual, grad_mine)[:rows] + (ffn_late[:rows] + ffn_got.astype(f32))
    result = result.astype(bf16).reshape(seqs, piece, width)
    own_inputs = token_rows.astype(f32)
    scale_mix = lax.rsqrt(jnp.mean(own_inputs * own_inputs, axis=-1, keepdims=True) + EPSILON)
    grad_in_norm, grad_gain_mix = norm_backward(own_inputs, scale_mix, first_gain, grad_normed)
    grad_tokens = (grad_residual + grad_in_norm).reshape(seqs, piece, width)

    mix_stages.advance(grad_mine)

    chunk_sum = jnp.stack([s.total for s in stages])
    both_sum = chunk_sum[:, : 4 * depth].reshape(CHUNKS, 2, 2, depth, lanes).transpose(2, 0, 1, 3, 4)
    both_mine, both_other = mine_other(both_sum)
    both_got = swap(both_other)
    both_sum = in_core_order(both_mine[None], both_got[None], 0)
    both_sum = both_sum.reshape(2, CHUNKS, 2, depth, groups, sub).transpose(2, 3, 4, 0, 1, 5)
    both_sum = both_sum.reshape(2, depth, 2 * CHUNKS * lanes)
    down_rest = chunk_sum[:, 4 * depth + sub :].reshape(CHUNKS, sub // 3, 3, 128)
    down_rest = down_rest.transpose(0, 2, 1, 3).reshape(CHUNKS, sub, 128)
    final_down = jnp.concatenate([chunk_sum[:, 4 * depth : 4 * depth + sub], down_rest], axis=2)
    final_down = final_down.reshape(CHUNKS * sub, wide)

    mix_stages.advance(both_sum, final_down)
    in_sum = mix_stages.total.reshape(in_parts, 2, depth, 256).transpose(1, 0, 2, 3)
    in_mine, in_other = mine_other(in_sum)
    in_sum = in_core_order(in_mine[None], swap(in_other)[None], 0)
    in_sum = in_sum.transpose(0, 2, 1, 3).reshape(2, depth, in_cols // depth, depth)
    final_in = in_sum.transpose(1, 2, 0, 3).reshape(depth, 2 * in_cols)
    final_out = out_sum.reshape(out_parts, depth, 256).transpose(1, 0, 2)
    final_out = final_out.reshape(depth, wide)

    grad_taps = grad_kernel.reshape(3, n_chip, 1, depth)
    grad_taps = jnp.where(
        jnp.arange(2).reshape(1, 1, 2, 1) == core, grad_taps, jnp.zeros_like(grad_taps)
    ).reshape(3, width)
    small_grad = jnp.concatenate([grad_gain_mix[None], grad_gain_ffn[None], grad_taps], axis=0)
    small_sum = small_grad.reshape(5, n_chip, 2 * depth).transpose(1, 0, 2)
    for bit in range(n_ctx.bit_length() - 1):
        small_sum = small_sum + across(small_sum, 1 << bit)
    for bit in range(n_chip.bit_length() - 1):
        mask = n_chip >> (bit + 1)
        low, high = small_sum[: small_sum.shape[0] // 2], small_sum[small_sum.shape[0] // 2 :]
        upper = jnp.bitwise_and(lax.axis_index("chip"), mask) != 0
        small_sum = jnp.where(upper, high, low) + across(jnp.where(upper, low, high), mask * n_ctx)
    small_mine, small_other = mine_other(small_sum[0].reshape(5, 2, depth).transpose(1, 0, 2))
    small_sum = small_mine + swap(small_other)
    return (
        result,
        grad_tokens,
        final_in,
        final_out,
        both_sum[0],
        both_sum[1],
        final_down,
        small_sum[0],
        small_sum[1],
        small_sum[2:5],
    )


def solution(mesh):
    n_dp, n_ctx = mesh.shape["dp"], mesh.shape["ctx"]

    def placed(dp):
        whole, cut = P(dp, "ctx", None), P(dp, "ctx")
        ins = (whole, cut, cut, cut, cut, cut, P(dp), P(dp), P(None, dp), whole)
        outs = (whole, whole, cut, cut, cut, cut, cut, P(dp), P(dp), P(None, dp))
        return ins, outs

    def run(tokens, w_in, w_out, w_gate, w_up, w_down, gain_mix, gain_ffn, kernel, cotangent):
        if fits(tokens, w_in, w_out, w_gate, w_down, n_dp, n_ctx):
            cut_mesh = Mesh(mesh.devices.reshape(n_dp // 2, 2, n_ctx), ("chip", "core", "ctx"))
            body, on, (ins, outs) = fast_shards, cut_mesh, placed(("chip", "core"))
        else:
            body, on, (ins, outs) = plain_shards, mesh, placed("dp")
        call = jax.shard_map(body, mesh=on, in_specs=ins, out_specs=outs, check_vma=False)
        return call(
            tokens, w_in, w_out, w_gate, w_up, w_down, gain_mix, gain_ffn, kernel, cotangent
        )

    return run
```

```python
import functools
import jax
import jax.numpy as jnp
from jax import lax
from jax.experimental import pallas as pl
from jax.experimental.pallas import tpu as pltpu
from jax.sharding import Mesh
from jax.sharding import PartitionSpec as P

EPSILON = 1e-05
CHUNKS = 3
f32 = jnp.float32
bf16 = jnp.bfloat16


def passed_along(block, axis, distance):
    devices = range(lax.axis_size(axis))
    route = [(i - distance, i) for i in devices if i - distance in devices]
    return lax.ppermute(block, axis, route)


def cross_rows(left_operand, right_operand):
    return lax.dot_general(
        left_operand, right_operand, (((0,), (0,)), ((), ())), preferred_element_type=jnp.float32
    )


def cross_cols(left_operand, right_operand):
    return lax.dot_general(
        left_operand, right_operand, (((1,), (1,)), ((), ())), preferred_element_type=jnp.float32
    )


def norm_forward(values, gain):
    scale = lax.rsqrt(jnp.mean(values * values, axis=-1, keepdims=True) + EPSILON)
    return (values * scale * gain, scale)


def norm_backward(values, scale, gain, incoming):
    weighted = incoming * gain
    gain_grad = jnp.sum(incoming * values * scale, axis=0)
    inner = jnp.mean(weighted * values, axis=-1, keepdims=True)
    return (scale * weighted - values * (scale * scale * scale) * inner, gain_grad)


def plain_shards(tokens, w_in, w_out, w_gate, w_up, w_down, gain_mix, gain_ffn, kernel, cotangent):
    seq_count, piece_len, model_width = tokens.shape
    row_count = seq_count * piece_len
    small_params = jnp.concatenate([gain_mix[None], gain_ffn[None], kernel], axis=0)
    input_columns, out_cols, gate_cols, up_cols, down_cols = (
        lax.all_gather(w_in, "ctx", axis=1, tiled=True),
        lax.all_gather(w_out, "ctx", axis=1, tiled=True),
        lax.all_gather(w_gate, "ctx", axis=1, tiled=True),
        lax.all_gather(w_up, "ctx", axis=1, tiled=True),
        lax.all_gather(w_down, "ctx", axis=1, tiled=True),
    )
    full_in, full_out, full_gate, full_up, full_down, small_full = (
        lax.all_gather(input_columns, "dp", axis=0, tiled=True),
        lax.all_gather(out_cols, "dp", axis=0, tiled=True),
        lax.all_gather(gate_cols, "dp", axis=0, tiled=True),
        lax.all_gather(up_cols, "dp", axis=0, tiled=True),
        lax.all_gather(down_cols, "dp", axis=0, tiled=True),
        lax.all_gather(small_params, "dp", axis=1, tiled=True),
    )
    small_float = small_full.astype(jnp.float32)
    first_gain = small_float[0]
    second_gain = small_float[1]
    taps = small_float[2:5]
    inputs = tokens.reshape(row_count, model_width).astype(jnp.float32)
    normed, scale_mix = norm_forward(inputs, first_gain)
    normed_low = normed.astype(jnp.bfloat16)
    projected = jnp.dot(normed_low, full_in, preferred_element_type=jnp.float32)
    gate_b = projected[:, :model_width]
    gate_c = projected[:, model_width : 2 * model_width]
    values = projected[:, 2 * model_width :]
    product = (gate_b * values).reshape(seq_count, piece_len, model_width)
    previous = passed_along(product[:, piece_len - 2 :].astype(jnp.bfloat16), "ctx", 1).astype(
        jnp.float32
    )
    padded = jnp.concatenate([previous, product], axis=1)
    convolved = taps[0] * padded[:, :-2] + taps[1] * padded[:, 1:-1] + taps[2] * padded[:, 2:]
    convolved = convolved.reshape(row_count, model_width)
    mixer_out = (gate_c * convolved).astype(jnp.bfloat16)
    residual = inputs + jnp.dot(mixer_out, full_out, preferred_element_type=jnp.float32)
    feedforward_normed, scale_ffn = norm_forward(residual, second_gain)
    nffn_low = feedforward_normed.astype(jnp.bfloat16)
    gate = jnp.dot(nffn_low, full_gate, preferred_element_type=jnp.float32)
    up_value = jnp.dot(nffn_low, full_up, preferred_element_type=jnp.float32)
    sigmoid_gate = jax.nn.sigmoid(gate)
    activated = gate * sigmoid_gate
    hidden = (activated * up_value).astype(jnp.bfloat16)
    result = residual + jnp.dot(hidden, full_down, preferred_element_type=jnp.float32)
    result = result.astype(jnp.bfloat16).reshape(seq_count, piece_len, model_width)
    back_in, output_backward, back_gate, back_up, back_down = (
        lax.all_gather(w_in, "ctx", axis=1, tiled=True),
        lax.all_gather(w_out, "ctx", axis=1, tiled=True),
        lax.all_gather(w_gate, "ctx", axis=1, tiled=True),
        lax.all_gather(w_up, "ctx", axis=1, tiled=True),
        lax.all_gather(w_down, "ctx", axis=1, tiled=True),
    )
    input_weight_used, use_out, use_gate, use_up, use_down = (
        lax.all_gather(back_in, "dp", axis=0, tiled=True),
        lax.all_gather(output_backward, "dp", axis=0, tiled=True),
        lax.all_gather(back_gate, "dp", axis=0, tiled=True),
        lax.all_gather(back_up, "dp", axis=0, tiled=True),
        lax.all_gather(back_down, "dp", axis=0, tiled=True),
    )
    grad_out = cotangent.reshape(row_count, model_width)
    grad_out_float = grad_out.astype(jnp.float32)
    grad_w_down = cross_rows(hidden, grad_out)
    grad_hidden = cross_cols(grad_out, use_down)
    grad_gate = (
        grad_hidden * up_value * sigmoid_gate * (1.0 + gate * (1.0 - sigmoid_gate))
    ).astype(jnp.bfloat16)
    grad_up = (grad_hidden * activated).astype(jnp.bfloat16)
    grad_w_gate = cross_rows(nffn_low, grad_gate)
    grad_w_up = cross_rows(nffn_low, grad_up)
    grad_nffn = cross_cols(grad_gate, use_gate) + cross_cols(grad_up, use_up)
    residual_norm_gradient, grad_gain_ffn = norm_backward(
        residual, scale_ffn, second_gain, grad_nffn
    )
    grad_residual = grad_out_float + residual_norm_gradient
    grad_branch = grad_residual.astype(jnp.bfloat16)
    grad_w_out = cross_rows(mixer_out, grad_branch)
    grad_mix = cross_cols(grad_branch, use_out)
    grad_c = grad_mix * convolved
    grad_conv = (grad_mix * gate_c).reshape(seq_count, piece_len, model_width)
    following = passed_along(grad_conv[:, :2].astype(jnp.bfloat16), "ctx", -1).astype(jnp.float32)
    extended = jnp.concatenate([grad_conv, following], axis=1)
    grad_product = (
        taps[2] * extended[:, :-2] + taps[1] * extended[:, 1:-1] + taps[0] * extended[:, 2:]
    )
    grad_kernel = jnp.stack(
        [
            jnp.sum(grad_conv * padded[:, shift_at : shift_at + piece_len], axis=(0, 1))
            for shift_at in range(3)
        ],
        axis=0,
    )
    grad_product = grad_product.reshape(row_count, model_width)
    grad_projected = jnp.concatenate(
        [grad_product * values, grad_c, grad_product * gate_b], axis=1
    ).astype(jnp.bfloat16)
    grad_w_in = cross_rows(normed_low, grad_projected)
    grad_normed = cross_cols(grad_projected, input_weight_used)
    grad_in_norm, grad_gain_mix = norm_backward(inputs, scale_mix, first_gain, grad_normed)
    grad_tokens = (grad_residual + grad_in_norm).reshape(seq_count, piece_len, model_width)
    small_grad = jnp.concatenate([grad_gain_mix[None], grad_gain_ffn[None], grad_kernel], axis=0)
    part_in, part_out, part_gate, part_up, part_down, small_part = (
        lax.psum_scatter(grad_w_in, "dp", scatter_dimension=0, tiled=True),
        lax.psum_scatter(grad_w_out, "dp", scatter_dimension=0, tiled=True),
        lax.psum_scatter(grad_w_gate, "dp", scatter_dimension=0, tiled=True),
        lax.psum_scatter(grad_w_up, "dp", scatter_dimension=0, tiled=True),
        lax.psum_scatter(grad_w_down, "dp", scatter_dimension=0, tiled=True),
        lax.psum_scatter(small_grad, "dp", scatter_dimension=1, tiled=True),
    )
    final_in, final_out, final_gate, final_up, final_down = (
        lax.psum_scatter(part_in, "ctx", scatter_dimension=1, tiled=True),
        lax.psum_scatter(part_out, "ctx", scatter_dimension=1, tiled=True),
        lax.psum_scatter(part_gate, "ctx", scatter_dimension=1, tiled=True),
        lax.psum_scatter(part_up, "ctx", scatter_dimension=1, tiled=True),
        lax.psum_scatter(part_down, "ctx", scatter_dimension=1, tiled=True),
    )
    small_total = lax.psum(small_part, "ctx")
    return (
        result,
        grad_tokens,
        final_in,
        final_out,
        final_gate,
        final_up,
        final_down,
        small_total[0],
        small_total[1],
        small_total[2:5],
    )


SMALL_COST = pl.CostEstimate(flops=1 << 16, bytes_accessed=1 << 16, transcendentals=0)
VMEM_LIMIT = 60 * 1024 * 1024
NT = (((1,), (1,)), ((), ()))
TN = (((0,), (0,)), ((), ()))


def swap(block):
    return lax.ppermute(block, "core", [(0, 1), (1, 0)])


def across(block, mask):
    count = lax.axis_size("chip") * lax.axis_size("ctx")
    return lax.ppermute(block, ("chip", "ctx"), [(i, i ^ mask) for i in range(count)])


def bit_masks():
    n_chip, n_ctx = lax.axis_size("chip"), lax.axis_size("ctx")
    ctx_bits = [1 << b for b in range(n_ctx.bit_length() - 1)]
    near = [n_ctx]
    far = [n_ctx << b for b in range(1, n_chip.bit_length() - 1)]
    return far, near + ctx_bits, ctx_bits + near


def after(value, *done):
    return lax.optimization_barrier((value, *done))[0]


def gather_plan(cut, total):
    far, first_order, second_order = bit_masks()
    plan = []
    for operand, order, row0, rows in ((0, first_order, 0, cut), (2, second_order, cut, total - cut)):
        masks = [0]
        for mask in far + order[:-1]:
            masks = masks + [m ^ mask for m in masks]
        for index, mask in enumerate(masks):
            plan.append((operand, index, mask, row0, rows))
            plan.append((operand + 1, index, mask ^ order[-1], row0, rows))
    return plan


def gather(block, cut):
    far, first_order, second_order = bit_masks()
    hold = block[None]
    for mask in far:
        hold = jnp.concatenate([hold, across(hold, mask)], axis=0)
    parts = []
    for order, half in ((first_order, hold[:, :cut]), (second_order, hold[:, cut:])):
        for mask in order[:-1]:
            half = jnp.concatenate([half, across(half, mask)], axis=0)
        parts += [half, across(half, order[-1])]
    return parts


def scatter_steps(parts):
    far, first_order, second_order = bit_masks()

    def send(block, mask):
        block = block.astype(bf16)
        return across(block, mask), block

    orders = (first_order, second_order)
    got = yield [send(parts[1], first_order[-1]), send(parts[3], second_order[-1])]
    keeps = [k.astype(f32) + g.astype(f32) for k, g in zip((parts[0], parts[2]), got)]
    for step in range(len(first_order) - 2, -1, -1):
        mid = keeps[0].shape[0] // 2
        got = yield [send(k[mid:], order[step]) for k, order in zip(keeps, orders)]
        keeps = [k[:mid] + g.astype(f32) for k, g in zip(keeps, got)]
    keep = jnp.concatenate(keeps, axis=1)
    for mask in reversed(far):
        mid = keep.shape[0] // 2
        (got,) = yield [send(keep[mid:], mask)]
        keep = keep[:mid] + got.astype(f32)
    return keep[0]


class Stages:
    def __init__(self, parts):
        self.steps = scatter_steps(parts)
        self.got, self.sent = zip(*next(self.steps))
        self.total = None

    def advance(self, *done):
        if self.total is not None:
            return
        try:
            pairs = self.steps.send([after(g, *done) for g in self.got])
            self.got, self.sent = zip(*pairs)
        except StopIteration as end:
            self.got, self.sent, self.total = (), (), end.value


def slot_pairs(own, plan, refs, segments, n_ctx, targets):
    pairs = []
    for operand, index, mask, row0, nrows in plan:
        slot = index if mask is None else jnp.bitwise_xor(own, mask)
        y = lax.rem(slot, n_ctx)
        chip = lax.div(slot, n_ctx)
        src = refs[operand].at[index]
        for seg_row, seg_rows, lane0, lanes, target, row_step, row_add, lane_step, lane_add in segments:
            low, high = max(seg_row, row0), min(seg_row + seg_rows, row0 + nrows)
            if low >= high:
                continue
            row = pl.multiple_of(chip * row_step + row_add + (low - seg_row), 16)
            lane = pl.multiple_of(y * lane_step + lane_add, 128)
            pairs.append(
                (
                    src.at[pl.ds(low - row0, high - low), pl.ds(lane0, lanes)],
                    targets[target].at[pl.ds(row, high - low), pl.ds(lane, lanes)],
                )
            )
    return pairs


def copy_all(pairs, sems):
    copies = [pltpu.make_async_copy(a, b, sems.at[i]) for i, (a, b) in enumerate(pairs)]
    for copy in copies:
        copy.start()
    for copy in copies:
        copy.wait()


def part_count(plan):
    return 1 + max(entry[0] for entry in plan)


def part_shapes(plan, lanes):
    shapes = {}
    for operand, index, _, _, rows in plan:
        shapes[operand] = (max(index + 1, shapes.get(operand, (0,))[0]), rows, lanes)
    return [shapes[operand] for operand in sorted(shapes)]


def ffn_kernel(geometry, out_geometry, first, own_ref, n_ref, go_ref, *refs):
    plan, segments, n_ctx = geometry
    out_plan = out_geometry[0]
    count, out_count = part_count(plan), part_count(out_plan)
    weights, refs = refs[:count], refs[count:]
    if not first:
        res_in, gn_in = refs[:2]
        refs = refs[2:]
    res_ref, gn_ref = refs[:2]
    refs = refs[2:]
    grads, refs = refs[:out_count], refs[out_count:]
    gate_m, up_m, down_m, d_gate, d_up, d_down, h_m, gg_m, gu_m, sems = refs
    own = own_ref[0]
    targets = (gate_m, up_m, down_m)

    @pl.when(pl.program_id(0) == 0)
    def _():
        d_gate[...] = jnp.zeros_like(d_gate)
        d_up[...] = jnp.zeros_like(d_up)
        d_down[...] = jnp.zeros_like(d_down)
        copy_all(slot_pairs(own, plan, weights, segments, n_ctx, targets), sems)

    n = n_ref[...]
    go = go_ref[...]
    hidden_count = gate_m.shape[1]
    step = 256
    for start in range(0, hidden_count, step):
        cols = slice(start, start + step)
        g = jnp.dot(n, gate_m[:, cols], preferred_element_type=f32)
        u = jnp.dot(n, up_m[:, cols], preferred_element_type=f32)
        gh = lax.dot_general(go, down_m[cols, :], NT, preferred_element_type=f32)
        s = jax.nn.sigmoid(g)
        act = g * s
        h_m[:, cols] = (act * u).astype(bf16)
        gg_m[:, cols] = (gh * u * s * (1.0 + g * (1.0 - s))).astype(bf16)
        gu_m[:, cols] = (gh * act).astype(bf16)
    res = jnp.dot(h_m[...], down_m[...], preferred_element_type=f32)
    gn = lax.dot_general(gg_m[...], gate_m[...], NT, preferred_element_type=f32)
    gn = gn + lax.dot_general(gu_m[...], up_m[...], NT, preferred_element_type=f32)
    if not first:
        res = res_in[...] + res
        gn = gn_in[...] + gn
    res_ref[...] = res
    gn_ref[...] = gn.astype(gn_ref.dtype)
    d_gate[...] += lax.dot_general(n, gg_m[...], TN, preferred_element_type=f32)
    d_up[...] += lax.dot_general(n, gu_m[...], TN, preferred_element_type=f32)
    d_down[...] += lax.dot_general(h_m[...], go, TN, preferred_element_type=f32)

    @pl.when(pl.program_id(0) == pl.num_programs(0) - 1)
    def _():
        gate_m[...] = d_gate[...].astype(bf16)
        up_m[...] = d_up[...].astype(bf16)
        down_m[...] = d_down[...].astype(bf16)
        pairs = slot_pairs(own, out_plan, grads, segments, n_ctx, targets)
        copy_all([(b, a) for a, b in pairs], sems)


def ffn_chunk(
    own, nffn, go, weights, totals, geometry, out_geometry, hidden_count, last=False, rows=256
):
    total, width = nffn.shape
    first = totals is None
    plan, segments, _ = geometry
    out_plan = out_geometry[0]
    count, out_count = part_count(plan), part_count(out_plan)
    lanes = weights[0].shape[-1]
    row_spec = pl.BlockSpec((rows, width), lambda i, o: (i, 0))
    any_spec = pl.BlockSpec(memory_space=pl.ANY)
    outs = pl.pallas_call(
        functools.partial(ffn_kernel, geometry, out_geometry, first),
        out_shape=[jax.ShapeDtypeStruct((total, width), d) for d in (f32, bf16 if last else f32)]
        + [jax.ShapeDtypeStruct(s, bf16) for s in part_shapes(out_plan, lanes)],
        grid_spec=pltpu.PrefetchScalarGridSpec(
            num_scalar_prefetch=1,
            grid=(total // rows,),
            in_specs=[row_spec] * 2 + [any_spec] * count + [row_spec] * (0 if first else 2),
            out_specs=[row_spec] * 2 + [any_spec] * out_count,
            scratch_shapes=[
                pltpu.VMEM((width, hidden_count), bf16),
                pltpu.VMEM((width, hidden_count), bf16),
                pltpu.VMEM((hidden_count, width), bf16),
                pltpu.VMEM((width, hidden_count), f32),
                pltpu.VMEM((width, hidden_count), f32),
                pltpu.VMEM((hidden_count, width), f32),
                pltpu.VMEM((rows, hidden_count), bf16),
                pltpu.VMEM((rows, hidden_count), bf16),
                pltpu.VMEM((rows, hidden_count), bf16),
                pltpu.SemaphoreType.DMA((max(len(plan), len(out_plan)) * len(segments),)),
            ],
        ),
        input_output_aliases={} if first else {3 + count: 0} if last else {3 + count: 0, 4 + count: 1},
        compiler_params=pltpu.CompilerParams(
            vmem_limit_bytes=VMEM_LIMIT, dimension_semantics=("arbitrary",)
        ),
        cost_estimate=SMALL_COST,
    )(own, nffn, go, *weights, *(() if first else totals))
    return outs[:2], outs[2:]


def move_kernel(geometry, count, outward, own_ref, *refs):
    plan, segments, n_ctx = geometry
    sems = refs[-1]
    refs = refs[:-1]
    if outward:
        targets, parts = refs[: len(refs) - count], refs[len(refs) - count :]
    else:
        parts, targets = refs[:count], refs[count:]
    pairs = slot_pairs(own_ref[0], plan, parts, segments, n_ctx, targets)
    copy_all([(b, a) for a, b in pairs] if outward else pairs, sems)


def move(own, arrays, shapes, geometry, count, outward):
    plan, segments, _ = geometry
    any_spec = pl.BlockSpec(memory_space=pl.ANY)
    vmem_spec = pl.BlockSpec(memory_space=pltpu.VMEM)
    return pl.pallas_call(
        functools.partial(move_kernel, geometry, count, outward),
        out_shape=[jax.ShapeDtypeStruct(s, bf16) for s in shapes],
        in_specs=[pl.BlockSpec(memory_space=pltpu.SMEM)]
        + [vmem_spec if outward else any_spec] * len(arrays),
        out_specs=[any_spec if outward else vmem_spec] * len(shapes),
        scratch_shapes=[pltpu.SemaphoreType.DMA((len(plan) * len(segments),))],
        compiler_params=pltpu.CompilerParams(vmem_limit_bytes=VMEM_LIMIT),
        cost_estimate=SMALL_COST,
    )(own, *arrays)


def shifted_down(block, before):
    row = lax.broadcasted_iota(jnp.int32, block.shape, 0)
    one = jnp.where(row == 0, before[1:2], pltpu.roll(block, 1, 0))
    two = jnp.where(row == 0, before[0:1], pltpu.roll(block, 2, 0))
    return one, jnp.where(row == 1, before[1:2], two)


def shifted_up(block, behind):
    count = block.shape[0]
    row = lax.broadcasted_iota(jnp.int32, block.shape, 0)
    one = jnp.where(row == count - 1, behind[0:1], pltpu.roll(block, count - 1, 0))
    two = jnp.where(row == count - 2, behind[0:1], pltpu.roll(block, count - 2, 0))
    return one, jnp.where(row == count - 1, behind[1:2], two)


def in_kernel(x_ref, gain_ref, w_ref, normed_ref, projected_ref, tail_ref):
    x = x_ref[...].astype(f32)
    scale = lax.rsqrt(jnp.mean(x * x, axis=-1, keepdims=True) + EPSILON)
    normed = (x * scale * gain_ref[...]).astype(bf16)
    normed_ref[...] = normed
    projected = jnp.dot(normed, w_ref[...], preferred_element_type=f32)
    projected_ref[...] = projected
    channels = projected.shape[1] // 3
    product = projected[-8:, :channels] * projected[-8:, 2 * channels :]
    tail_ref[0] = product[6:].astype(bf16)


def conv_kernel(projected_ref, before_ref, taps_ref, w_ref, mixer_ref, conv_ref, branch_ref):
    channels = conv_ref.shape[1]
    product = projected_ref[:, :channels] * projected_ref[:, 2 * channels :]
    one, two = shifted_down(product, before_ref[0].astype(f32))
    conv = taps_ref[0:1] * two + taps_ref[1:2] * one + taps_ref[2:3] * product
    conv_ref[...] = conv
    mixer = (projected_ref[:, channels : 2 * channels] * conv).astype(bf16)
    mixer_ref[...] = mixer
    branch_ref[...] = jnp.dot(mixer, w_ref[...], preferred_element_type=f32).astype(bf16)


def norm_kernel(x_ref, branch_ref, got_ref, gain_ref, residual_ref, normed_ref):
    residual = x_ref[...].astype(f32) + (branch_ref[...].astype(f32) + got_ref[...].astype(f32))
    residual_ref[...] = residual
    scale = lax.rsqrt(jnp.mean(residual * residual, axis=-1, keepdims=True) + EPSILON)
    normed_ref[...] = (residual * scale * gain_ref[...]).astype(bf16)


def branch_grad_kernel(
    own_first, geometry, own_ref, gn_ref, got_ref, residual_ref, go_ref, gain_ref, mixer_ref,
    conv_ref, gate_c_ref, w_ref, grad_residual_ref, grad_conv_ref, grad_c_ref, grad_gain_ref,
    head_ref, part_ref, total_ref, low_ref, sems,
):
    plan, segments, n_ctx = geometry
    step = pl.program_id(0)

    @pl.when(step == 0)
    def _():
        total_ref[...] = jnp.zeros_like(total_ref)
        grad_gain_ref[...] = jnp.zeros_like(grad_gain_ref)

    incoming = gn_ref[...].astype(f32) + got_ref[...].astype(f32)
    residual = residual_ref[...]
    scale = lax.rsqrt(jnp.mean(residual * residual, axis=-1, keepdims=True) + EPSILON)
    weighted = incoming * gain_ref[...]

    @pl.when(step >= own_first)
    def _():
        grad_gain_ref[...] += jnp.sum(incoming * residual * scale, axis=0, keepdims=True)

    inner = jnp.mean(weighted * residual, axis=-1, keepdims=True)
    grad_residual = go_ref[...].astype(f32) + (
        scale * weighted - residual * (scale * scale * scale) * inner
    )
    grad_residual_ref[...] = grad_residual
    grad_branch = grad_residual.astype(bf16)
    grad_mix = lax.dot_general(grad_branch, w_ref[...], NT, preferred_element_type=f32)
    grad_c_ref[...] = (grad_mix * conv_ref[...]).astype(bf16)
    grad_conv = grad_mix * gate_c_ref[...]
    grad_conv_ref[...] = grad_conv
    head_ref[0] = grad_conv[:8][:2].astype(bf16)
    total_ref[...] += lax.dot_general(mixer_ref[...], grad_branch, TN, preferred_element_type=f32)

    @pl.when(step == pl.num_programs(0) - 1)
    def _():
        low_ref[...] = total_ref[...].astype(bf16)
        pairs = slot_pairs(own_ref[0], plan, (part_ref,), segments, n_ctx, (low_ref,))
        copy_all([(b, a) for a, b in pairs], sems)


def in_grad_kernel(
    geometry, count, own_ref, grad_conv_ref, behind_ref, before_ref, projected_ref, grad_c_ref,
    normed_ref, taps_ref, grad_projected_ref, grad_taps_ref, *refs
):
    parts, (total_ref, low_ref, sems) = refs[:count], refs[count:]
    plan, segments, n_ctx = geometry
    step = pl.program_id(0)

    @pl.when(step == 0)
    def _():
        total_ref[...] = jnp.zeros_like(total_ref)
        grad_taps_ref[...] = jnp.zeros_like(grad_taps_ref)

    channels = grad_c_ref.shape[1]
    grad_conv = grad_conv_ref[...]
    gate_b = projected_ref[:, :channels]
    values = projected_ref[:, 2 * channels :]
    product = gate_b * values
    one, two = shifted_down(product, before_ref[0].astype(f32))
    for k, shifted in enumerate((two, one, product)):
        grad_taps_ref[k : k + 1] += jnp.sum(grad_conv * shifted, axis=0, keepdims=True)
    one, two = shifted_up(grad_conv, behind_ref[0].astype(f32))
    grad_product = taps_ref[2:3] * grad_conv + taps_ref[1:2] * one + taps_ref[0:1] * two
    grad_projected_ref[:, :channels] = (grad_product * values).astype(bf16)
    grad_projected_ref[:, channels : 2 * channels] = grad_c_ref[...]
    grad_projected_ref[:, 2 * channels :] = (grad_product * gate_b).astype(bf16)
    total_ref[...] += lax.dot_general(
        normed_ref[...], grad_projected_ref[...], TN, preferred_element_type=f32
    )

    @pl.when(step == pl.num_programs(0) - 1)
    def _():
        low_ref[...] = total_ref[...].astype(bf16)
        pairs = slot_pairs(own_ref[0], plan, parts, segments, n_ctx, (low_ref,))
        copy_all([(b, a) for a, b in pairs], sems)


def row_call(body, steps, ins, outs, scratch=()):
    return pl.pallas_call(
        body,
        grid=(steps,),
        in_specs=[
            pl.BlockSpec(memory_space=pltpu.SMEM) if block is None else pl.BlockSpec(block, place)
            for _, block, place in ins
        ],
        out_specs=[
            pl.BlockSpec(memory_space=pl.ANY) if block is None else pl.BlockSpec(block, place)
            for _, _, block, place in outs
        ],
        out_shape=[jax.ShapeDtypeStruct(shape, dtype) for shape, dtype, _, _ in outs],
        scratch_shapes=list(scratch),
        compiler_params=pltpu.CompilerParams(
            vmem_limit_bytes=VMEM_LIMIT, dimension_semantics=("arbitrary",)
        ),
        cost_estimate=SMALL_COST,
    )(*[a for a, _, _ in ins])


def fits(tokens, w_in, w_out, w_gate, w_down, n_dp, n_ctx):
    width, hidden = w_gate.shape
    if n_dp % 2 or n_dp % (2 * n_ctx) or n_dp & (n_dp - 1) or n_ctx & (n_ctx - 1) or n_ctx < 2:
        return False
    depth = width // n_dp
    if width % n_dp or hidden % (n_dp * CHUNKS * 48) or w_in.shape[1] % (2 * n_ctx * 256):
        return False
    lanes = hidden // n_dp // CHUNKS * (n_dp // n_ctx // 2)
    wide = width // n_ctx
    return (
        lanes % 128 == 0
        and wide == lanes + 128
        and lanes == 384
        and wide % 256 == 0
        and depth % 16 == 0
        and 2 * depth <= 256
        and (w_in.shape[1] // n_ctx) % (2 * depth) == 0
        and width % (2 * depth) == 0
        and tokens.shape[1] % n_ctx == 0
        and n_ctx == 2
        and n_dp >= 16
    )


def fast_shards(tokens, w_in, w_out, w_gate, w_up, w_down, gain_mix, gain_ffn, kernel, cotangent):
    seqs, piece, width = tokens.shape
    rows = seqs * piece
    n_chip, n_ctx = lax.axis_size("chip"), lax.axis_size("ctx")
    slots = n_chip * n_ctx
    core = lax.axis_index("core")
    own_slot = lax.axis_index("chip") * n_ctx + lax.axis_index("ctx")
    own = own_slot.astype(jnp.int32)[None]
    depth = w_in.shape[0]
    groups = n_chip // n_ctx
    sub = w_down.shape[0] // CHUNKS
    lanes = groups * sub
    wide = w_out.shape[1]
    in_cols = w_in.shape[1] // 2
    in_parts, out_parts = in_cols // 256, wide // 256
    hidden_count = n_chip * sub
    channels = width // 2

    def mine_other(pair):
        return jnp.where(core == 0, pair[0], pair[1]), jnp.where(core == 0, pair[1], pair[0])

    def in_core_order(mine, other, axis):
        return jnp.where(
            core == 0,
            jnp.concatenate([mine, other], axis=axis),
            jnp.concatenate([other, mine], axis=axis),
        )

    small = jnp.concatenate([gain_mix[None], gain_ffn[None], kernel], axis=0)
    in_pair = w_in.reshape(depth, in_cols // depth, 2, depth).transpose(2, 0, 1, 3)
    in_pair = in_pair.reshape(2, depth, in_parts, 256).transpose(0, 2, 1, 3)
    in_mine, in_other = mine_other(in_pair)
    small_rows = jnp.pad(small, ((0, 11), (0, 256 - depth)))
    swapped = swap(jnp.concatenate([in_other.reshape(in_parts * depth, 256), small_rows], axis=0))
    in_got = swapped[: in_parts * depth].reshape(in_parts, depth, 256)
    in_block = in_core_order(in_mine, in_got, 1).reshape(in_parts * 2 * depth, 256)
    small_block = in_core_order(small, swapped[in_parts * depth :][:5, :depth], 1)
    small_block = jnp.pad(small_block, ((0, 11), (0, 256 - 2 * depth)))
    out_block = w_out.reshape(depth, out_parts, 256).transpose(1, 0, 2).reshape(-1, 256)
    mix_block = jnp.concatenate([in_block, out_block, small_block], axis=0)

    both = jnp.stack([after(w_gate, mix_block), after(w_up, mix_block)]).reshape(2, depth, groups, 2, CHUNKS, sub)
    both = both.transpose(3, 4, 0, 1, 2, 5).reshape(2, CHUNKS, 2, depth, lanes)
    both_mine, both_other = mine_other(both)
    both_block = in_core_order(both_mine, swap(both_other), 2)
    both_block = both_block.reshape(CHUNKS, 4 * depth, lanes)
    down = w_down.reshape(CHUNKS, sub, wide)
    down_rest = down[:, :, lanes:].reshape(CHUNKS, 3, sub // 3, 128).transpose(0, 2, 1, 3)
    chunk_blocks = jnp.concatenate(
        [both_block, down[:, :, :lanes], down_rest.reshape(CHUNKS, sub // 3, lanes)], axis=1
    )

    mix_rows = mix_block.shape[0]
    mix_cut = -(-mix_rows // 32) * 16
    in_rows = in_parts * 2 * depth
    mix_segments = [
        (k * 2 * depth, 2 * depth, 0, 256, 0, 2 * depth, 0, in_cols, 256 * k)
        for k in range(in_parts)
    ]
    def out_segments(base, target):
        return [
            (base + k * depth, depth, 0, 256, target, depth, 0, wide, 256 * k)
            for k in range(out_parts)
        ]

    small_segment = (in_rows + out_parts * depth, 16, 0, 256, 2, 16, 0, 256, 0)
    mix_plan = gather_plan(mix_cut, mix_rows)
    chunk_rows = chunk_blocks.shape[1]
    chunk_cut = chunk_rows // 2
    chunk_segments = [
        (0, 2 * depth, 0, lanes, 0, 2 * depth, 0, lanes, 0),
        (2 * depth, 2 * depth, 0, lanes, 1, 2 * depth, 0, lanes, 0),
        (4 * depth, sub, 0, lanes, 2, sub, 0, wide, 0),
    ] + [
        (4 * depth + sub, sub // 3, 128 * k, 128, 2, sub, k * (sub // 3), wide, lanes)
        for k in range(3)
    ]
    whole_plan = [(0, i, None, 0, chunk_rows) for i in range(slots)]
    whole_geometry = (whole_plan, chunk_segments, n_ctx)
    step_geometry = (gather_plan(chunk_cut, chunk_rows), chunk_segments, n_ctx)

    token_rows = tokens.reshape(rows, width)
    inputs = jnp.concatenate([token_rows, swap(token_rows)], axis=0)
    go_rows = cotangent.reshape(rows, width)
    go = jnp.concatenate([go_rows, swap(go_rows)], axis=0)

    far, first_order, second_order = bit_masks()
    orders = (first_order, second_order)

    def doubled(hold, got):
        return jnp.concatenate([hold, got], axis=0)

    hold = mix_block[None]
    for mask in far:
        hold = doubled(hold, across(hold, mask))
    second_all, last_all = [
        lax.all_gather(after(block, hold), ("chip", "ctx")) for block in chunk_blocks[1:]
    ]
    mix_halves = [hold[:, :mix_cut], hold[:, mix_cut:]]
    next_hold = after(chunk_blocks[0][None], hold)
    far_left = list(far)
    early = [inputs, go]
    for step in range(len(first_order)):
        got = [across(h, order[step]) for h, order in zip(mix_halves, orders)]
        if far_left:
            next_got = across(next_hold, far_left.pop(0))
            next_hold = doubled(next_hold, next_got)
        if early:
            got = [after(g, early[0]) for g in got]
            early = early[1:]
        got = [after(g, next_got) for g in got]
        if step + 1 < len(first_order):
            mix_halves = [doubled(h, g) for h, g in zip(mix_halves, got)]
    mix_parts = [mix_halves[0], got[0], mix_halves[1], got[1]]
    for mask in far_left:
        next_got = across(next_hold, mask)
        next_hold = doubled(next_hold, next_got)
    in_half, out_half, small_all = move(
        own,
        mix_parts,
        [(width, n_ctx * in_cols), (channels, width), (n_chip * 16, n_ctx * 256)],
        (mix_plan, mix_segments + out_segments(in_rows, 1) + [small_segment], n_ctx),
        4,
        False,
    )
    in_half = after(in_half, next_got)
    next_halves = [next_hold[:, :chunk_cut], next_hold[:, chunk_cut:]]

    def step_of(halves, step):
        return [across(h, order[step]) for h, order in zip(halves, orders)]

    def all_after(blocks, *done):
        return [after(block, *done) for block in blocks]

    small_all = small_all.reshape(n_chip, 16, n_ctx * 256)[:, :5, : 2 * depth].astype(f32)
    first_gain = small_all[:, 0].reshape(width)
    second_gain = small_all[:, 1].reshape(width)
    taps = small_all[:, 2:].reshape(n_chip, 3, 2, depth)
    taps = jnp.where(core == 0, taps[:, :, 0], taps[:, :, 1]).transpose(1, 0, 2)
    taps = taps.reshape(3, channels)

    blocks = 2 * seqs

    def at(i):
        return (i, 0)

    def still(i):
        return (0, 0)

    def other(i):
        return ((i + seqs) % blocks, 0)

    wide_rows, thin_rows = (piece, width), (piece, channels)
    taps = jnp.pad(taps, ((0, 5), (0, 0)))
    next_got = step_of(next_halves, 0)
    halo = (1, 2, channels)

    def halo_at(i):
        return (i, 0, 0)

    normed_low, projected, tail = row_call(
        in_kernel,
        blocks,
        [
            (inputs, wide_rows, at),
            (first_gain[None], (1, width), still),
            (in_half, in_half.shape, still),
        ],
        [
            ((2 * rows, width), bf16, wide_rows, at),
            ((2 * rows, 3 * channels), f32, (piece, 3 * channels), at),
            ((blocks, 2, channels), bf16, (1, 2, channels), halo_at),
        ],
    )
    before = passed_along(tail, "ctx", 1)
    conv_taps = after(taps, *next_got)
    next_halves = [
        doubled(h, g) for h, g in zip(next_halves, all_after(next_got, projected))
    ]
    next_got = step_of(next_halves, 1)
    mixer_out, convolved, branch = row_call(
        conv_kernel,
        blocks,
        [
            (projected, (piece, 3 * channels), at),
            (before, halo, halo_at),
            (conv_taps, taps.shape, still),
            (out_half, out_half.shape, still),
        ],
        [
            ((2 * rows, channels), bf16, thin_rows, at),
            ((2 * rows, channels), f32, thin_rows, at),
            ((2 * rows, width), bf16, wide_rows, at),
        ],
    )
    residual, nffn_low = row_call(
        norm_kernel,
        blocks,
        [
            (inputs, wide_rows, at),
            (branch, wide_rows, at),
            (swap(branch), wide_rows, other),
            (second_gain[None], (1, width), still),
        ],
        [((2 * rows, width), f32, wide_rows, at), ((2 * rows, width), bf16, wide_rows, at)],
    )

    next_parts = [next_halves[0], next_got[0], next_halves[1], next_got[1]]
    next_parts = all_after(next_parts, nffn_low)

    totals, first_grads = ffn_chunk(
        own, nffn_low, go, next_parts, None, step_geometry, step_geometry, hidden_count
    )
    first_stages = Stages(first_grads)
    totals, second_grads = ffn_chunk(
        own, nffn_low, go, [second_all], totals, whole_geometry, step_geometry, hidden_count
    )
    second_stages = Stages(second_grads)
    nffn_then = after(nffn_low, *first_stages.got)
    first_stages.advance(totals[1])
    totals, last_grads = ffn_chunk(
        own, nffn_then, go, [last_all], totals, whole_geometry, step_geometry, hidden_count, last=True
    )
    ffn_out, grad_low = totals
    last_stages = Stages(last_grads)
    grad_got = swap(after(grad_low, *first_stages.got, *second_stages.got))
    first_stages.advance(grad_low)
    second_stages.advance(grad_low)

    def turned(i):
        return ((i + seqs) % blocks, 0)

    def turned_back(i):
        return (i, 0)

    def own_place(i):
        return (jnp.maximum(i - seqs, 0), 0)

    def gate_c_place(i):
        return ((i + seqs) % blocks, 1)

    out_plan = [(0, i, None, 0, out_parts * depth) for i in range(slots)]
    grad_residual, grad_conv, grad_c, grad_gain_ffn, head, grad_out_slots = row_call(
        functools.partial(branch_grad_kernel, seqs, (out_plan, out_segments(0, 0), n_ctx)),
        blocks,
        [
            (own, None, None),
            (grad_low, wide_rows, turned),
            (grad_got, wide_rows, turned_back),
            (residual, wide_rows, turned),
            (go, wide_rows, turned),
            (second_gain[None], (1, width), still),
            (mixer_out, thin_rows, turned),
            (convolved, thin_rows, turned),
            (projected, thin_rows, gate_c_place),
            (out_half, out_half.shape, still),
        ],
        [
            ((rows, width), f32, wide_rows, own_place),
            ((2 * rows, channels), f32, thin_rows, turned),
            ((2 * rows, channels), bf16, thin_rows, turned),
            ((1, width), f32, (1, width), still),
            ((blocks, 2, channels), bf16, halo, lambda i: ((i + seqs) % blocks, 0, 0)),
            ((slots, out_parts * depth, 256), bf16, None, None),
        ],
        scratch=[
            pltpu.VMEM((channels, width), f32),
            pltpu.VMEM((channels, width), bf16),
            pltpu.SemaphoreType.DMA((slots * out_parts,)),
        ],
    )
    grad_gain_ffn = grad_gain_ffn[0]
    stages = (first_stages, second_stages, last_stages)
    behind = passed_along(head, "ctx", -1)
    second_stages.advance(grad_c)
    last_stages.advance(grad_c)
    grad_c_then = after(grad_c, *second_stages.sent, *last_stages.sent)
    out_sum = lax.psum_scatter(grad_out_slots, ("chip", "ctx"), scatter_dimension=0).astype(f32)
    sum_plan = gather_plan(in_rows // 2, in_rows)
    grad_projected, grad_kernel, *mix_grad_parts = row_call(
        functools.partial(in_grad_kernel, (sum_plan, mix_segments, n_ctx), 4),
        blocks,
        [
            (own, None, None),
            (grad_conv, thin_rows, at),
            (behind, halo, halo_at),
            (before, halo, halo_at),
            (projected, (piece, 3 * channels), at),
            (grad_c_then, thin_rows, at),
            (normed_low, wide_rows, at),
            (taps, taps.shape, still),
        ],
        [
            ((2 * rows, 3 * channels), bf16, (piece, 3 * channels), at),
            ((8, channels), f32, (8, channels), still),
        ]
        + [(shape, bf16, None, None) for shape in part_shapes(sum_plan, 256)],
        scratch=[
            pltpu.VMEM((width, 3 * channels), f32),
            pltpu.VMEM((width, 3 * channels), bf16),
            pltpu.SemaphoreType.DMA((len(sum_plan) * len(mix_segments),)),
        ],
    )
    grad_kernel = grad_kernel[:3]
    mix_stages = Stages(mix_grad_parts)
    stages = (first_stages, second_stages, last_stages)
    for s in stages:
        s.advance(grad_projected)
    mix_stages.advance()
    late_projected = after(grad_projected, *mix_stages.got)
    mix_stages.advance()
    grad_other = cross_cols(late_projected[rows:], in_half).astype(bf16)
    for s in stages:
        s.advance(grad_other)
    other_got = swap(grad_other)
    grad_mine = cross_cols(after(late_projected, grad_other)[:rows], in_half)
    for s in (*stages, mix_stages):
        s.advance(grad_mine)
    grad_normed = grad_mine + other_got.astype(f32)
    ffn_late = after(ffn_out, grad_other)
    ffn_got = swap(ffn_late[rows:].astype(bf16))
    result = after(residual, grad_mine)[:rows] + (ffn_late[:rows] + ffn_got.astype(f32))
    result = result.astype(bf16).reshape(seqs, piece, width)
    own_inputs = token_rows.astype(f32)
    scale_mix = lax.rsqrt(jnp.mean(own_inputs * own_inputs, axis=-1, keepdims=True) + EPSILON)
    grad_in_norm, grad_gain_mix = norm_backward(own_inputs, scale_mix, first_gain, grad_normed)
    grad_tokens = (grad_residual + grad_in_norm).reshape(seqs, piece, width)

    chunk_sum = jnp.stack([s.total for s in stages])
    both_sum = chunk_sum[:, : 4 * depth].reshape(CHUNKS, 2, 2, depth, lanes).transpose(2, 0, 1, 3, 4)
    both_mine, both_other = mine_other(both_sum)
    both_got = swap(both_other)
    both_sum = in_core_order(both_mine[None], both_got[None], 0)
    both_sum = both_sum.reshape(2, CHUNKS, 2, depth, groups, sub).transpose(2, 3, 4, 0, 1, 5)
    both_sum = both_sum.reshape(2, depth, 2 * CHUNKS * lanes)
    down_rest = chunk_sum[:, 4 * depth + sub :].reshape(CHUNKS, sub // 3, 3, 128)
    down_rest = down_rest.transpose(0, 2, 1, 3).reshape(CHUNKS, sub, 128)
    final_down = jnp.concatenate([chunk_sum[:, 4 * depth : 4 * depth + sub], down_rest], axis=2)
    final_down = final_down.reshape(CHUNKS * sub, wide)

    mix_stages.advance(both_sum, final_down)
    in_sum = mix_stages.total.reshape(in_parts, 2, depth, 256).transpose(1, 0, 2, 3)
    in_mine, in_other = mine_other(in_sum)
    in_sum = in_core_order(in_mine[None], swap(in_other)[None], 0)
    in_sum = in_sum.transpose(0, 2, 1, 3).reshape(2, depth, in_cols // depth, depth)
    final_in = in_sum.transpose(1, 2, 0, 3).reshape(depth, 2 * in_cols)
    final_out = out_sum.reshape(out_parts, depth, 256).transpose(1, 0, 2)
    final_out = final_out.reshape(depth, wide)

    grad_taps = grad_kernel.reshape(3, n_chip, 1, depth)
    grad_taps = jnp.where(
        jnp.arange(2).reshape(1, 1, 2, 1) == core, grad_taps, jnp.zeros_like(grad_taps)
    ).reshape(3, width)
    small_grad = jnp.concatenate([grad_gain_mix[None], grad_gain_ffn[None], grad_taps], axis=0)
    small_sum = small_grad.reshape(5, n_chip, 2 * depth).transpose(1, 0, 2)
    for bit in range(n_ctx.bit_length() - 1):
        small_sum = small_sum + across(small_sum, 1 << bit)
    for bit in range(n_chip.bit_length() - 1):
        mask = n_chip >> (bit + 1)
        low, high = small_sum[: small_sum.shape[0] // 2], small_sum[small_sum.shape[0] // 2 :]
        upper = jnp.bitwise_and(lax.axis_index("chip"), mask) != 0
        small_sum = jnp.where(upper, high, low) + across(jnp.where(upper, low, high), mask * n_ctx)
    small_mine, small_other = mine_other(small_sum[0].reshape(5, 2, depth).transpose(1, 0, 2))
    small_sum = small_mine + swap(small_other)
    return (
        result,
        grad_tokens,
        final_in,
        final_out,
        both_sum[0],
        both_sum[1],
        final_down,
        small_sum[0],
        small_sum[1],
        small_sum[2:5],
    )


def solution(mesh):
    n_dp, n_ctx = mesh.shape["dp"], mesh.shape["ctx"]

    def placed(dp):
        whole, cut = P(dp, "ctx", None), P(dp, "ctx")
        ins = (whole, cut, cut, cut, cut, cut, P(dp), P(dp), P(None, dp), whole)
        outs = (whole, whole, cut, cut, cut, cut, cut, P(dp), P(dp), P(None, dp))
        return ins, outs

    def run(tokens, w_in, w_out, w_gate, w_up, w_down, gain_mix, gain_ffn, kernel, cotangent):
        if fits(tokens, w_in, w_out, w_gate, w_down, n_dp, n_ctx):
            cut_mesh = Mesh(mesh.devices.reshape(n_dp // 2, 2, n_ctx), ("chip", "core", "ctx"))
            body, on, (ins, outs) = fast_shards, cut_mesh, placed(("chip", "core"))
        else:
            body, on, (ins, outs) = plain_shards, mesh, placed("dp")
        call = jax.shard_map(body, mesh=on, in_specs=ins, out_specs=outs, check_vma=False)
        return call(
            tokens, w_in, w_out, w_gate, w_up, w_down, gain_mix, gain_ffn, kernel, cotangent
        )

    return run
```
